32 devices in a mesh: seq: 8 (over z, x), slot: 4 (over y, core).
Axes of the slice: x: 2, y: 2, z: 4, core: 2. Of those that a mesh axis runs over, the one named last changes fastest.
Arguments:
- hidden_in: bfloat16 [16, 1024, 768], P('slot', 'seq'), may hold values from -6 to 6
- lengths: int32 [16], P('slot'), may hold values from 64 to 1024, as said below
- out_grad: bfloat16 [16, 1024, 768], P('slot', 'seq'), may hold values from -6 to 6
- ln1_gain: bfloat16 [768], replicated, may hold values from 0.25 to 1.75
- ln1_bias: bfloat16 [768], replicated, may hold values from -1.75 to 1.75
- ln2_gain: bfloat16 [768], replicated, may hold values from 0.25 to 1.75
- ln2_bias: bfloat16 [768], replicated, may hold values from -1.75 to 1.75
- w_query: bfloat16 [768, 768], replicated, may hold values from -0.21875 to 0.21875
- b_query: bfloat16 [768], replicated, may hold values from -3 to 3
- w_keyval: bfloat16 [768, 128], replicated, may hold values from -0.21875 to 0.21875
- b_keyval: bfloat16 [128], replicated, may hold values from -3 to 3
- w_out: bfloat16 [768, 768], replicated, may hold values from -3 to 3
- b_out: bfloat16 [768], replicated, may hold values from -3 to 3
- w_up: bfloat16 [768, 3072], replicated, may hold values from -0.21875 to 0.21875
- b_up: bfloat16 [3072], replicated, may hold values from -3 to 3
- w_down: bfloat16 [3072, 768], replicated, may hold values from -0.109375 to 0.109375
- b_down: bfloat16 [768], replicated, may hold values from -3 to 3
Outputs:
- layer_out: bfloat16 [16, 1024, 768], P('slot', 'seq')
- grad_input: float32 [16, 1024, 768], P('slot', 'seq')
- grad_ln1_gain: float32 [768], replicated
- grad_ln1_bias: float32 [768], replicated
- grad_ln2_gain: float32 [768], replicated
- grad_ln2_bias: float32 [768], replicated
- grad_w_query: float32 [768, 768], P('seq', 'slot')
- grad_b_query: float32 [768], replicated
- grad_w_keyval: float32 [768, 128], P('seq', 'slot')
- grad_b_keyval: float32 [128], replicated
- grad_w_out: float32 [768, 768], P('seq', 'slot')
- grad_b_out: float32 [768], replicated
- grad_w_up: float32 [768, 3072], P('seq', 'slot')
- grad_b_up: float32 [3072], replicated
- grad_w_down: float32 [3072, 768], P('seq', 'slot')
- grad_b_down: float32 [768], replicated
The draws below stay inside these ranges and needn't reach their ends.
Inputs may be any that keep to these rules, and one draw needn't show every extreme that they name: `lengths`: true length of each slot. Of the 4 consecutive slots that share an index of slot, one has length exactly 1024.
All inputs are finite; a program needn't handle non-finite values.
Results may differ from the reference program's by a relative error of at most 0.011.
Values may be sent and summed in bfloat16 or wider, within the bound.
A program may use at most 128 MiB of HBM per device.

```python
import jax
import jax.numpy as jnp
from jax import lax

D = 768
HEADS = 12
HEAD = 64
ROT = 16
FF = 3072
SPAN = 128
SLOTS_DEV = 4
LEN = 1024
SLOTS = 16
N_SEQ = 8


def draw_lengths(key, part):
    key = jax.random.fold_in(key, 11)
    first, second, third = jax.random.split(key, 3)
    lowest = LEN // 16
    one_draw = jax.random.randint(first, (SLOTS,), lowest, LEN + 1)
    two_draw = jax.random.randint(second, (SLOTS,), lowest, LEN + 1)
    lengths = jnp.maximum(one_draw, two_draw)
    groups = SLOTS // SLOTS_DEV
    picked = jax.random.randint(third, (groups,), 0, SLOTS_DEV)
    within = jnp.arange(SLOTS, dtype=jnp.int32) % SLOTS_DEV
    owner = jnp.repeat(picked, SLOTS_DEV)
    lengths = jnp.where(within == owner, LEN, lengths)
    shortest = (picked[0] + 1) % SLOTS_DEV
    place = jnp.arange(SLOTS, dtype=jnp.int32) == shortest
    lengths = jnp.where(place, lowest, lengths)
    return lengths.astype(jnp.int32)


def block_levels(rng, dims, pieces, smallest, high):
    loudness, own = 1.0, jax.random.fold_in(rng, 6)
    for position, blocks in pieces:
        heights = jnp.exp(jax.random.uniform(jax.random.fold_in(own, position), (blocks,), jnp.float32, smallest / len(pieces), high / len(pieces)))
        loudness = loudness * jnp.repeat(heights, dims[position] // blocks).reshape([-1 if axis == position else 1 for axis in range(len(dims))])
    return loudness


def scatter_about(own_key, shape, scale, limit, shards=(), held_as=jnp.bfloat16):
    level = block_levels(own_key, shape, shards, -0.22, 0.18) if shards else 1.0
    drawn = jax.random.normal(own_key, shape, jnp.float32) * scale * level
    return jnp.minimum(jnp.maximum(drawn, -limit), limit).astype(held_as)


def setup_inputs(seed: int = 0) -> dict:
    seeds = jax.random.split(jax.random.key(seed), 18)
    return {
        "hidden_in": scatter_about(seeds[0], (SLOTS, LEN, D), 1.0, 6.0, ((0, 4), (1, 8))),
        "lengths": draw_lengths(jax.random.fold_in(seeds[17], 71), 0),
        "out_grad": scatter_about(seeds[2], (SLOTS, LEN, D), 1.0, 6.0, ((0, 4), (1, 8))),
        "ln1_gain": jnp.clip(1.0 + 0.15 * jax.random.normal(seeds[3], (D,), jnp.float32), 0.25, 1.75).astype(jnp.bfloat16),
        "ln1_bias": scatter_about(seeds[4], (D,), 0.3, 1.75),
        "ln2_gain": jnp.clip(1.0 + 0.15 * jax.random.normal(seeds[5], (D,), jnp.float32), 0.25, 1.75).astype(jnp.bfloat16),
        "ln2_bias": scatter_about(seeds[6], (D,), 0.3, 1.75),
        "w_query": scatter_about(seeds[7], (D, D), D ** -0.5, 0.21875),
        "b_query": scatter_about(seeds[8], (D,), 0.5, 3.0),
        "w_keyval": scatter_about(seeds[9], (D, 2 * HEAD), D ** -0.5, 0.21875),
        "b_keyval": scatter_about(seeds[10], (2 * HEAD,), 0.5, 3.0),
        "w_out": scatter_about(seeds[11], (D, D), 4 ** -0.5, 3.0),
        "b_out": scatter_about(seeds[12], (D,), 0.5, 3.0),
        "w_up": scatter_about(seeds[13], (D, FF), D ** -0.5, 0.21875),
        "b_up": scatter_about(seeds[14], (FF,), 0.5, 3.0),
        "w_down": scatter_about(seeds[15], (FF, D), FF ** -0.5, 0.109375),
        "b_down": scatter_about(seeds[16], (D,), 0.5, 3.0),
    }


@jax.custom_vjp
def low(v):
    return lax.optimization_barrier(v.astype(jnp.bfloat16)).astype(jnp.float32)

@jax.custom_vjp
def low_back(v):
    return v

def low_keep(v):
    return (low(v), None)

def low_pass(kept, grad):
    return (grad,)

def back_keep(v):
    return (v, None)

def back_low(kept, grad):
    return (low(grad),)
low.defvjp(low_keep, low_pass)
low_back.defvjp(back_keep, back_low)
HIGH = lax.Precision.HIGHEST

def matmul(left, right):
    return jnp.matmul(left, right, precision=HIGH)

def norm(value, gain, bias):
    center = value - lax.optimization_barrier(jnp.mean(value, axis=-1, keepdims=True))
    spread = lax.optimization_barrier(jnp.mean(center * center, axis=-1, keepdims=True))
    return center * lax.rsqrt(spread + 1e-05) * gain + bias

def angles(positions):
    half = ROT // 2
    inverse = 10000.0 ** (-(jnp.arange(half, dtype=jnp.float32) * 2.0 / ROT))
    turns = positions[:, None] * inverse[None, :]
    turns = jnp.concatenate([turns, turns], axis=-1)
    return (jnp.cos(turns), jnp.sin(turns))

def turn(value, cosine, sine):
    half = ROT // 2
    part = value[..., :ROT]
    swapped = jnp.concatenate([-part[..., half:], part[..., :half]], axis=-1)
    return jnp.concatenate([part * cosine + swapped * sine, value[..., ROT:]], axis=-1)

def forward(hidden, params, length):
    g1, c1, g2, c2, wq, bq, wkv, bkv, wo, bo, wu, bu, wd, bd = params
    positions = jnp.arange(LEN, dtype=jnp.int32)
    valid = (positions < length).astype(jnp.float32)[:, None]
    cosine, sine = angles(positions.astype(jnp.float32))
    attn_in = low(norm(hidden, g1, c1))
    mlp_in = low(norm(hidden, g2, c2))
    q_pre = low_back(matmul(attn_in, wq) + bq).reshape(LEN, HEADS, HEAD)
    queries = low(turn(q_pre, cosine[:, None, :], sine[:, None, :]))
    kv_pre = low_back(matmul(attn_in, wkv) + bkv)
    keys = low(turn(kv_pre[:, :HEAD], cosine, sine))
    values = low(kv_pre[:, HEAD:])
    scale = HEAD ** (-0.5)
    blocks = queries.reshape(N_SEQ, SPAN, HEADS, HEAD).transpose(0, 2, 1, 3)
    starts = jnp.arange(N_SEQ, dtype=jnp.int32) * SPAN

    def block(item):
        query_block, start = item
        rows = start + jnp.arange(SPAN, dtype=jnp.int32)
        allowed = (positions[None, :] <= rows[:, None]) & (positions[None, :] < length)
        scores = low_back(jnp.einsum('hcd,kd->hck', query_block, keys, precision=HIGH) * scale)
        scores = jnp.where(allowed[None], scores, -1000000000.0)
        top = lax.optimization_barrier(jnp.max(scores, axis=-1, keepdims=True))
        weights = jnp.exp(scores - top)
        probs = low(weights / lax.optimization_barrier(jnp.sum(weights, axis=-1, keepdims=True)))
        return jnp.einsum('hck,kd->hcd', probs, values, precision=HIGH)
    outputs = lax.map(jax.checkpoint(block), (blocks, starts))
    attn = outputs.transpose(0, 2, 1, 3).reshape(LEN, D)
    attn = low(low_back(attn))
    up_pre = low_back(matmul(mlp_in, wu) + bu)
    act = low(jax.nn.gelu(up_pre, approximate=False))
    total = hidden + matmul(attn, wo) + bo + matmul(act, wd) + bd
    return valid * total

def reference(hidden_in, lengths, out_grad, ln1_gain, ln1_bias, ln2_gain, ln2_bias, w_query, b_query, w_keyval, b_keyval, w_out, b_out, w_up, b_up, w_down, b_down):
    params = tuple((p.astype(jnp.float32) for p in (ln1_gain, ln1_bias, ln2_gain, ln2_bias, w_query, b_query, w_keyval, b_keyval, w_out, b_out, w_up, b_up, w_down, b_down)))

    def one(totals, item):
        slot_in, slot_grad, length = item
        result, back = jax.vjp(lambda h, p: forward(h, p, length), slot_in.astype(jnp.float32), params)
        grad_hidden, grad_params = back(slot_grad.astype(jnp.float32))
        totals = tuple((a + b for a, b in zip(totals, grad_params)))
        return (totals, (result.astype(jnp.bfloat16), grad_hidden))
    start = tuple((jnp.zeros_like(p) for p in params))
    totals, (layer_out, grad_input) = lax.scan(one, start, (hidden_in, out_grad, lengths))
    return (layer_out, grad_input, totals[0], totals[1], totals[2], totals[3], totals[4], totals[5], totals[6], totals[7], totals[8], totals[9], totals[10], totals[11], totals[12], totals[13])
```

```python
import jax
import jax.numpy as jnp
from jax import lax
from jax.experimental import pallas as pl
from jax.experimental.pallas import tpu as pltpu
from jax.sharding import PartitionSpec as P

HEAD = 64
ROT = 16
MESH = pl.DeviceIdType.MESH
BF = jnp.bfloat16
F32 = jnp.float32


def dot(a, b, ca=1, cb=0):
    return lax.dot_general(a, b, (((ca,), (cb,)), ((), ())), preferred_element_type=F32)


def gelu_pair(u):
    cdf = 0.5 * (1.0 + lax.erf(u * 0.7071067811865476))
    pdf = 0.3989422804014327 * jnp.exp(-0.5 * u * u)
    return u * cdf, cdf + u * pdf


def bit_of(value, bit):
    return lax.rem(lax.div(value, 2**bit), 2)


def flip(value, bit):
    return value + (1 - 2 * bit_of(value, bit)) * 2**bit


def put(value, bit, new):
    return value + (new - bit_of(value, bit)) * 2**bit


def placed(index, bits):
    at = 0
    for bit in bits:
        at = at * 2 + (index >> bit) % 2
    return at


class Links:
    def __init__(self, send, recv):
        self.send, self.recv, self.used, self.waits = send, recv, 0, []

    def take(self, count=1):
        first = self.used
        self.used += count
        return first

    def start(self, src, dst, device):
        k = self.take()
        copy = pltpu.make_async_remote_copy(
            src_ref=src,
            dst_ref=dst,
            send_sem=self.send.at[k],
            recv_sem=self.recv.at[k],
            device_id=device,
            device_id_type=MESH,
        )
        copy.start()
        self.waits.append(copy)
        return copy

    def finish(self):
        for copy in self.waits:
            copy.wait_send()


def halving(links, cur, stages, recvs):
    blocks = cur.shape[0]
    off = jnp.int32(0)
    for (mine, partner), recv in zip(stages, recvs):
        half = blocks // 2
        copy = links.start(cur.at[pl.ds(off + (1 - mine) * half, half)], recv, partner)
        yield None
        copy.wait_recv()
        off = off + mine * half

        def add(i, _, off=off, recv=recv):
            cur[off + i] = cur[off + i] + recv[i]
            return 0

        lax.fori_loop(0, half, add, 0)
        blocks = half
    yield off


def kernel(sizes, x_hbm, g_hbm, lens, pars, wup_hbm, wdn_hbm, *rest):
    NS, NJ, BS, BJ, SL, SPAN, D, FF = sizes
    ROWS = SL * SPAN
    HF = FF // 2
    W = FF // NJ
    MID = NJ // 4
    R = D // NS
    QN = NJ // 2
    FRH = FF // NS // 2
    DW = D // QN
    (o_mlp, o_dmlp, o_up, o_dn, o_bup) = rest[:5]
    (x, g, wup, wdn, mlp2, g2, act, dup, dmine, dsend, drecv, msend, mrecv) = rest[5:18]
    ups, upr, dns, dnr = rest[18:20], rest[20:22], rest[22:24], rest[24:26]
    (upm, dnp, dnm, sv, svr, send, recv, lsem) = rest[26:]
    links = Links(send, recv)
    s = lax.axis_index("seq")
    j = lax.axis_index("slot")
    c = bit_of(j, 0)
    tj = bit_of(j, BJ - 1)
    ts = bit_of(s, BS - 1)
    buddy = (s, flip(j, 0))

    loads = [
        pltpu.make_async_copy(x_hbm, x, lsem.at[0]),
        pltpu.make_async_copy(g_hbm, g, lsem.at[1]),
        pltpu.make_async_copy(
            wup_hbm.at[:, pl.ds(pl.multiple_of(c * HF, HF), HF)], wup, lsem.at[2]
        ),
        pltpu.make_async_copy(
            wdn_hbm.at[pl.ds(pl.multiple_of(c * HF, HF), HF), :], wdn, lsem.at[3]
        ),
    ]
    for copy in loads:
        copy.start()

    near = [(flip(s, b), j) for b in range(BS)] + [(s, flip(j, b)) for b in range(BJ)]
    near += [(s, flip(flip(j, BJ - 1), 0)), (flip(s, BS - 1), flip(j, 0))]
    barrier = pltpu.get_barrier_semaphore()
    for device in near:
        pl.semaphore_signal(barrier, inc=1, device_id=device, device_id_type=MESH)
    pl.semaphore_wait(barrier, len(near))

    sv[...] = jnp.zeros_like(sv)
    loads[0].wait()
    loads[1].wait()
    spot = s * SPAN + lax.broadcasted_iota(jnp.int32, (SPAN, 1), 0)
    for i in range(SL):
        rows = pl.ds(i * SPAN, SPAN)
        v = x[rows, :].astype(F32)
        v = v - jnp.mean(v, axis=-1, keepdims=True)
        v = v * lax.rsqrt(jnp.mean(v * v, axis=-1, keepdims=True) + 1e-05)
        mlp2[rows, :] = (v * pars[2:3, :] + pars[3:4, :]).astype(BF)
        g2[rows, :] = jnp.where(spot < lens[i], g[rows, :].astype(F32), 0.0).astype(BF)
    own = pl.ds(0, ROWS)
    theirs = pl.ds(ROWS, ROWS)
    got_m = links.start(mlp2.at[own, :], mlp2.at[theirs, :], buddy)
    got_g = links.start(g2.at[own, :], g2.at[theirs, :], buddy)
    loads[2].wait()
    loads[3].wait()

    RB = 256
    NB = 512

    def first(i, _):
        rows = pl.ds(pl.multiple_of(i * RB, RB), RB)
        for f in range(HF // NB):
            cols = slice(f * NB, (f + 1) * NB)
            at = f * NB
            bias = jnp.where(
                c == 0,
                pars[7 + at // D : 8 + at // D, at % D : at % D + NB]
                if at % D + NB <= D
                else jnp.concatenate(
                    [
                        pars[7 + at // D : 8 + at // D, at % D :],
                        pars[8 + at // D : 9 + at // D, : NB - (D - at % D)],
                    ],
                    axis=1,
                ),
                pars[7 + (at + HF) // D : 8 + (at + HF) // D, (at + HF) % D : (at + HF) % D + NB]
                if (at + HF) % D + NB <= D
                else jnp.concatenate(
                    [
                        pars[7 + (at + HF) // D : 8 + (at + HF) // D, (at + HF) % D :],
                        pars[
                            8 + (at + HF) // D : 9 + (at + HF) // D,
                            : NB - (D - (at + HF) % D),
                        ],
                    ],
                    axis=1,
                ),
            )
            up = dot(mlp2[rows, :], wup[:, cols]) + bias
            back = dot(g2[rows, :], wdn[cols, :], 1, 1)
            a, slope = gelu_pair(up)
            act[rows, cols] = a.astype(BF)
            dup[rows, cols] = (back * slope).astype(BF)
        return 0

    lax.fori_loop(0, ROWS // RB, first, 0)
    got_m.wait_recv()
    got_g.wait_recv()
    lax.fori_loop(ROWS // RB, 2 * ROWS // RB, first, 0)

    orders = [list(range(BS - 1)), list(range(BS - 1))]
    if BS > 2:
        orders[1] = orders[1][1:] + orders[1][:1]
    for k in range(NS // 2):
        ff = slice(k * 2 * FRH, (k + 1) * 2 * FRH)
        part = dot(act[:, ff], g2[...], 0, 0).astype(BF)
        for p in range(2):
            at = placed(k, orders[p])
            for q in range(QN):
                dns[p][q * (NS // 2) + at] = part[p * FRH : (p + 1) * FRH, q * DW : (q + 1) * DW]
    slot_bits = [(bit_of(j, b), (s, flip(j, b))) for b in range(BJ - 1, 0, -1)]
    pipes = []
    for p in range(2):
        stages = slot_bits + [(bit_of(s, b), (flip(s, b), j)) for b in orders[p]]
        recvs, at = [], 0
        blocks = QN * NS // 2
        for _ in stages:
            blocks //= 2
            recvs.append(dnr[p].at[pl.ds(at, blocks)])
            at += blocks
        pipes.append(halving(links, dns[p], stages, recvs))
    for pipe in pipes:
        next(pipe)
    RK = 4 * R
    for k in range(NS // 4):
        for p in range(2):
            for q in range(MID):
                at = (q * 2 + p) * W
                part = dot(mlp2[:, k * RK : (k + 1) * RK], dup[:, at : at + W], 0, 0).astype(BF)
                for r in range(4):
                    block = placed(k * 4 + r, orders[p] + [BS - 1]) * MID + q
                    ups[p][block] = part[r * R : (r + 1) * R, :]
    mid_bits = [(bit_of(j, b), (s, flip(j, b))) for b in range(BJ - 2, 0, -1)]
    for p in range(2):
        stages = [(bit_of(s, b), (flip(s, b), j)) for b in orders[p] + [BS - 1]] + mid_bits
        recvs, at = [], 0
        blocks = NS * MID
        for _ in stages:
            blocks //= 2
            recvs.append(upr[p].at[pl.ds(at, blocks)])
            at += blocks
        pipes.append(halving(links, ups[p], stages, recvs))
    for pipe in pipes[2:]:
        next(pipe)

    for k in range(ROWS // RB):
        rows = slice(ROWS + k * RB, ROWS + (k + 1) * RB)
        here = slice(k * RB, (k + 1) * RB)
        msend[here, :] = dot(act[rows, :], wdn[...]).astype(BF)
        dsend[here, :] = dot(dup[rows, :], wup[...], 1, 1).astype(BF)
    got_out = links.start(msend, mrecv, buddy)
    got_back = links.start(dsend, drecv, buddy)

    half = jnp.sum(dup[...].astype(F32), axis=0, keepdims=True)
    for q in range(FF // D):
        piece = half[:, (q * D) % HF : (q * D) % HF + D]
        sv[q : q + 1, :] = jnp.where(c == (q * D) // HF, piece, 0.0)

    for k in range(ROWS // RB):
        here = slice(k * RB, (k + 1) * RB)
        o_mlp[here, :] = dot(act[here, :], wdn[...])
        o_dmlp[here, :] = dot(dup[here, :], wup[...], 1, 1)
    got_out.wait_recv()
    got_back.wait_recv()
    for k in range(ROWS // 128):
        here = slice(k * 128, (k + 1) * 128)
        o_mlp[here, :] = o_mlp[here, :] + mrecv[here, :].astype(F32)
        o_dmlp[here, :] = o_dmlp[here, :] + drecv[here, :].astype(F32)

    ends = [None] * 4
    live = [0, 1, 2, 3]
    while live:
        for n in list(live):
            ends[n] = next(pipes[n])
            if ends[n] is not None:
                live.remove(n)

    def scatter_pair(src, dst, first_k, mine, target, is_self):
        k = links.take()
        remote = pltpu.make_async_remote_copy(
            src_ref=src,
            dst_ref=dst.at[mine],
            send_sem=links.send.at[k],
            recv_sem=links.recv.at[first_k + mine],
            device_id=target,
            device_id_type=MESH,
        )
        local = pltpu.make_async_copy(src, dst.at[mine], links.recv.at[first_k + mine])

        @pl.when(is_self)
        def _():
            local.start()

        @pl.when(jnp.logical_not(is_self))
        def _():
            remote.start()

        def done():
            @pl.when(jnp.logical_not(is_self))
            def _():
                remote.wait_send()

        return done

    dones, arrivals = [], []

    def arrive(dst, first_k):
        for t in range(2):
            arrivals.append(
                pltpu.make_async_copy(dst.at[t], dst.at[t], links.recv.at[first_k + t])
            )

    for p in range(2):
        upp = upm[p]
        upp[...] = ups[p][ends[2 + p]]
    for p in range(2):
        part = dns[p][ends[p]]
        for h in range(2):
            dnm[2 * p + h] = part[:, h * (DW // 2) : (h + 1) * (DW // 2)]
    first_k = links.take(2)
    for p in range(2):
        is_self = jnp.logical_and(tj == c, c == p)
        target = (s, put(put(j, 0, p), BJ - 1, c))
        dones.append(scatter_pair(upm[p], upm[2], first_k, tj, target, is_self))
    arrive(upm[2], first_k)
    for p in range(2):
        first_k = links.take(2)
        for h in range(2):
            is_self = jnp.logical_and(ts == c, c == h)
            target = (put(s, BS - 1, c), put(j, 0, h))
            dones.append(
                scatter_pair(dnm.at[2 * p + h], dnp.at[p], first_k, ts, target, is_self)
            )
        arrive(dnp.at[p], first_k)

    stages = [(s, flip(j, b)) for b in range(BJ)] + [(flip(s, b), j) for b in range(BS)]
    for n, partner in enumerate(stages):
        out = svr.at[2 * n]
        out[...] = sv[...]
        copy = links.start(out, svr.at[2 * n + 1], partner)
        copy.wait_recv()
        sv[...] = sv[...] + svr[2 * n + 1]
    o_bup[...] = sv[...]
    for copy in arrivals:
        copy.wait()
    o_up[...] = upm[2][0].astype(F32) + upm[2][1].astype(F32)
    for p in range(2):
        o_dn[p * FRH : (p + 1) * FRH, :] = dnp[p, 0].astype(F32) + dnp[p, 1].astype(F32)
    for done in dones:
        done()
    links.finish()


def mlp_call(mesh_sizes, x, g, lengths, pars, w_up, w_down):
    NS, NJ = mesh_sizes
    BS, BJ = NS.bit_length() - 1, NJ.bit_length() - 1
    SL, SPAN, D = x.shape
    FF = w_up.shape[1]
    ROWS = SL * SPAN
    HF, W, MID, R, QN, FRH, DW = (
        FF // 2,
        FF // NJ,
        NJ // 4,
        D // NS,
        NJ // 2,
        FF // NS // 2,
        2 * D // NJ,
    )
    vm = pltpu.VMEM
    n_stage = BS + BJ
    scratch = [
        vm((ROWS, D), BF),
        vm((ROWS, D), BF),
        vm((D, HF), BF),
        vm((HF, D), BF),
        vm((2 * ROWS, D), BF),
        vm((2 * ROWS, D), BF),
        vm((2 * ROWS, HF), BF),
        vm((2 * ROWS, HF), BF),
        vm((8, 128), F32),
        vm((ROWS, D), BF),
        vm((ROWS, D), BF),
        vm((ROWS, D), BF),
        vm((ROWS, D), BF),
        vm((NS * MID, R, W), BF),
        vm((NS * MID, R, W), BF),
        vm((NS * MID, R, W), BF),
        vm((NS * MID, R, W), BF),
        vm((QN * NS // 2, FRH, DW), BF),
        vm((QN * NS // 2, FRH, DW), BF),
        vm((QN * NS // 2, FRH, DW), BF),
        vm((QN * NS // 2, FRH, DW), BF),
        vm((4, R, W), BF),
        vm((2, 2, FRH, DW // 2), BF),
        vm((4, FRH, DW // 2), BF),
        vm((8, D), F32),
        vm((2 * n_stage, 8, D), F32),
        pltpu.SemaphoreType.DMA((64,)),
        pltpu.SemaphoreType.DMA((64,)),
        pltpu.SemaphoreType.DMA((4,)),
    ]
    sizes = (NS, NJ, BS, BJ, SL, SPAN, D, FF)

    def call(*refs):
        refs = list(refs)
        at = 11 + 21
        upm = refs[at]
        refs[at] = [upm.at[0], upm.at[1], upm.at[pl.ds(2, 2)]]
        kernel(sizes, *refs)

    anyspace = pl.BlockSpec(memory_space=pl.ANY)
    return pl.pallas_call(
        call,
        out_shape=[
            jax.ShapeDtypeStruct((ROWS, D), F32),
            jax.ShapeDtypeStruct((ROWS, D), F32),
            jax.ShapeDtypeStruct((R, W), F32),
            jax.ShapeDtypeStruct((2 * FRH, DW // 2), F32),
            jax.ShapeDtypeStruct((8, D), F32),
        ],
        in_specs=[
            anyspace,
            anyspace,
            pl.BlockSpec(memory_space=pltpu.SMEM),
            pl.BlockSpec(memory_space=pltpu.VMEM),
            anyspace,
            anyspace,
        ],
        out_specs=[pl.BlockSpec(memory_space=pltpu.VMEM)] * 5,
        scratch_shapes=scratch,
        compiler_params=pltpu.CompilerParams(
            collective_id=0, has_side_effects=True, vmem_limit_bytes=60 * 2**20
        ),
    )(x.reshape(ROWS, D), g.reshape(ROWS, D), lengths, pars, w_up, w_down)


def norm(value, gain, bias):
    center = value - jnp.mean(value, axis=-1, keepdims=True)
    spread = jnp.mean(center * center, axis=-1, keepdims=True)
    return center * lax.rsqrt(spread + 1e-05) * gain + bias


def angles(positions):
    half = ROT // 2
    inverse = 10000.0 ** (-(jnp.arange(half, dtype=jnp.float32) * 2.0 / ROT))
    turns = positions[:, None] * inverse[None, :]
    turns = jnp.concatenate([turns, turns], axis=-1)
    return (jnp.cos(turns), jnp.sin(turns))


def turn(value, cosine, sine):
    half = ROT // 2
    part = value[..., :ROT]
    swapped = jnp.concatenate([-part[..., half:], part[..., :half]], axis=-1)
    return jnp.concatenate([part * cosine + swapped * sine, value[..., ROT:]], axis=-1)


def body(
    hidden_in,
    lengths,
    out_grad,
    ln1_gain,
    ln1_bias,
    ln2_gain,
    ln2_bias,
    w_query,
    b_query,
    w_keyval,
    b_keyval,
    w_out,
    b_out,
    w_up,
    b_up,
    w_down,
    b_down,
):
    slots_here, span_len, width = hidden_in.shape
    heads = width // HEAD
    total_len = span_len * lax.axis_size("seq")
    scale = HEAD ** (-0.5)
    positions = lax.axis_index("seq") * span_len + jnp.arange(span_len, dtype=jnp.int32)
    key_ids = jnp.arange(total_len, dtype=jnp.int32)
    valid = (positions[None, :] < lengths[:, None]).astype(jnp.float32)[..., None]
    cosine, sine = angles(positions.astype(jnp.float32))
    hidden = hidden_in.astype(jnp.float32)
    attn_in32, norm_one_back = jax.vjp(
        norm, hidden, ln1_gain.astype(jnp.float32), ln1_bias.astype(jnp.float32)
    )
    mlp_in32, norm_two_back = jax.vjp(
        norm, hidden, ln2_gain.astype(jnp.float32), ln2_bias.astype(jnp.float32)
    )
    attn_in = attn_in32.astype(jnp.bfloat16)
    mlp_in = mlp_in32.astype(jnp.bfloat16)
    q_pre = jnp.dot(attn_in, w_query, preferred_element_type=jnp.float32) + b_query.astype(
        jnp.float32
    )
    q_pre = q_pre.reshape(slots_here, span_len, heads, HEAD)
    q_turned, query_back = jax.vjp(lambda v: turn(v, cosine[:, None, :], sine[:, None, :]), q_pre)
    queries = q_turned.astype(jnp.bfloat16)
    kv_pre = jnp.dot(attn_in, w_keyval, preferred_element_type=jnp.float32) + b_keyval.astype(
        jnp.float32
    )
    key_turned, key_back = jax.vjp(lambda v: turn(v, cosine, sine), kv_pre[..., :HEAD])
    kv_local = jnp.concatenate([key_turned, kv_pre[..., HEAD:]], axis=-1).astype(jnp.bfloat16)
    kv_whole = lax.all_gather(kv_local, "seq", axis=1, tiled=True)
    pars = jnp.concatenate(
        [
            v.astype(jnp.float32)
            for v in (ln1_gain, ln1_bias, ln2_gain, ln2_bias, b_query, b_out, b_down, b_up)
        ]
    ).reshape(7 + b_up.shape[0] // width, width)
    mlp_part, d_mlp, up_part, down_part, bup = mlp_call(
        (lax.axis_size("seq"), lax.axis_size("slot")),
        hidden_in,
        out_grad,
        lengths,
        pars,
        w_up,
        w_down,
    )
    mlp_out = mlp_part.reshape(hidden.shape) + b_down.astype(jnp.float32)

    def scores_of(query_slot, kv_slot, length):
        raw = (
            jnp.einsum(
                "chd,kd->hck", query_slot, kv_slot[:, :HEAD], preferred_element_type=jnp.float32
            )
            * scale
        )
        allowed = (key_ids[None, :] <= positions[:, None]) & (key_ids[None, :] < length)
        return jnp.where(allowed[None], raw, -1000000000.0)

    def forward_slot(item):
        query_slot, kv_slot, length = item
        scores = scores_of(query_slot, kv_slot, length)
        top = jnp.max(scores, axis=-1, keepdims=True)
        weights = jnp.exp(scores - top)
        summed = jnp.sum(weights, axis=-1, keepdims=True)
        probs = (weights / summed).astype(jnp.bfloat16)
        mixed = jnp.einsum(
            "hck,kd->chd", probs, kv_slot[:, HEAD:], preferred_element_type=jnp.float32
        )
        return (mixed.reshape(span_len, width).astype(jnp.bfloat16), top + jnp.log(summed))

    attn, log_totals = lax.map(forward_slot, (queries, kv_whole, lengths))
    attn_out = jnp.dot(attn, w_out, preferred_element_type=jnp.float32) + b_out.astype(jnp.float32)
    layer_out = (valid * (hidden + attn_out + mlp_out)).astype(jnp.bfloat16)
    grad_low = (out_grad.astype(jnp.float32) * valid).astype(jnp.bfloat16)
    grad_full = grad_low.astype(jnp.float32)
    grad_bias_out = jnp.sum(grad_full, axis=(0, 1))
    grad_w_out = jnp.einsum("std,ste->de", attn, grad_low, preferred_element_type=jnp.float32)
    d_attn = jnp.dot(grad_low, w_out.T, preferred_element_type=jnp.float32).astype(jnp.bfloat16)
    d_mlp_in = d_mlp.reshape(hidden.shape)
    grad_b_up = bup[: b_up.shape[0] // width].reshape(b_up.shape)

    def backward_slot(item):
        query_slot, kv_slot, length, log_total, d_slot = item
        scores = scores_of(query_slot, kv_slot, length)
        probs = jnp.exp(scores - log_total)
        d_probs = jnp.einsum(
            "chd,kd->hck", d_slot, kv_slot[:, HEAD:], preferred_element_type=jnp.float32
        )
        d_scores = (probs * (d_probs - jnp.sum(probs * d_probs, axis=-1, keepdims=True))).astype(
            jnp.bfloat16
        )
        d_query = (
            jnp.einsum(
                "hck,kd->chd", d_scores, kv_slot[:, :HEAD], preferred_element_type=jnp.float32
            )
            * scale
        )
        d_key = (
            jnp.einsum("hck,chd->kd", d_scores, query_slot, preferred_element_type=jnp.float32)
            * scale
        )
        d_value = jnp.einsum(
            "hck,chd->kd", probs.astype(jnp.bfloat16), d_slot, preferred_element_type=jnp.float32
        )
        return (d_query, jnp.concatenate([d_key, d_value], axis=-1))

    d_attn_heads = d_attn.reshape(slots_here, span_len, heads, HEAD)
    d_query, d_kv_terms = lax.map(
        backward_slot, (queries, kv_whole, lengths, log_totals, d_attn_heads)
    )
    d_kv = lax.psum_scatter(d_kv_terms, "seq", scatter_dimension=1, tiled=True)
    d_key_pre = key_back(d_kv[..., :HEAD])[0]
    d_kv_pre = jnp.concatenate([d_key_pre, d_kv[..., HEAD:]], axis=-1).astype(jnp.bfloat16)
    d_q_pre = query_back(d_query)[0].reshape(slots_here, span_len, width).astype(jnp.bfloat16)
    grad_b_query = jnp.sum(d_q_pre.astype(jnp.float32), axis=(0, 1))
    grad_b_keyval = jnp.sum(d_kv_pre.astype(jnp.float32), axis=(0, 1))
    grad_w_query = jnp.einsum("std,ste->de", attn_in, d_q_pre, preferred_element_type=jnp.float32)
    grad_w_keyval = jnp.einsum("std,ste->de", attn_in, d_kv_pre, preferred_element_type=jnp.float32)
    d_attn_in = jnp.dot(d_q_pre, w_query.T, preferred_element_type=jnp.float32) + jnp.dot(
        d_kv_pre, w_keyval.T, preferred_element_type=jnp.float32
    )
    d_hidden_one, grad_gain_one, grad_shift_one = norm_one_back(d_attn_in)
    d_hidden_two, grad_gain_two, grad_shift_two = norm_two_back(d_mlp_in)
    grad_input = grad_full + d_hidden_one + d_hidden_two
    small = lax.psum(
        (
            grad_gain_one,
            grad_shift_one,
            grad_gain_two,
            grad_shift_two,
            grad_b_query,
            grad_b_keyval,
            grad_bias_out,
        ),
        ("seq", "slot"),
    )
    query_rows, keyval_rows, out_rows = (
        lax.psum_scatter(grad_w_query, "seq", scatter_dimension=0, tiled=True),
        lax.psum_scatter(grad_w_keyval, "seq", scatter_dimension=0, tiled=True),
        lax.psum_scatter(grad_w_out, "seq", scatter_dimension=0, tiled=True),
    )
    query_part, keyval_part, out_part = (
        lax.psum_scatter(query_rows, "slot", scatter_dimension=1, tiled=True),
        lax.psum_scatter(keyval_rows, "slot", scatter_dimension=1, tiled=True),
        lax.psum_scatter(out_rows, "slot", scatter_dimension=1, tiled=True),
    )
    return (
        layer_out,
        grad_input,
        small[0],
        small[1],
        small[2],
        small[3],
        query_part,
        small[4],
        keyval_part,
        small[5],
        out_part,
        small[6],
        up_part,
        grad_b_up,
        down_part,
        small[6],
    )


def solution(mesh):
    placed = (
        P("slot", "seq", None),
        P("slot"),
        P("slot", "seq", None),
        P(),
        P(),
        P(),
        P(),
        P(),
        P(),
        P(),
        P(),
        P(),
        P(),
        P(),
        P(),
        P(),
        P(),
    )
    return jax.shard_map(
        body,
        mesh=mesh,
        in_specs=placed,
        out_specs=(
            P("slot", "seq", None),
            P("slot", "seq", None),
            P(),
            P(),
            P(),
            P(),
            P("seq", "slot"),
            P(),
            P("seq", "slot"),
            P(),
            P("seq", "slot"),
            P(),
            P("seq", "slot"),
            P(),
            P("seq", "slot"),
            P(),
        ),
        check_vma=False,
    )
```

```python
import math

import jax
import jax.numpy as jnp
import numpy as np
from jax import lax
from jax.experimental import pallas as pl
from jax.experimental.pallas import tpu as pltpu
from jax.sharding import PartitionSpec as P

HEAD = 64
ROT = 16
PAIR = 2 * HEAD
MESH = pl.DeviceIdType.MESH
BF = jnp.bfloat16
F32 = jnp.float32


def dot(a, b, ca=1, cb=0):
    return lax.dot_general(a, b, (((ca,), (cb,)), ((), ())), preferred_element_type=F32)


def gelu_pair(u):
    cdf = 0.5 * (1.0 + lax.erf(u * 0.7071067811865476))
    pdf = 0.3989422804014327 * jnp.exp(-0.5 * u * u)
    return u * cdf, cdf + u * pdf


def bit_of(value, bit):
    return lax.rem(lax.div(value, 2**bit), 2)


def flip(value, bit):
    return value + (1 - 2 * bit_of(value, bit)) * 2**bit


def put(value, bit, new):
    return value + (new - bit_of(value, bit)) * 2**bit


def placed(index, bits):
    at = 0
    for bit in bits:
        at = at * 2 + (index >> bit) % 2
    return at


def turned(value, tables):
    same, after, before = tables
    return value * same + pltpu.roll(value, PAIR - 8, 1) * after + pltpu.roll(value, 8, 1) * before


def turned_back(value, tables):
    same, after, before = tables
    return (
        value * same
        + pltpu.roll(value * after, 8, 1)
        + pltpu.roll(value * before, PAIR - 8, 1)
    )


def rotary_tables(length):
    half = ROT // 2
    inverse = (10000.0 ** (-(np.arange(half, dtype=np.float32) * 2.0 / ROT))).astype(np.float32)
    turns = np.arange(length, dtype=np.float32)[:, None] * inverse[None, :]
    cosine = np.cos(turns.astype(np.float64)).astype(np.float32)
    sine = np.sin(turns.astype(np.float64)).astype(np.float32)
    out = np.zeros((3, length, PAIR), np.float32)
    out[0] = 1.0
    for head in range(2):
        at = head * HEAD
        out[0, :, at : at + half] = cosine
        out[0, :, at + half : at + ROT] = cosine
        out[1, :, at : at + half] = -sine
        out[2, :, at + half : at + ROT] = sine
    return out


class Links:
    def __init__(self, send, recv):
        self.send, self.recv, self.used, self.waits = send, recv, 0, []

    def take(self, count=1):
        first = self.used
        self.used += count
        return first

    def copy(self, src, dst, device, arrival=None):
        k = self.take()
        return pltpu.make_async_remote_copy(
            src_ref=src,
            dst_ref=dst,
            send_sem=self.send.at[k],
            recv_sem=self.recv.at[k if arrival is None else arrival],
            device_id=device,
            device_id_type=MESH,
        )

    def start(self, src, dst, device):
        copy = self.copy(src, dst, device)
        copy.start()
        self.waits.append(copy)
        return copy

    def unless(self, own, src, dst, device, arrival):
        remote = self.copy(src, dst, device, arrival)
        local = pltpu.make_async_copy(src, dst, self.recv.at[arrival])
        other = jnp.logical_not(own)
        self.waits.append((other, remote))

        def start():
            @pl.when(own)
            def _():
                local.start()

            @pl.when(other)
            def _():
                remote.start()

        return start

    def arrived(self, dst, arrival):
        pltpu.make_async_copy(dst, dst, self.recv.at[arrival]).wait()

    def finish(self):
        for copy in self.waits:
            if isinstance(copy, tuple):

                @pl.when(copy[0])
                def _(copy=copy):
                    copy[1].wait_send()

            else:
                copy.wait_send()


class Halving:
    def __init__(self, links, cur, stages, recv):
        blocks = cur.shape[0]
        off, at = jnp.int32(0), 0
        self.cur, self.steps, self.links = cur, [], links
        for mine, partner in stages:
            blocks //= 2
            src = cur.at[pl.ds(off + (1 - mine) * blocks, blocks)]
            dst = recv.at[pl.ds(at, blocks)]
            off = off + mine * blocks
            self.steps.append((links.copy(src, dst, partner), dst, off, blocks))
            at += blocks
        self.end = off

    def start(self, k):
        self.steps[k][0].start()
        self.links.waits.append(self.steps[k][0])

    def finish(self, k):
        copy, recv, off, blocks = self.steps[k]
        cur = self.cur
        copy.wait_recv()

        def add(i, _):
            cur[off + i] = cur[off + i] + recv[i]
            return 0

        lax.fori_loop(0, blocks, add, 0)

    def step(self, k):
        if k:
            self.finish(k - 1)
        if k < len(self.steps):
            self.start(k)


class Direct:
    def __init__(self, links, size, me, device_of, source, dst):
        self.links, self.size, self.me, self.dst = links, size, me, dst
        self.source = source
        self.out = []
        for d in range(1, size):
            target = lax.rem(me + d, size)
            self.out.append(links.copy(source(target), dst.at[me], device_of(target)))

    def start(self):
        for copy in self.out:
            copy.start()
            self.links.waits.append(copy)

    def finish(self):
        for d in range(1, self.size):
            sender = lax.rem(self.me + self.size - d, self.size)
            self.out[d - 1].wait_recv()


class Sizes:
    def __init__(self, NS, NJ, SL, SPAN, D, FF):
        self.NS, self.NJ, self.SL, self.SPAN, self.D, self.FF = NS, NJ, SL, SPAN, D, FF
        self.BS, self.BJ = NS.bit_length() - 1, NJ.bit_length() - 1
        self.ROWS, self.LEN, self.HF = SL * SPAN, NS * SPAN, FF // 2
        self.QN = NJ // 2
        self.R, self.W = D // NS, FF // NJ
        self.CH = NS // 2
        self.CW = self.HF // self.CH
        self.CPP = self.W // self.CW
        self.FRH, self.DW = self.CW // 2, D // self.QN
        self.R2, self.C4 = self.R // 2, D // NJ
        self.PAIRS = D // PAIR
        self.PG = self.PAIRS // 2
        self.PR = self.PG * SPAN
        self.KR = PAIR // NJ
        self.STEP = self.PG if self.LEN <= 1024 else 1


def scratch_of(z):
    vm = pltpu.VMEM
    rows, d = z.ROWS, z.D
    return dict(
        x=vm((rows, d), BF),
        g2=vm((2 * rows, d), BF),
        mlp2=vm((2 * rows, d), BF),
        ain=vm((rows, d), BF),
        wq=vm((d, d), BF),
        wkv=vm((d, PAIR), BF),
        wout=vm((d, d), BF),
        wup=vm((d, z.HF), BF),
        wdn=vm((z.HF, d), BF),
        tab=vm((3, z.SPAN, PAIR), F32),
        act=vm((2 * rows, z.HF), BF),
        dup=vm((2 * rows, z.HF), BF),
        l1=vm((2, z.SL, 2 * z.PR, PAIR), BF),
        l2=vm((2, z.SL, 2 * z.PR, PAIR), BF),
        att=vm((rows, d), BF),
        dq=vm((rows, d), BF),
        kv=vm((z.SL, z.NS, z.SPAN, PAIR), BF),
        kvs=vm((z.LEN, PAIR), BF),
        vks=vm((z.LEN, PAIR), BF),
        r1=vm((2 * z.STEP * z.SPAN, z.LEN), BF),
        r2=vm((2 * z.STEP * z.SPAN, z.LEN), BF),
        bias=vm((z.SPAN, z.LEN), F32),
        dkt=vm((z.SL, PAIR, z.LEN), F32 if z.LEN <= 1024 else BF),
        dks=vm((z.SL, z.NS, PAIR, z.SPAN), BF),
        dkr=vm((z.SL, z.NS - 1, PAIR, z.SPAN), BF),
        up=vm((z.CH, z.NS, z.R, z.CW), BF),
        upr=vm((z.CH, z.NS - 1, z.R, z.CW), BF),
        upf=vm((z.CPP, z.QN, z.R, z.CW), BF),
        dn=vm((z.CH, 2, z.QN, z.FRH, z.DW), BF),
        dnr=vm((z.CH, 2, z.QN - 1, z.FRH, z.DW), BF),
        dnr2=vm((2 * z.CH - 2, z.FRH, z.DW), BF),
        dnm=vm((4, z.FRH, z.DW // 2), BF),
        dnf=vm((2, 2, z.FRH, z.DW // 2), BF),
        wo=vm((2, z.NS, z.R2, d), BF),
        wor=vm((2, z.NS - 1, z.R2, d), BF),
        wos=vm((2, z.NJ, z.R2, z.C4), BF),
        wof=vm((2, z.NJ, z.R2, z.C4), BF),
        wox=vm((2, 2, z.R2, z.C4), F32),
        woy=vm((2, 2, z.R2, z.C4), BF),
        gq=vm((2, 2 * z.NS, z.R2, d // 2), BF),
        gqr=vm((2, 2 * z.NS - 1, z.R2, d // 2), BF),
        gqs=vm((2, z.QN, z.R2, z.C4), BF),
        gqf=vm((z.NJ, z.R2, z.C4), BF),
        kgs=vm((z.NJ, z.KR, d), BF),
        kgf=vm((z.NJ, z.KR, d), BF),
        kg2=vm((z.NS, z.KR, z.R), BF),
        kgx=vm((z.NS, z.KR, z.R), BF),
        sv=vm((2, 8, d), F32),
        sva=vm((z.NJ, 8, d), F32),
        svb=vm((z.NS, 8, d), F32),
        sw=vm((2, 24, 128), F32),
        swa=vm((z.NJ, 24, 128), F32),
        swb=vm((z.NS, 24, 128), F32),
        own_mlp=vm((rows, d), F32),
        own_d=vm((rows, d), F32 if z.LEN <= 1024 else BF),
        send=pltpu.SemaphoreType.DMA((48 * z.NS // 2,)),
        recv=pltpu.SemaphoreType.DMA((48 * z.NS // 2,)),
        lsem=pltpu.SemaphoreType.DMA((12,)),
    )


def kernel(z, ins, outs, m):
    x_hbm, g_hbm, lens, pars, wq_hbm, wkv_hbm, wout_hbm, wup_hbm, wdn_hbm, tab_hbm = ins
    o_lo, o_gi, o_up, o_dn, o_wo, o_wq, o_wkv, o_sv, o_sw = outs
    NS, NJ, BS, BJ, SL, SPAN, D, HF = z.NS, z.NJ, z.BS, z.BJ, z.SL, z.SPAN, z.D, z.HF
    ROWS, LEN, QN, R, R2, CW, C4, PG, PR = (
        z.ROWS, z.LEN, z.QN, z.R, z.R2, z.CW, z.C4, z.PG, z.PR,
    )
    links = Links(m.send, m.recv)
    s = lax.axis_index("seq")
    j = lax.axis_index("slot")
    c = bit_of(j, 0)
    ts = bit_of(s, BS - 1)
    rank = lax.div(j, 2)
    buddy = (s, flip(j, 0))
    scale = HEAD**-0.5

    def seq_device(n):
        return (n, j)

    def slot_device(n):
        return (s, n)

    def load(k, src, dst):
        copy = pltpu.make_async_copy(src, dst, m.lsem.at[k])
        copy.start()
        return copy

    load_x = load(0, x_hbm, m.x)
    load_g = load(1, g_hbm, m.g2.at[pl.ds(0, ROWS), :])
    load_tab = load(2, tab_hbm.at[:, pl.ds(pl.multiple_of(s * SPAN, SPAN), SPAN), :], m.tab)
    load_wkv = load(3, wkv_hbm, m.wkv)
    load_wq = load(4, wq_hbm, m.wq)
    load_wout = load(5, wout_hbm, m.wout)
    load_wup = load(6, wup_hbm.at[:, pl.ds(pl.multiple_of(c * HF, HF), HF)], m.wup)
    load_wdn = load(7, wdn_hbm.at[pl.ds(pl.multiple_of(c * HF, HF), HF), :], m.wdn)

    for i in range(SL):
        m.kv[i] = jnp.zeros((NS, SPAN, PAIR), BF)
    near = [seq_device(lax.rem(s + d, NS)) for d in range(1, NS)]
    near += [slot_device(lax.rem(j + d, NJ)) for d in range(1, NJ)]
    near += [(flip(s, BS - 1), flip(j, 0))]
    barrier = pltpu.get_barrier_semaphore()
    for device in near:
        pl.semaphore_signal(barrier, inc=1, device_id=device, device_id_type=MESH)
    pl.semaphore_wait(barrier, len(near))

    spot = s * SPAN + lax.broadcasted_iota(jnp.int32, (SPAN, 1), 0)
    load_x.wait()
    load_g.wait()
    for i in range(SL):
        rows = slice(i * SPAN, (i + 1) * SPAN)
        v = m.x[rows, :].astype(F32)
        v = v - jnp.mean(v, axis=-1, keepdims=True)
        v = v * lax.rsqrt(jnp.mean(v * v, axis=-1, keepdims=True) + 1e-05)
        m.ain[rows, :] = (v * pars[0:1, :] + pars[1:2, :]).astype(BF)
        m.mlp2[rows, :] = (v * pars[2:3, :] + pars[3:4, :]).astype(BF)
        m.g2[rows, :] = jnp.where(spot < lens[i], m.g2[rows, :].astype(F32), 0.0).astype(BF)
    own, theirs = pl.ds(0, ROWS), pl.ds(ROWS, ROWS)
    msend, dsend = m.g2.at[theirs, :], m.act.at[theirs, pl.ds(0, D)]
    mrecv, drecv = m.mlp2.at[own, :], m.mlp2.at[theirs, :]
    got_m = links.copy(m.mlp2.at[own, :], m.mlp2.at[theirs, :], buddy)
    got_g = links.copy(m.g2.at[own, :], m.g2.at[theirs, :], buddy)
    got_m.start()
    got_g.start()

    lane = lax.broadcasted_iota(jnp.int32, (SPAN, PAIR), 1)
    low = lane < HEAD
    load_tab.wait()
    tables = (m.tab[0], m.tab[1], m.tab[2])
    key_tables = (
        jnp.where(low, tables[0], 1.0),
        jnp.where(low, tables[1], 0.0),
        jnp.where(low, tables[2], 0.0),
    )
    load_wkv.wait()
    kv_pre = dot(m.ain[...], m.wkv[...]) + pars[11:12, 0:PAIR]
    for i in range(SL):
        m.kv[i, s] = turned(kv_pre[i * SPAN : (i + 1) * SPAN, :], key_tables).astype(BF)
    gather = []
    for d in range(1, NS):
        up_to = lax.rem(s + d, NS)
        copy = links.copy(m.kv.at[:, s], m.kv.at[:, s], seq_device(up_to))
        sends = s + d < NS
        gets = s - d >= 0
        gather.append((copy, sends, gets))

        @pl.when(sends)
        def _(copy=copy):
            copy.start()

        links.waits.append((sends, copy))

    load_wq.wait()
    load_wout.wait()
    for i in range(SL):
        rows = slice(i * SPAN, (i + 1) * SPAN)
        q_pre = dot(m.ain[rows, :], m.wq[...]) + pars[4:5, :]
        back = dot(m.g2[rows, :], m.wout[...], 1, 1)
        for p in range(z.PAIRS):
            hg, at = p // PG, (p % PG) * SPAN
            cols = slice(p * PAIR, (p + 1) * PAIR)
            q = turned(q_pre[:, cols], tables)
            a = back[:, cols]
            m.l1[hg, i, at : at + SPAN, :] = jnp.where(low, q, 0.0).astype(BF)
            m.l2[hg, i, PR + at : PR + at + SPAN, :] = jnp.where(low, 0.0, q).astype(BF)
            m.l2[hg, i, at : at + SPAN, :] = jnp.where(low, a, 0.0).astype(BF)
            m.l1[hg, i, PR + at : PR + at + SPAN, :] = jnp.where(low, 0.0, a).astype(BF)

    load_wup.wait()
    load_wdn.wait()
    m.sv[0] = jnp.zeros((8, D), F32)
    low_bits = list(range(BS - 1))
    turned_bits = low_bits[1:] + low_bits[:1]
    seq_stage = lambda b: (bit_of(s, b), (flip(s, b), j))
    slot_stage = lambda b: (bit_of(j, b), (s, flip(j, b)))
    dn_first = [
        [
            Halving(
                links,
                m.dn.at[k, p],
                [slot_stage(b) for b in range(BJ - 1, 0, -1)],
                m.dnr.at[k, p],
            )
            for p in range(2)
        ]
        for k in range(z.CH)
    ]
    up_order = [(low_bits if k % 2 == 0 else turned_bits) + [BS - 1] for k in range(z.CH)]
    ups = [
        Halving(links, m.up.at[k], [seq_stage(b) for b in up_order[k]], m.upr.at[k])
        for k in range(z.CH)
    ]

    RB = 256

    def bias_of(at):
        row, col = at // D, at % D
        if col + CW <= D:
            return pars[7 + row : 8 + row, col : col + CW]
        return jnp.concatenate(
            [pars[7 + row : 8 + row, col:], pars[8 + row : 9 + row, : col + CW - D]], axis=1
        )

    def feed(k, first, last):
        cols = slice(k * CW, (k + 1) * CW)
        bias = jnp.where(c == 0, bias_of(k * CW), bias_of(k * CW + HF))

        def block(i, total):
            rows = pl.ds(pl.multiple_of(i * RB, RB), RB)
            up = dot(m.mlp2[rows, :], m.wup[:, cols]) + bias
            back = dot(m.g2[rows, :], m.wdn[cols, :], 1, 1)
            a, slope = gelu_pair(up)
            back = back * slope
            m.act[rows, cols] = a.astype(BF)
            m.dup[rows, cols] = back.astype(BF)
            return total + jnp.sum(back, axis=0, keepdims=True)

        return lax.fori_loop(first, last, block, jnp.zeros((1, CW), F32))

    def feed_grads(k):
        cols = slice(k * CW, (k + 1) * CW)
        part = dot(m.act[:, cols], m.g2[...], 0, 0).astype(BF)
        for p in range(2):
            for q in range(QN):
                m.dn[k, p, q] = part[p * z.FRH : (p + 1) * z.FRH, q * z.DW : (q + 1) * z.DW]
            dn_first[k][p].start(0)
        part = dot(m.mlp2[...], m.dup[:, cols], 0, 0).astype(BF)
        for n in range(NS):
            m.up[k, placed(n, up_order[k])] = part[n * R : (n + 1) * R, :]
        ups[k].start(0)

    halfway = ROWS // RB
    totals = []
    for k in range(z.CH):
        total = feed(k, 0, halfway)
        if k == 0:
            got_m.wait()
            got_g.wait()
        totals.append(total + feed(k, halfway, 2 * halfway))
        feed_grads(k)
    total = jnp.concatenate(totals, axis=1)
    for q in range(z.FF // D):
        piece = total[:, (q * D) % HF : (q * D) % HF + D]
        m.sv[0, q : q + 1, :] = jnp.where(c == (q * D) // HF, piece, 0.0)

    kept = rank
    dn_levels, at = [], 0
    for l in range(BS - 1):
        level = []
        for n in range(z.CH >> (l + 1)):
            base = n * 2 ** (l + 1) + lax.rem(s, 2**l)
            mine = bit_of(s, l)
            keep = base + mine * 2**l
            give = base + (1 - mine) * 2**l
            for p in range(2):
                copy = links.copy(m.dn.at[give, p, kept], m.dnr2.at[at], (flip(s, l), j))
                level.append((copy, keep, p, at, n))
                at += 1
        dn_levels.append(level)

    def dn_start(l, n):
        for copy, keep, p, at, group in dn_levels[l]:
            if group == n:
                copy.start()
                links.waits.append(copy)

    def dn_finish(l, n):
        for copy, keep, p, at, group in dn_levels[l]:
            if group == n:
                copy.wait_recv()
                m.dn[keep, p, kept] = m.dn[keep, p, kept] + m.dnr2[at]

    dn_arrivals = links.take(4)

    def dn_last():
        mine = lax.rem(s, z.CH)
        for p in range(2):
            part = m.dn[mine, p, kept]
            for h in range(2):
                m.dnm[2 * p + h] = part[:, h * (z.DW // 2) : (h + 1) * (z.DW // 2)]
                links.unless(
                    jnp.logical_and(ts == c, c == h),
                    m.dnm.at[2 * p + h],
                    m.dnf.at[p, ts],
                    (put(s, BS - 1, c), put(j, 0, h)),
                    dn_arrivals + 2 * p + ts,
                )()

    up_arrivals = links.take(z.CPP * QN)

    def up_end(k):
        piece, n = (k * CW) // z.W, k % z.CPP
        target = c * QN + piece
        return links.unless(
            target == j,
            m.up.at[k, ups[k].end],
            m.upf.at[n, rank],
            (s, target),
            up_arrivals + n * QN + rank,
        )

    up_last = [up_end(k) for k in range(z.CH)]

    dkvs = [
        Halving(links, m.dks.at[i], [seq_stage(b) for b in range(BS)], m.dkr.at[i])
        for i in range(SL)
    ]
    pos = [placed(n, list(range(BS))) for n in range(NS)]
    coef = scale * math.log2(math.e)
    key_spot = lax.broadcasted_iota(jnp.int32, (SPAN, LEN), 1)
    row_spot = s * SPAN + lax.broadcasted_iota(jnp.int32, (SPAN, LEN), 0)

    def attend(hg, i):
        kv = m.kv[i].reshape(LEN, PAIR)
        m.kvs[...] = kv
        m.vks[...] = pltpu.roll(kv.astype(F32), HEAD, 1).astype(BF)
        length = jnp.int32(0)
        for n in range(SL):
            length = jnp.where(i == n, lens[n], length)
        allowed = jnp.logical_and(key_spot <= row_spot, key_spot < length)
        m.bias[...] = jnp.where(allowed, 0.0, -1e9)
        sides = (m.kvs, m.vks)
        rows = pl.ds(pl.multiple_of(i * SPAN, SPAN), SPAN)
        step = z.STEP
        d_key = d_value = None
        for first in range(0, PG, step):
            count = step * SPAN
            even = slice(first * SPAN, first * SPAN + count)
            odd = slice(PR + first * SPAN, PR + first * SPAN + count)
            halves = (slice(0, count), slice(count, 2 * count))
            q = (m.l1[hg, i, even, :], m.l2[hg, i, odd, :])
            a = (m.l2[hg, i, even, :], m.l1[hg, i, odd, :])
            mask = jnp.concatenate([m.bias[...]] * step, axis=0)
            mixed, dqs = {}, {}
            for group in ((0, 1),) if LEN <= 1024 else ((0,), (1,)):
                raw = {e: dot(q[e], sides[e][...], 1, 1) for e in group}
                dps = {e: dot(a[e], sides[1 - e][...], 1, 1) for e in group}
                probs = {}
                for e in group:
                    score = raw[e] * coef + mask
                    w = jnp.exp2(score - jnp.max(score, axis=-1, keepdims=True))
                    probs[e] = w * (1.0 / jnp.sum(w, axis=-1, keepdims=True))
                for e in group:
                    rounded = probs[e].astype(BF)
                    mixed[e] = dot(rounded, sides[1 - e][...])
                    (m.r2 if e == 0 else m.r1)[halves[e], :] = rounded
                for e in group:
                    pd = probs[e] * dps[e]
                    ds = (pd - probs[e] * jnp.sum(pd, axis=-1, keepdims=True)).astype(BF)
                    (m.r1 if e == 0 else m.r2)[halves[e], :] = ds
                    dqs[e] = dot(ds, sides[e][...])
            for p in range(step):
                at = slice(p * SPAN, (p + 1) * SPAN)
                n = hg * PG + first + p
                cols = slice(n * PAIR, (n + 1) * PAIR)
                m.att[rows, cols] = jnp.where(low, mixed[0][at], mixed[1][at]).astype(BF)
                dq = jnp.where(low, dqs[0][at], dqs[1][at]) * scale
                m.dq[rows, cols] = turned_back(dq, tables).astype(BF)
            if step == PG:
                one = dot(m.l1[hg, i], m.r1[...], 0, 0)
                two = dot(m.l2[hg, i], m.r2[...], 0, 0)
            else:
                one = dot(m.l1[hg, i, even, :], m.r1[halves[0], :], 0, 0)
                one = one + dot(m.l1[hg, i, odd, :], m.r1[halves[1], :], 0, 0)
                two = dot(m.l2[hg, i, even, :], m.r2[halves[0], :], 0, 0)
                two = two + dot(m.l2[hg, i, odd, :], m.r2[halves[1], :], 0, 0)
            key_part = one[:HEAD] + two[HEAD:]
            value_part = one[HEAD:] + two[:HEAD]
            d_key = key_part if d_key is None else d_key + key_part
            d_value = value_part if d_value is None else d_value + value_part
        d_key = d_key * scale
        return jnp.concatenate([d_key, d_value], axis=0)

    def hooked(hooks, i):
        for n, steps in hooks.items():

            @pl.when(i == n)
            def _(steps=steps):
                for step in steps:
                    step()

    kv_in = []
    for copy, sends, gets in gather:

        @pl.when(gets)
        def _(copy=copy):
            copy.wait_recv()

    def up_step(k, n):
        return lambda: ups[k].step(n)

    def dn_y(k):
        def go():
            for p in range(2):
                for n in range(BJ - 1):
                    dn_first[k][p].finish(n)
                    if n + 1 < BJ - 1:
                        dn_first[k][p].start(n + 1)

        return go

    early = {n: [] for n in range(SL)}
    late = {n: [] for n in range(SL)}
    tail = []
    plan = [early[n] for n in range(SL)] + [late[n] for n in range(SL)] + [tail]

    def at_point(n, step):
        plan[min(n, 2 * SL)].append(step)

    for k in range(z.CH):
        for n in range(1, BS + 1):
            at_point(k // 2 + 2 * (n - 1) if BS == 3 else 2 * SL, up_step(k, n))
        at_point(k // 2 + 2 * BS - 2 if BS == 3 else 2 * SL, lambda k=k: up_last[k]())
    for k in range(z.CH):
        at_point(1 + k if BS == 3 else 2 * SL, dn_y(k))
        if k % 2 == 1:
            at_point(1 + k if BS == 3 else 2 * SL, lambda k=k: dn_start(0, k // 2))
    for l in range(BS - 1):
        for n in range(z.CH >> (l + 1)):
            point = (5 + 2 * n if l == 0 else 8) if BS == 3 else 2 * SL
            at_point(point, lambda l=l, n=n: dn_finish(l, n))
            if l + 1 < BS - 1 and n % 2 == 1:
                at_point(point, lambda l=l, n=n: dn_start(l + 1, n // 2))
    at_point(2 * SL, dn_last)

    def early_body(i, _):
        m.dkt[i] = attend(0, i).astype(m.dkt.dtype)
        hooked(early, i)
        return 0

    lax.fori_loop(0, SL, early_body, 0)

    wo_order = [turned_bits, low_bits]
    wo_pipes = [
        Halving(
            links,
            m.wo.at[hg],
            [slot_stage(0)] + [seq_stage(b) for b in wo_order[hg]],
            m.wor.at[hg],
        )
        for hg in range(2)
    ]
    gq_order = [low_bits + [BS - 1], turned_bits + [BS - 1]]
    gq_pipes = [
        Halving(
            links,
            m.gq.at[hg],
            [slot_stage(0)] + [seq_stage(b) for b in gq_order[hg]],
            m.gqr.at[hg],
        )
        for hg in range(2)
    ]
    gq_arrivals = links.take(NJ)

    def project(hg):
        cols = slice(hg * (D // 2), (hg + 1) * (D // 2))
        part = dot(m.att[:, cols], m.g2[0:ROWS, :], 0, 0).astype(BF)
        for n in range(NS // 2):
            for r in range(2):
                at = n * R + r * R2
                m.wo[hg, r * (NS // 2) + placed(n, wo_order[hg])] = part[at : at + R2, :]
        wo_pipes[hg].start(0)
        part = dot(m.ain[...], m.dq[:, cols], 0, 0).astype(BF)
        for n in range(NS):
            for r in range(2):
                at = n * R + r * R2
                m.gq[hg, r * NS + placed(n, gq_order[hg])] = part[at : at + R2, :]
        gq_pipes[hg].start(0)

    wo_direct = [
        Direct(links, NJ, j, slot_device, lambda n, hg=hg: m.wos.at[hg, n], m.wof.at[hg])
        for hg in range(2)
    ]

    def wo_last(hg):
        part = m.wo[hg, wo_pipes[hg].end]
        for n in range(NJ):
            m.wos[hg, n] = part[:, n * C4 : (n + 1) * C4]
        m.wof[hg, j] = m.wos[hg, j]
        wo_direct[hg].start()

    def wo_sum(hg):
        wo_direct[hg].finish()
        for r in range(2):
            total = m.wof[hg, r].astype(F32)
            for n in range(1, QN):
                total = total + m.wof[hg, 2 * n + r].astype(F32)
            m.wox[hg, r] = total

    def gq_last(hg):
        part = m.gq[hg, gq_pipes[hg].end]
        for n in range(QN):
            m.gqs[hg, n] = part[:, n * C4 : (n + 1) * C4]
            target = hg * QN + n
            links.unless(
                target == j, m.gqs.at[hg, n], m.gqf.at[j], (s, target), gq_arrivals + j
            )()

    project(0)
    small = BS == 3
    if small:
        late[0] += [lambda: wo_pipes[0].step(1), lambda: gq_pipes[0].step(1)]
        late[2] += [lambda: wo_pipes[0].step(2), lambda: gq_pipes[0].step(2)]
        late[3] += [lambda: wo_pipes[0].step(3), lambda: gq_pipes[0].step(3)]
        late[3] += [lambda: wo_last(0)]
        tail += [lambda: gq_pipes[0].step(4), lambda: gq_last(0)]
    else:
        for n in range(1, BS + 1):
            tail += [lambda n=n: wo_pipes[0].step(n)]
        tail += [lambda: wo_last(0)]
        for n in range(1, BS + 2):
            tail += [lambda n=n: gq_pipes[0].step(n)]
        tail += [lambda: gq_last(0)]
    for i in range(SL):
        for n in range(1, BS + 1):
            if i + n < SL:
                late[i + n] += [lambda i=i, n=n: dkvs[i].step(n)]

    def late_body(i, _):
        total = (m.dkt[i] + attend(1, i)).astype(BF)
        for n in range(NS):
            m.dks[i, pos[n]] = total[:, n * SPAN : (n + 1) * SPAN]
        for n in range(SL):

            @pl.when(i == n)
            def _(n=n):
                dkvs[n].start(0)

        hooked(late, i)
        return 0

    lax.fori_loop(0, SL, late_body, 0)

    left = []
    for i in range(SL):
        for n in range(1, BS + 1):
            if i + n >= SL:
                left.append((i + n - SL, lambda i=i, n=n: dkvs[i].step(n)))

    def dkv_round(r):
        for at, step in left:
            if at == r:
                step()

    project(1)
    dkv_round(0)
    for step in tail:
        step()
    for k in range(halfway):
        rows = slice(ROWS + k * RB, ROWS + (k + 1) * RB)
        here = slice(k * RB, (k + 1) * RB)
        msend[here, :] = dot(m.act[rows, :], m.wdn[...]).astype(BF)
    for k in range(halfway):
        rows = slice(ROWS + k * RB, ROWS + (k + 1) * RB)
        here = slice(k * RB, (k + 1) * RB)
        dsend[here, :] = dot(m.dup[rows, :], m.wup[...], 1, 1).astype(BF)
    got_out = links.start(msend, mrecv, buddy)
    got_back = links.start(dsend, drecv, buddy)
    wo_pipes[1].step(1)
    gq_pipes[1].step(1)
    dkv_round(1)
    for k in range(halfway):
        here = slice(k * RB, (k + 1) * RB)
        m.own_mlp[here, :] = dot(m.act[here, :], m.wdn[...]) + dot(m.att[here, :], m.wout[...])
        m.own_d[here, :] = dot(m.dup[here, :], m.wup[...], 1, 1).astype(m.own_d.dtype)
    got_out.wait_recv()
    got_back.wait_recv()
    dkv_round(2)
    for step in range(2, BS + 1):
        wo_pipes[1].step(step)
        gq_pipes[1].step(step)
    wo_last(1)

    def normed(rows):
        v = m.x[rows, :].astype(F32)
        v = v - jnp.mean(v, axis=-1, keepdims=True)
        inv = lax.rsqrt(jnp.mean(v * v, axis=-1, keepdims=True) + 1e-05)
        return v * inv, inv

    g_sum = jnp.zeros((1, D), F32)
    gain_two = jnp.zeros((1, D), F32)
    shift_two = jnp.zeros((1, D), F32)
    out_copies = []
    for i in range(SL):
        rows = slice(i * SPAN, (i + 1) * SPAN)
        total = m.x[rows, :].astype(F32) + m.own_mlp[rows, :] + mrecv[rows, :].astype(F32)
        total = total + (pars[5:6, :] + pars[6:7, :])
        mrecv[rows, :] = jnp.where(spot < lens[i], total, 0.0).astype(BF)
        d_mlp = m.own_d[rows, :] + drecv[rows, :].astype(F32)
        unit, _ = normed(rows)
        gain_two = gain_two + jnp.sum(d_mlp * unit, axis=0, keepdims=True)
        shift_two = shift_two + jnp.sum(d_mlp, axis=0, keepdims=True)
        m.own_d[rows, :] = (d_mlp * pars[2:3, :]).astype(m.own_d.dtype)
        g_sum = g_sum + jnp.sum(m.g2[rows, :].astype(F32), axis=0, keepdims=True)
    copy = pltpu.make_async_copy(mrecv, o_lo, m.lsem.at[8])
    copy.start()
    out_copies.append(copy)
    m.sv[0, 4:5, :] = gain_two
    m.sv[0, 5:6, :] = shift_two
    m.sv[0, 6:7, :] = g_sum
    sv_one = Direct(links, NJ, j, slot_device, lambda n: m.sv.at[0], m.sva)
    sv_two = Direct(links, NS, s, seq_device, lambda n: m.sv.at[1], m.svb)
    m.sva[j] = m.sv[0]
    sv_one.start()

    dkv_round(3)
    gq_pipes[1].step(BS + 1)
    gq_last(1)

    bkv = jnp.zeros((1, PAIR), F32)
    for i in range(SL):
        d_kv = jnp.transpose(m.dks[i, dkvs[i].end].astype(F32))
        d_kv = turned_back(d_kv, key_tables)
        bkv = bkv + jnp.sum(d_kv, axis=0, keepdims=True)
        m.kvs[i * SPAN : (i + 1) * SPAN, :] = d_kv.astype(BF)
    d_kv_pre = m.kvs[0:ROWS, :]
    part = dot(d_kv_pre, m.ain[...], 0, 0).astype(BF)
    for n in range(NJ):
        m.kgs[n] = part[n * z.KR : (n + 1) * z.KR, :]
    kg_one = Direct(links, NJ, j, slot_device, lambda n: m.kgs.at[n], m.kgf)
    kg_two = Direct(links, NS, s, seq_device, lambda n: m.kg2.at[n], m.kgx)
    m.kgf[j] = m.kgs[j]
    kg_one.start()

    gain_one = jnp.zeros((1, D), F32)
    shift_one = jnp.zeros((1, D), F32)
    bq = jnp.zeros((1, D), F32)
    for i in range(SL):
        rows = slice(i * SPAN, (i + 1) * SPAN)
        dq = m.dq[rows, :]
        bq = bq + jnp.sum(dq.astype(F32), axis=0, keepdims=True)
        d_in = dot(dq, m.wq[...], 1, 1) + dot(m.kvs[rows, :], m.wkv[...], 1, 1)
        unit, inv = normed(rows)
        gain_one = gain_one + jnp.sum(d_in * unit, axis=0, keepdims=True)
        shift_one = shift_one + jnp.sum(d_in, axis=0, keepdims=True)
        d_unit = d_in * pars[0:1, :] + m.own_d[rows, :]
        along = jnp.mean(d_unit * unit, axis=-1, keepdims=True)
        d_unit = d_unit - jnp.mean(d_unit, axis=-1, keepdims=True) - unit * along
        m.own_mlp[rows, :] = m.g2[rows, :].astype(F32) + d_unit * inv
    copy = pltpu.make_async_copy(m.own_mlp, o_gi, m.lsem.at[9])
    copy.start()
    out_copies.append(copy)
    m.sw[0] = jnp.zeros((24, 128), F32)
    for n in range(D // 128):
        cols = slice(n * 128, (n + 1) * 128)
        m.sw[0, n : n + 1, :] = gain_one[:, cols]
        m.sw[0, 6 + n : 7 + n, :] = shift_one[:, cols]
        m.sw[0, 12 + n : 13 + n, :] = bq[:, cols]
    m.sw[0, 18:19, :] = bkv
    sw_one = Direct(links, NJ, j, slot_device, lambda n: m.sw.at[0], m.swa)
    sw_two = Direct(links, NS, s, seq_device, lambda n: m.sw.at[1], m.swb)
    m.swa[j] = m.sw[0]
    sw_one.start()

    def summed(ref, size):
        total = ref[0].astype(F32)
        for n in range(1, size):
            total = total + ref[n].astype(F32)
        return total

    sv_one.finish()
    m.sv[1] = summed(m.sva, NJ)
    m.svb[s] = m.sv[1]
    sv_two.start()
    kg_one.finish()
    part = summed(m.kgf, NJ).astype(BF)
    for n in range(NS):
        m.kg2[n] = part[:, n * R : (n + 1) * R]
    m.kgx[s] = m.kg2[s]
    kg_two.start()
    sw_one.finish()
    m.sw[1] = summed(m.swa, NJ)
    m.swb[s] = m.sw[1]
    sw_two.start()

    wo_sum(0)
    wo_sum(1)
    for r in range(2):
        m.woy[0, r] = m.wox[1 - ts, r].astype(BF)
    wo_end = links.start(m.woy.at[0], m.woy.at[1], (flip(s, BS - 1), j))

    for n in range(z.CPP):
        for r in range(QN):
            links.arrived(m.upf.at[n, r], up_arrivals + n * QN + r)
        o_up[:, n * CW : (n + 1) * CW] = summed(m.upf.at[n], QN)
    for p in range(2):
        for t in range(2):
            links.arrived(m.dnf.at[p, t], dn_arrivals + 2 * p + t)
        o_dn[p * z.FRH : (p + 1) * z.FRH, :] = summed(m.dnf.at[p], 2)
    for n in range(NJ):
        links.arrived(m.gqf.at[n], gq_arrivals + n)
    for r in range(2):
        total = m.gqf[r].astype(F32)
        for n in range(1, QN):
            total = total + m.gqf[2 * n + r].astype(F32)
        o_wq[r * R2 : (r + 1) * R2, :] = total
    wo_end.wait_recv()
    for r in range(2):
        o_wo[r * R2 : (r + 1) * R2, :] = m.wox[ts, r] + m.woy[1, r].astype(F32)
    sv_two.finish()
    o_sv[...] = summed(m.svb, NS)
    kg_two.finish()
    o_wkv[...] = jnp.transpose(summed(m.kgx, NS))
    sw_two.finish()
    o_sw[...] = summed(m.swb, NS)
    for copy in out_copies:
        copy.wait()
    links.finish()


class Names:
    pass


def body(
    hidden_in, lengths, out_grad, ln1_gain, ln1_bias, ln2_gain, ln2_bias, w_query, b_query,
    w_keyval, b_keyval, w_out, b_out, w_up, b_up, w_down, b_down,
):
    SL, SPAN, D = hidden_in.shape
    FF = w_up.shape[1]
    z = Sizes(lax.axis_size("seq"), lax.axis_size("slot"), SL, SPAN, D, FF)
    pad = jnp.zeros((D - b_keyval.shape[0],), BF)
    pars = jnp.concatenate(
        [ln1_gain, ln1_bias, ln2_gain, ln2_bias, b_query, b_out, b_down, b_up, b_keyval, pad]
    )
    pars = pars.astype(F32).reshape(8 + FF // D, D)
    scratch = scratch_of(z)
    names = list(scratch)
    n_in, n_out = 10, 9

    def call(*refs):
        m = Names()
        for name, ref in zip(names, refs[n_in + n_out :]):
            setattr(m, name, ref)
        kernel(z, refs[:n_in], refs[n_in : n_in + n_out], m)

    anywhere = pl.BlockSpec(memory_space=pl.ANY)
    vmem = pl.BlockSpec(memory_space=pltpu.VMEM)
    shape = jax.ShapeDtypeStruct
    lo, gi, up, dn, wo, wq, wkv, sv, sw = pl.pallas_call(
        call,
        out_shape=[
            shape((z.ROWS, D), BF),
            shape((z.ROWS, D), F32),
            shape((z.R, z.W), F32),
            shape((z.CW, z.DW // 2), F32),
            shape((z.R, z.C4), F32),
            shape((z.R, z.C4), F32),
            shape((z.R, z.KR), F32),
            shape((8, D), F32),
            shape((24, 128), F32),
        ],
        in_specs=[
            anywhere,
            anywhere,
            pl.BlockSpec(memory_space=pltpu.SMEM),
            vmem,
            anywhere,
            anywhere,
            anywhere,
            anywhere,
            anywhere,
            anywhere,
        ],
        out_specs=[anywhere, anywhere] + [vmem] * 7,
        scratch_shapes=list(scratch.values()),
        compiler_params=pltpu.CompilerParams(
            collective_id=0, has_side_effects=True, vmem_limit_bytes=62 * 2**20
        ),
    )(
        hidden_in.reshape(z.ROWS, D),
        out_grad.reshape(z.ROWS, D),
        lengths,
        pars,
        w_query,
        w_keyval,
        w_out,
        w_up,
        w_down,
        jnp.asarray(rotary_tables(z.LEN)),
    )
    flat = sw.reshape(-1)
    b_down_grad = sv[6]
    return (
        lo.reshape(hidden_in.shape),
        gi.reshape(hidden_in.shape),
        flat[0:D],
        flat[D : 2 * D],
        sv[4],
        sv[5],
        wq,
        flat[2 * D : 3 * D],
        wkv,
        flat[3 * D : 3 * D + 2 * HEAD],
        wo,
        b_down_grad,
        up,
        sv[: FF // D].reshape(FF),
        dn,
        b_down_grad,
    )


def solution(mesh):
    rows, whole, cut = P("slot", "seq", None), P(), P("seq", "slot")
    return jax.shard_map(
        body,
        mesh=mesh,
        in_specs=(rows, P("slot"), rows) + (whole,) * 14,
        out_specs=(
            rows, rows, whole, whole, whole, whole, cut, whole, cut, whole, cut, whole, cut, whole,
            cut, whole,
        ),
        check_vma=False,
    )
```

```python
import math

import jax
import jax.numpy as jnp
import numpy as np
from jax import lax
from jax.experimental import pallas as pl
from jax.experimental.pallas import tpu as pltpu
from jax.sharding import PartitionSpec as P

HEAD = 64
ROT = 16
PAIR = 2 * HEAD
MESH = pl.DeviceIdType.MESH
BF = jnp.bfloat16
F32 = jnp.float32


def dot(a, b, ca=1, cb=0):
    return lax.dot_general(a, b, (((ca,), (cb,)), ((), ())), preferred_element_type=F32)


def gelu_pair(u):
    cdf = 0.5 * (1.0 + lax.erf(u * 0.7071067811865476))
    pdf = 0.3989422804014327 * jnp.exp(-0.5 * u * u)
    return u * cdf, cdf + u * pdf


def bit_of(value, bit):
    return lax.rem(lax.div(value, 2**bit), 2)


def flip(value, bit):
    return value + (1 - 2 * bit_of(value, bit)) * 2**bit


def put(value, bit, new):
    return value + (new - bit_of(value, bit)) * 2**bit


def placed(index, bits):
    at = 0
    for bit in bits:
        at = at * 2 + (index >> bit) % 2
    return at


def turned(value, tables):
    same, after, before = tables
    return value * same + pltpu.roll(value, PAIR - 8, 1) * after + pltpu.roll(value, 8, 1) * before


def turned_back(value, tables):
    same, after, before = tables
    return (
        value * same
        + pltpu.roll(value * after, 8, 1)
        + pltpu.roll(value * before, PAIR - 8, 1)
    )


def rotary_tables(length):
    half = ROT // 2
    inverse = (10000.0 ** (-(np.arange(half, dtype=np.float32) * 2.0 / ROT))).astype(np.float32)
    turns = np.arange(length, dtype=np.float32)[:, None] * inverse[None, :]
    cosine = np.cos(turns.astype(np.float64)).astype(np.float32)
    sine = np.sin(turns.astype(np.float64)).astype(np.float32)
    out = np.zeros((3, length, PAIR), np.float32)
    out[0] = 1.0
    for head in range(2):
        at = head * HEAD
        out[0, :, at : at + half] = cosine
        out[0, :, at + half : at + ROT] = cosine
        out[1, :, at : at + half] = -sine
        out[2, :, at + half : at + ROT] = sine
    return out


class Links:
    def __init__(self, send, recv):
        self.send, self.recv, self.used, self.waits = send, recv, 0, []

    def take(self, count=1):
        first = self.used
        self.used += count
        return first

    def copy(self, src, dst, device, arrival=None):
        k = self.take()
        return pltpu.make_async_remote_copy(
            src_ref=src,
            dst_ref=dst,
            send_sem=self.send.at[k],
            recv_sem=self.recv.at[k if arrival is None else arrival],
            device_id=device,
            device_id_type=MESH,
        )

    def start(self, src, dst, device):
        copy = self.copy(src, dst, device)
        copy.start()
        self.waits.append(copy)
        return copy

    def unless(self, own, src, dst, device, arrival):
        remote = self.copy(src, dst, device, arrival)
        local = pltpu.make_async_copy(src, dst, self.recv.at[arrival])
        other = jnp.logical_not(own)
        self.waits.append((other, remote))

        def start():
            @pl.when(own)
            def _():
                local.start()

            @pl.when(other)
            def _():
                remote.start()

        return start

    def arrived(self, dst, arrival):
        pltpu.make_async_copy(dst, dst, self.recv.at[arrival]).wait()

    def finish(self):
        for copy in self.waits:
            if isinstance(copy, tuple):

                @pl.when(copy[0])
                def _(copy=copy):
                    copy[1].wait_send()

            else:
                copy.wait_send()


class Halving:
    def __init__(self, links, cur, stages, recv):
        blocks = cur.shape[0]
        off, at = jnp.int32(0), 0
        self.cur, self.steps, self.links = cur, [], links
        for mine, partner in stages:
            blocks //= 2
            src = cur.at[pl.ds(off + (1 - mine) * blocks, blocks)]
            dst = recv.at[pl.ds(at, blocks)]
            off = off + mine * blocks
            self.steps.append((links.copy(src, dst, partner), dst, off, blocks))
            at += blocks
        self.end = off

    def start(self, k):
        self.steps[k][0].start()
        self.links.waits.append(self.steps[k][0])

    def finish(self, k):
        copy, recv, off, blocks = self.steps[k]
        cur = self.cur
        copy.wait_recv()

        def add(i, _):
            cur[off + i] = cur[off + i] + recv[i]
            return 0

        lax.fori_loop(0, blocks, add, 0)

    def step(self, k):
        if k:
            self.finish(k - 1)
        if k < len(self.steps):
            self.start(k)


class Direct:
    def __init__(self, links, size, me, device_of, source, dst):
        self.links, self.size, self.me, self.dst = links, size, me, dst
        self.source = source
        self.out = []
        for d in range(1, size):
            target = lax.rem(me + d, size)
            self.out.append(links.copy(source(target), dst.at[me], device_of(target)))

    def start(self):
        for copy in self.out:
            copy.start()
            self.links.waits.append(copy)

    def finish(self):
        for d in range(1, self.size):
            sender = lax.rem(self.me + self.size - d, self.size)
            self.out[d - 1].wait_recv()


class Sizes:
    def __init__(self, NS, NJ, SL, SPAN, D, FF):
        self.NS, self.NJ, self.SL, self.SPAN, self.D, self.FF = NS, NJ, SL, SPAN, D, FF
        self.BS, self.BJ = NS.bit_length() - 1, NJ.bit_length() - 1
        self.ROWS, self.LEN, self.HF = SL * SPAN, NS * SPAN, FF // 2
        self.QN = NJ // 2
        self.R, self.W = D // NS, FF // NJ
        self.CH = NS // 2
        self.CW = self.HF // self.CH
        self.CPP = self.W // self.CW
        self.FRH, self.DW = self.CW // 2, D // self.QN
        self.R2, self.C4 = self.R // 2, D // NJ
        self.PAIRS = D // PAIR
        self.PG = self.PAIRS // 2
        self.PR = self.PG * SPAN
        self.KR = PAIR // NJ
        self.STEP = self.PG if self.LEN <= 1024 else 1


def scratch_of(z):
    vm = pltpu.VMEM
    rows, d = z.ROWS, z.D
    return dict(
        pars=vm((8 + z.FF // d, d), F32),
        x=vm((rows, d), BF),
        g2=vm((2 * rows, d), BF),
        mlp2=vm((2 * rows, d), BF),
        ain=vm((rows, d), BF),
        wq=vm((d, d), BF),
        wkv=vm((d, PAIR), BF),
        wout=vm((d, d), BF),
        wup=vm((d, z.HF), BF),
        wdn=vm((z.HF, d), BF),
        tab=vm((3, z.SPAN, PAIR), F32),
        act=vm((2 * rows, z.HF), BF),
        dup=vm((2 * rows, z.HF), BF),
        l1=vm((2, z.SL, 2 * z.PR, PAIR), BF),
        l2=vm((2, z.SL, 2 * z.PR, PAIR), BF),
        att=vm((rows, d), BF),
        dq=vm((rows, d), BF),
        kv=vm((z.SL, z.NS, z.SPAN, PAIR), BF),
        kvs=vm((z.LEN, PAIR), BF),
        vks=vm((z.LEN, PAIR), BF),
        r1=vm((2 * z.STEP * z.SPAN, z.LEN), BF),
        r2=vm((2 * z.STEP * z.SPAN, z.LEN), BF),
        bias=vm((z.SPAN, z.LEN), F32),
        dkt=vm((z.SL, PAIR, z.LEN), F32 if z.LEN <= 1024 else BF),
        dks=vm((z.SL, z.NS, PAIR, z.SPAN), BF),
        dkr=vm((z.SL, z.NS - 1, PAIR, z.SPAN), BF),
        up=vm((z.CH, z.NS, z.R, z.CW), BF),
        upr=vm((z.CH, z.NS - 1, z.R, z.CW), BF),
        upf=vm((z.CPP, z.QN, z.R, z.CW), BF),
        dn=vm((z.CH, 2, z.QN, z.FRH, z.DW), BF),
        dnr=vm((z.CH, 2, z.QN - 1, z.FRH, z.DW), BF),
        dnr2=vm((2 * z.CH - 2, z.FRH, z.DW), BF),
        dnm=vm((4, z.FRH, z.DW // 2), BF),
        dnf=vm((2, 2, z.FRH, z.DW // 2), BF),
        wo=vm((2, z.NS, z.R2, d), BF),
        wor=vm((2, z.NS - 1, z.R2, d), BF),
        wos=vm((2, z.NJ, z.R2, z.C4), BF),
        wof=vm((2, z.NJ, z.R2, z.C4), BF),
        wox=vm((2, 2, z.R2, z.C4), F32),
        woy=vm((2, 2, z.R2, z.C4), BF),
        gq=vm((2, 2 * z.NS, z.R2, d // 2), BF),
        gqr=vm((2, 2 * z.NS - 1, z.R2, d // 2), BF),
        gqs=vm((2, z.QN, z.R2, z.C4), BF),
        gqf=vm((z.NJ, z.R2, z.C4), BF),
        kgs=vm((z.NJ, z.KR, d), BF),
        kgf=vm((z.NJ, z.KR, d), BF),
        kg2=vm((z.NS, z.KR, z.R), BF),
        kgx=vm((z.NS, z.KR, z.R), BF),
        sv=vm((2, 8, d), F32),
        sva=vm((z.NJ, 8, d), F32),
        svb=vm((z.NS, 8, d), F32),
        sw=vm((2, 24, 128), F32),
        swa=vm((z.NJ, 24, 128), F32),
        swb=vm((z.NS, 24, 128), F32),
        own_mlp=vm((rows, d), F32),
        own_d=vm((rows, d), F32 if z.LEN <= 1024 else BF),
        send=pltpu.SemaphoreType.DMA((48 * z.NS // 2,)),
        recv=pltpu.SemaphoreType.DMA((48 * z.NS // 2,)),
        lsem=pltpu.SemaphoreType.DMA((12,)),
    )


def kernel(z, ins, outs, m):
    x_hbm, g_hbm, lens = ins[:3]
    wq_hbm, wkv_hbm, wout_hbm, wup_hbm, wdn_hbm, tab_hbm = ins[3:9]
    vectors = ins[9:]
    o_lo, o_gi, o_up, o_dn, o_wo, o_wq, o_wkv, o_sv, o_sw = outs
    NS, NJ, BS, BJ, SL, SPAN, D, HF = z.NS, z.NJ, z.BS, z.BJ, z.SL, z.SPAN, z.D, z.HF
    ROWS, LEN, QN, R, R2, CW, C4, PG, PR = (
        z.ROWS, z.LEN, z.QN, z.R, z.R2, z.CW, z.C4, z.PG, z.PR,
    )
    links = Links(m.send, m.recv)
    s = lax.axis_index("seq")
    j = lax.axis_index("slot")
    c = bit_of(j, 0)
    ts = bit_of(s, BS - 1)
    rank = lax.div(j, 2)
    buddy = (s, flip(j, 0))
    scale = HEAD**-0.5

    def seq_device(n):
        return (n, j)

    def slot_device(n):
        return (s, n)

    def load(k, src, dst):
        copy = pltpu.make_async_copy(src, dst, m.lsem.at[k])
        copy.start()
        return copy

    load_x = load(0, x_hbm, m.x)
    load_g = load(1, g_hbm, m.g2.at[pl.ds(0, ROWS), :])
    load_tab = load(2, tab_hbm.at[:, pl.ds(pl.multiple_of(s * SPAN, SPAN), SPAN), :], m.tab)
    load_wkv = load(3, wkv_hbm, m.wkv)
    load_wq = load(4, wq_hbm, m.wq)
    load_wout = load(5, wout_hbm, m.wout)
    load_wup = load(6, wup_hbm.at[:, pl.ds(pl.multiple_of(c * HF, HF), HF)], m.wup)
    load_wdn = load(7, wdn_hbm.at[pl.ds(pl.multiple_of(c * HF, HF), HF), :], m.wdn)

    for i in range(SL):
        m.kv[i] = jnp.zeros((NS, SPAN, PAIR), BF)
    near = [seq_device(lax.rem(s + d, NS)) for d in range(1, NS)]
    near += [slot_device(lax.rem(j + d, NJ)) for d in range(1, NJ)]
    near += [(flip(s, BS - 1), flip(j, 0))]
    barrier = pltpu.get_barrier_semaphore()
    for device in near:
        pl.semaphore_signal(barrier, inc=1, device_id=device, device_id_type=MESH)

    pars = m.pars
    for n, vector in enumerate(vectors[:7]):
        pars[n : n + 1, :] = vector[...].astype(F32).reshape(1, D)
    wide = vectors[7][...].astype(F32).reshape(1, z.FF)
    for n in range(z.FF // D):
        pars[7 + n : 8 + n, :] = wide[:, n * D : (n + 1) * D]
    b_keyval = vectors[8][...].astype(F32).reshape(1, PAIR)
    spot = s * SPAN + lax.broadcasted_iota(jnp.int32, (SPAN, 1), 0)
    load_x.wait()
    load_g.wait()
    for i in range(SL):
        rows = slice(i * SPAN, (i + 1) * SPAN)
        v = m.x[rows, :].astype(F32)
        v = v - jnp.mean(v, axis=-1, keepdims=True)
        v = v * lax.rsqrt(jnp.mean(v * v, axis=-1, keepdims=True) + 1e-05)
        m.ain[rows, :] = (v * pars[0:1, :] + pars[1:2, :]).astype(BF)
        m.mlp2[rows, :] = (v * pars[2:3, :] + pars[3:4, :]).astype(BF)
        m.g2[rows, :] = jnp.where(spot < lens[i], m.g2[rows, :].astype(F32), 0.0).astype(BF)
    own, theirs = pl.ds(0, ROWS), pl.ds(ROWS, ROWS)
    msend, dsend = m.g2.at[theirs, :], m.act.at[theirs, pl.ds(0, D)]
    mrecv, drecv = m.mlp2.at[own, :], m.mlp2.at[theirs, :]
    got_m = links.copy(m.mlp2.at[own, :], m.mlp2.at[theirs, :], buddy)
    got_g = links.copy(m.g2.at[own, :], m.g2.at[theirs, :], buddy)

    lane = lax.broadcasted_iota(jnp.int32, (SPAN, PAIR), 1)
    low = lane < HEAD
    load_tab.wait()
    tables = (m.tab[0], m.tab[1], m.tab[2])
    key_tables = (
        jnp.where(low, tables[0], 1.0),
        jnp.where(low, tables[1], 0.0),
        jnp.where(low, tables[2], 0.0),
    )
    load_wkv.wait()
    kv_pre = dot(m.ain[...], m.wkv[...]) + b_keyval
    for i in range(SL):
        m.kv[i, s] = turned(kv_pre[i * SPAN : (i + 1) * SPAN, :], key_tables).astype(BF)
    pl.semaphore_wait(barrier, len(near))
    got_m.start()
    got_g.start()
    gather = []
    for d in range(1, NS):
        up_to = lax.rem(s + d, NS)
        copy = links.copy(m.kv.at[:, s], m.kv.at[:, s], seq_device(up_to))
        sends = s + d < NS
        gets = s - d >= 0
        gather.append((copy, sends, gets))

        @pl.when(sends)
        def _(copy=copy):
            copy.start()

        links.waits.append((sends, copy))

    load_wq.wait()
    load_wout.wait()
    for i in range(SL):
        rows = slice(i * SPAN, (i + 1) * SPAN)
        q_pre = dot(m.ain[rows, :], m.wq[...]) + pars[4:5, :]
        back = dot(m.g2[rows, :], m.wout[...], 1, 1)
        for p in range(z.PAIRS):
            hg, at = p // PG, (p % PG) * SPAN
            cols = slice(p * PAIR, (p + 1) * PAIR)
            q = turned(q_pre[:, cols], tables)
            a = back[:, cols]
            m.l1[hg, i, at : at + SPAN, :] = jnp.where(low, q, 0.0).astype(BF)
            m.l2[hg, i, PR + at : PR + at + SPAN, :] = jnp.where(low, 0.0, q).astype(BF)
            m.l2[hg, i, at : at + SPAN, :] = jnp.where(low, a, 0.0).astype(BF)
            m.l1[hg, i, PR + at : PR + at + SPAN, :] = jnp.where(low, 0.0, a).astype(BF)

    load_wup.wait()
    load_wdn.wait()
    m.sv[0] = jnp.zeros((8, D), F32)
    low_bits = list(range(BS - 1))
    turned_bits = low_bits[1:] + low_bits[:1]
    seq_stage = lambda b: (bit_of(s, b), (flip(s, b), j))
    slot_stage = lambda b: (bit_of(j, b), (s, flip(j, b)))
    dn_first = [
        [
            Halving(
                links,
                m.dn.at[k, p],
                [slot_stage(b) for b in range(BJ - 1, 0, -1)],
                m.dnr.at[k, p],
            )
            for p in range(2)
        ]
        for k in range(z.CH)
    ]
    up_order = [(low_bits if k % 2 == 0 else turned_bits) + [BS - 1] for k in range(z.CH)]
    ups = [
        Halving(links, m.up.at[k], [seq_stage(b) for b in up_order[k]], m.upr.at[k])
        for k in range(z.CH)
    ]

    RB = 256

    def bias_of(at):
        row, col = at // D, at % D
        if col + CW <= D:
            return pars[7 + row : 8 + row, col : col + CW]
        return jnp.concatenate(
            [pars[7 + row : 8 + row, col:], pars[8 + row : 9 + row, : col + CW - D]], axis=1
        )

    def feed(k, first, last):
        cols = slice(k * CW, (k + 1) * CW)
        bias = jnp.where(c == 0, bias_of(k * CW), bias_of(k * CW + HF))

        def block(i, total):
            rows = pl.ds(pl.multiple_of(i * RB, RB), RB)
            up = dot(m.mlp2[rows, :], m.wup[:, cols]) + bias
            back = dot(m.g2[rows, :], m.wdn[cols, :], 1, 1)
            a, slope = gelu_pair(up)
            back = back * slope
            m.act[rows, cols] = a.astype(BF)
            m.dup[rows, cols] = back.astype(BF)
            return total + jnp.sum(back, axis=0, keepdims=True)

        return lax.fori_loop(first, last, block, jnp.zeros((1, CW), F32))

    def feed_grads(k):
        cols = slice(k * CW, (k + 1) * CW)
        part = dot(m.act[:, cols], m.g2[...], 0, 0).astype(BF)
        for p in range(2):
            for q in range(QN):
                m.dn[k, p, q] = part[p * z.FRH : (p + 1) * z.FRH, q * z.DW : (q + 1) * z.DW]
            dn_first[k][p].start(0)
        part = dot(m.mlp2[...], m.dup[:, cols], 0, 0).astype(BF)
        for n in range(NS):
            m.up[k, placed(n, up_order[k])] = part[n * R : (n + 1) * R, :]
        ups[k].start(0)

    halfway = ROWS // RB
    totals = []
    for k in range(z.CH):
        total = feed(k, 0, halfway)
        if k == 0:
            got_m.wait()
            got_g.wait()
        totals.append(total + feed(k, halfway, 2 * halfway))
        feed_grads(k)
    total = jnp.concatenate(totals, axis=1)
    for q in range(z.FF // D):
        piece = total[:, (q * D) % HF : (q * D) % HF + D]
        m.sv[0, q : q + 1, :] = jnp.where(c == (q * D) // HF, piece, 0.0)

    kept = rank
    dn_levels, at = [], 0
    for l in range(BS - 1):
        level = []
        for n in range(z.CH >> (l + 1)):
            base = n * 2 ** (l + 1) + lax.rem(s, 2**l)
            mine = bit_of(s, l)
            keep = base + mine * 2**l
            give = base + (1 - mine) * 2**l
            for p in range(2):
                copy = links.copy(m.dn.at[give, p, kept], m.dnr2.at[at], (flip(s, l), j))
                level.append((copy, keep, p, at, n))
                at += 1
        dn_levels.append(level)

    def dn_start(l, n):
        for copy, keep, p, at, group in dn_levels[l]:
            if group == n:
                copy.start()
                links.waits.append(copy)

    def dn_finish(l, n):
        for copy, keep, p, at, group in dn_levels[l]:
            if group == n:
                copy.wait_recv()
                m.dn[keep, p, kept] = m.dn[keep, p, kept] + m.dnr2[at]

    dn_arrivals = links.take(4)

    def dn_last():
        mine = lax.rem(s, z.CH)
        for p in range(2):
            part = m.dn[mine, p, kept]
            for h in range(2):
                m.dnm[2 * p + h] = part[:, h * (z.DW // 2) : (h + 1) * (z.DW // 2)]
                links.unless(
                    jnp.logical_and(ts == c, c == h),
                    m.dnm.at[2 * p + h],
                    m.dnf.at[p, ts],
                    (put(s, BS - 1, c), put(j, 0, h)),
                    dn_arrivals + 2 * p + ts,
                )()

    up_arrivals = links.take(z.CPP * QN)

    def up_end(k):
        piece, n = (k * CW) // z.W, k % z.CPP
        target = c * QN + piece
        return links.unless(
            target == j,
            m.up.at[k, ups[k].end],
            m.upf.at[n, rank],
            (s, target),
            up_arrivals + n * QN + rank,
        )

    up_last = [up_end(k) for k in range(z.CH)]

    dkvs = [
        Halving(links, m.dks.at[i], [seq_stage(b) for b in range(BS)], m.dkr.at[i])
        for i in range(SL)
    ]
    pos = [placed(n, list(range(BS))) for n in range(NS)]
    coef = scale * math.log2(math.e)
    key_spot = lax.broadcasted_iota(jnp.int32, (SPAN, LEN), 1)
    row_spot = s * SPAN + lax.broadcasted_iota(jnp.int32, (SPAN, LEN), 0)

    def attend(hg, i):
        kv = m.kv[i].reshape(LEN, PAIR)
        m.kvs[...] = kv
        m.vks[...] = pltpu.roll(kv.astype(F32), HEAD, 1).astype(BF)
        length = jnp.int32(0)
        for n in range(SL):
            length = jnp.where(i == n, lens[n], length)
        allowed = jnp.logical_and(key_spot <= row_spot, key_spot < length)
        m.bias[...] = jnp.where(allowed, 0.0, -1e9)
        sides = (m.kvs, m.vks)
        rows = pl.ds(pl.multiple_of(i * SPAN, SPAN), SPAN)
        step = z.STEP
        d_key = d_value = None
        for first in range(0, PG, step):
            count = step * SPAN
            even = slice(first * SPAN, first * SPAN + count)
            odd = slice(PR + first * SPAN, PR + first * SPAN + count)
            halves = (slice(0, count), slice(count, 2 * count))
            q = (m.l1[hg, i, even, :], m.l2[hg, i, odd, :])
            a = (m.l2[hg, i, even, :], m.l1[hg, i, odd, :])
            mask = jnp.concatenate([m.bias[...]] * step, axis=0)
            mixed, dqs = {}, {}
            for group in ((0, 1),) if LEN <= 1024 else ((0,), (1,)):
                raw = {e: dot(q[e], sides[e][...], 1, 1) for e in group}
                dps = {e: dot(a[e], sides[1 - e][...], 1, 1) for e in group}
                probs = {}
                for e in group:
                    score = raw[e] * coef + mask
                    w = jnp.exp2(score - jnp.max(score, axis=-1, keepdims=True))
                    probs[e] = w * (1.0 / jnp.sum(w, axis=-1, keepdims=True))
                for e in group:
                    rounded = probs[e].astype(BF)
                    mixed[e] = dot(rounded, sides[1 - e][...])
                    (m.r2 if e == 0 else m.r1)[halves[e], :] = rounded
                for e in group:
                    pd = probs[e] * dps[e]
                    ds = (pd - probs[e] * jnp.sum(pd, axis=-1, keepdims=True)).astype(BF)
                    (m.r1 if e == 0 else m.r2)[halves[e], :] = ds
                    dqs[e] = dot(ds, sides[e][...])
            for p in range(step):
                at = slice(p * SPAN, (p + 1) * SPAN)
                n = hg * PG + first + p
                cols = slice(n * PAIR, (n + 1) * PAIR)
                m.att[rows, cols] = jnp.where(low, mixed[0][at], mixed[1][at]).astype(BF)
                dq = jnp.where(low, dqs[0][at], dqs[1][at]) * scale
                m.dq[rows, cols] = turned_back(dq, tables).astype(BF)
            if step == PG:
                one = dot(m.l1[hg, i], m.r1[...], 0, 0)
                two = dot(m.l2[hg, i], m.r2[...], 0, 0)
            else:
                one = dot(m.l1[hg, i, even, :], m.r1[halves[0], :], 0, 0)
                one = one + dot(m.l1[hg, i, odd, :], m.r1[halves[1], :], 0, 0)
                two = dot(m.l2[hg, i, even, :], m.r2[halves[0], :], 0, 0)
                two = two + dot(m.l2[hg, i, odd, :], m.r2[halves[1], :], 0, 0)
            key_part = one[:HEAD] + two[HEAD:]
            value_part = one[HEAD:] + two[:HEAD]
            d_key = key_part if d_key is None else d_key + key_part
            d_value = value_part if d_value is None else d_value + value_part
        d_key = d_key * scale
        return jnp.concatenate([d_key, d_value], axis=0)

    def hooked(hooks, i):
        for n, steps in hooks.items():

            @pl.when(i == n)
            def _(steps=steps):
                for step in steps:
                    step()

    kv_in = []
    for copy, sends, gets in gather:

        @pl.when(gets)
        def _(copy=copy):
            copy.wait_recv()

    def up_step(k, n):
        return lambda: ups[k].step(n)

    def dn_y(k):
        def go():
            for p in range(2):
                for n in range(BJ - 1):
                    dn_first[k][p].finish(n)
                    if n + 1 < BJ - 1:
                        dn_first[k][p].start(n + 1)

        return go

    early = {n: [] for n in range(SL)}
    late = {n: [] for n in range(SL)}
    tail = []
    plan = [early[n] for n in range(SL)] + [late[n] for n in range(SL)] + [tail]

    def at_point(n, step):
        plan[min(n, 2 * SL)].append(step)

    for k in range(z.CH):
        for n in range(1, BS + 1):
            at_point(k // 2 + 2 * (n - 1) if BS == 3 else 2 * SL, up_step(k, n))
        at_point(k // 2 + 2 * BS - 2 if BS == 3 else 2 * SL, lambda k=k: up_last[k]())
    for k in range(z.CH):
        at_point(1 + k if BS == 3 else 2 * SL, dn_y(k))
        if k % 2 == 1:
            at_point(1 + k if BS == 3 else 2 * SL, lambda k=k: dn_start(0, k // 2))
    for l in range(BS - 1):
        for n in range(z.CH >> (l + 1)):
            point = (5 + 2 * n if l == 0 else 8) if BS == 3 else 2 * SL
            at_point(point, lambda l=l, n=n: dn_finish(l, n))
            if l + 1 < BS - 1 and n % 2 == 1:
                at_point(point, lambda l=l, n=n: dn_start(l + 1, n // 2))
    at_point(2 * SL, dn_last)

    def early_body(i, _):
        m.dkt[i] = attend(0, i).astype(m.dkt.dtype)
        hooked(early, i)
        return 0

    lax.fori_loop(0, SL, early_body, 0)

    wo_order = [turned_bits, low_bits]
    wo_pipes = [
        Halving(
            links,
            m.wo.at[hg],
            [slot_stage(0)] + [seq_stage(b) for b in wo_order[hg]],
            m.wor.at[hg],
        )
        for hg in range(2)
    ]
    gq_order = [low_bits + [BS - 1], turned_bits + [BS - 1]]
    gq_pipes = [
        Halving(
            links,
            m.gq.at[hg],
            [slot_stage(0)] + [seq_stage(b) for b in gq_order[hg]],
            m.gqr.at[hg],
        )
        for hg in range(2)
    ]
    gq_arrivals = links.take(NJ)

    def project(hg):
        cols = slice(hg * (D // 2), (hg + 1) * (D // 2))
        part = dot(m.att[:, cols], m.g2[0:ROWS, :], 0, 0).astype(BF)
        for n in range(NS // 2):
            for r in range(2):
                at = n * R + r * R2
                m.wo[hg, r * (NS // 2) + placed(n, wo_order[hg])] = part[at : at + R2, :]
        wo_pipes[hg].start(0)
        part = dot(m.ain[...], m.dq[:, cols], 0, 0).astype(BF)
        for n in range(NS):
            for r in range(2):
                at = n * R + r * R2
                m.gq[hg, r * NS + placed(n, gq_order[hg])] = part[at : at + R2, :]
        gq_pipes[hg].start(0)

    wo_direct = [
        Direct(links, NJ, j, slot_device, lambda n, hg=hg: m.wos.at[hg, n], m.wof.at[hg])
        for hg in range(2)
    ]

    def wo_last(hg):
        part = m.wo[hg, wo_pipes[hg].end]
        for n in range(NJ):
            m.wos[hg, n] = part[:, n * C4 : (n + 1) * C4]
        m.wof[hg, j] = m.wos[hg, j]
        wo_direct[hg].start()

    def wo_sum(hg):
        wo_direct[hg].finish()
        for r in range(2):
            total = m.wof[hg, r].astype(F32)
            for n in range(1, QN):
                total = total + m.wof[hg, 2 * n + r].astype(F32)
            m.wox[hg, r] = total

    def gq_last(hg):
        part = m.gq[hg, gq_pipes[hg].end]
        for n in range(QN):
            m.gqs[hg, n] = part[:, n * C4 : (n + 1) * C4]
            target = hg * QN + n
            links.unless(
                target == j, m.gqs.at[hg, n], m.gqf.at[j], (s, target), gq_arrivals + j
            )()

    project(0)
    small = BS == 3
    if small:
        late[0] += [lambda: wo_pipes[0].step(1), lambda: gq_pipes[0].step(1)]
        late[2] += [lambda: wo_pipes[0].step(2), lambda: gq_pipes[0].step(2)]
        late[3] += [lambda: wo_pipes[0].step(3), lambda: gq_pipes[0].step(3)]
        late[3] += [lambda: wo_last(0)]
        tail += [lambda: gq_pipes[0].step(4), lambda: gq_last(0)]
    else:
        for n in range(1, BS + 1):
            tail += [lambda n=n: wo_pipes[0].step(n)]
        tail += [lambda: wo_last(0)]
        for n in range(1, BS + 2):
            tail += [lambda n=n: gq_pipes[0].step(n)]
        tail += [lambda: gq_last(0)]
    for i in range(SL):
        for n in range(1, BS + 1):
            if i + n < SL:
                late[i + n] += [lambda i=i, n=n: dkvs[i].step(n)]

    def late_body(i, _):
        total = (m.dkt[i] + attend(1, i)).astype(BF)
        for n in range(NS):
            m.dks[i, pos[n]] = total[:, n * SPAN : (n + 1) * SPAN]
        for n in range(SL):

            @pl.when(i == n)
            def _(n=n):
                dkvs[n].start(0)

        hooked(late, i)
        return 0

    lax.fori_loop(0, SL, late_body, 0)

    left = []
    for i in range(SL):
        for n in range(1, BS + 1):
            if i + n >= SL:
                left.append((i + n - SL, lambda i=i, n=n: dkvs[i].step(n)))

    def dkv_round(r):
        for at, step in left:
            if at == r:
                step()

    project(1)
    dkv_round(0)
    for step in tail:
        step()
    for k in range(halfway):
        rows = slice(ROWS + k * RB, ROWS + (k + 1) * RB)
        here = slice(k * RB, (k + 1) * RB)
        msend[here, :] = dot(m.act[rows, :], m.wdn[...]).astype(BF)
    for k in range(halfway):
        rows = slice(ROWS + k * RB, ROWS + (k + 1) * RB)
        here = slice(k * RB, (k + 1) * RB)
        dsend[here, :] = dot(m.dup[rows, :], m.wup[...], 1, 1).astype(BF)
    got_out = links.start(msend, mrecv, buddy)
    got_back = links.start(dsend, drecv, buddy)
    wo_pipes[1].step(1)
    gq_pipes[1].step(1)
    dkv_round(1)
    for k in range(halfway):
        here = slice(k * RB, (k + 1) * RB)
        m.own_mlp[here, :] = dot(m.act[here, :], m.wdn[...]) + dot(m.att[here, :], m.wout[...])
        m.own_d[here, :] = dot(m.dup[here, :], m.wup[...], 1, 1).astype(m.own_d.dtype)
    got_out.wait_recv()
    got_back.wait_recv()
    dkv_round(2)
    for step in range(2, BS + 1):
        wo_pipes[1].step(step)
        gq_pipes[1].step(step)
    wo_last(1)

    def normed(rows):
        v = m.x[rows, :].astype(F32)
        v = v - jnp.mean(v, axis=-1, keepdims=True)
        inv = lax.rsqrt(jnp.mean(v * v, axis=-1, keepdims=True) + 1e-05)
        return v * inv, inv

    g_sum = jnp.zeros((1, D), F32)
    gain_two = jnp.zeros((1, D), F32)
    shift_two = jnp.zeros((1, D), F32)
    out_copies = []
    for i in range(SL):
        rows = slice(i * SPAN, (i + 1) * SPAN)
        total = m.x[rows, :].astype(F32) + m.own_mlp[rows, :] + mrecv[rows, :].astype(F32)
        total = total + (pars[5:6, :] + pars[6:7, :])
        mrecv[rows, :] = jnp.where(spot < lens[i], total, 0.0).astype(BF)
        d_mlp = m.own_d[rows, :] + drecv[rows, :].astype(F32)
        unit, _ = normed(rows)
        gain_two = gain_two + jnp.sum(d_mlp * unit, axis=0, keepdims=True)
        shift_two = shift_two + jnp.sum(d_mlp, axis=0, keepdims=True)
        m.own_d[rows, :] = (d_mlp * pars[2:3, :]).astype(m.own_d.dtype)
        g_sum = g_sum + jnp.sum(m.g2[rows, :].astype(F32), axis=0, keepdims=True)
    copy = pltpu.make_async_copy(mrecv, o_lo, m.lsem.at[8])
    copy.start()
    out_copies.append(copy)
    m.sv[0, 4:5, :] = gain_two
    m.sv[0, 5:6, :] = shift_two
    m.sv[0, 6:7, :] = g_sum
    sv_one = Direct(links, NJ, j, slot_device, lambda n: m.sv.at[0], m.sva)
    sv_two = Direct(links, NS, s, seq_device, lambda n: m.sv.at[1], m.svb)
    m.sva[j] = m.sv[0]
    sv_one.start()

    dkv_round(3)
    gq_pipes[1].step(BS + 1)
    gq_last(1)

    bkv = jnp.zeros((1, PAIR), F32)
    for i in range(SL):
        d_kv = jnp.transpose(m.dks[i, dkvs[i].end].astype(F32))
        d_kv = turned_back(d_kv, key_tables)
        bkv = bkv + jnp.sum(d_kv, axis=0, keepdims=True)
        m.kvs[i * SPAN : (i + 1) * SPAN, :] = d_kv.astype(BF)
    d_kv_pre = m.kvs[0:ROWS, :]
    part = dot(d_kv_pre, m.ain[...], 0, 0).astype(BF)
    for n in range(NJ):
        m.kgs[n] = part[n * z.KR : (n + 1) * z.KR, :]
    kg_one = Direct(links, NJ, j, slot_device, lambda n: m.kgs.at[n], m.kgf)
    kg_two = Direct(links, NS, s, seq_device, lambda n: m.kg2.at[n], m.kgx)
    m.kgf[j] = m.kgs[j]
    kg_one.start()

    gain_one = jnp.zeros((1, D), F32)
    shift_one = jnp.zeros((1, D), F32)
    bq = jnp.zeros((1, D), F32)
    for i in range(SL):
        rows = slice(i * SPAN, (i + 1) * SPAN)
        dq = m.dq[rows, :]
        bq = bq + jnp.sum(dq.astype(F32), axis=0, keepdims=True)
        d_in = dot(dq, m.wq[...], 1, 1) + dot(m.kvs[rows, :], m.wkv[...], 1, 1)
        unit, inv = normed(rows)
        gain_one = gain_one + jnp.sum(d_in * unit, axis=0, keepdims=True)
        shift_one = shift_one + jnp.sum(d_in, axis=0, keepdims=True)
        d_unit = d_in * pars[0:1, :] + m.own_d[rows, :]
        along = jnp.mean(d_unit * unit, axis=-1, keepdims=True)
        d_unit = d_unit - jnp.mean(d_unit, axis=-1, keepdims=True) - unit * along
        m.own_mlp[rows, :] = m.g2[rows, :].astype(F32) + d_unit * inv
    copy = pltpu.make_async_copy(m.own_mlp, o_gi, m.lsem.at[9])
    copy.start()
    out_copies.append(copy)
    m.sw[0] = jnp.zeros((24, 128), F32)
    for n in range(D // 128):
        cols = slice(n * 128, (n + 1) * 128)
        m.sw[0, n : n + 1, :] = gain_one[:, cols]
        m.sw[0, 6 + n : 7 + n, :] = shift_one[:, cols]
        m.sw[0, 12 + n : 13 + n, :] = bq[:, cols]
    m.sw[0, 18:19, :] = bkv
    sw_one = Direct(links, NJ, j, slot_device, lambda n: m.sw.at[0], m.swa)
    sw_two = Direct(links, NS, s, seq_device, lambda n: m.sw.at[1], m.swb)
    m.swa[j] = m.sw[0]
    sw_one.start()

    def summed(ref, size):
        total = ref[0].astype(F32)
        for n in range(1, size):
            total = total + ref[n].astype(F32)
        return total

    sv_one.finish()
    m.sv[1] = summed(m.sva, NJ)
    m.svb[s] = m.sv[1]
    sv_two.start()
    kg_one.finish()
    part = summed(m.kgf, NJ).astype(BF)
    for n in range(NS):
        m.kg2[n] = part[:, n * R : (n + 1) * R]
    m.kgx[s] = m.kg2[s]
    kg_two.start()
    sw_one.finish()
    m.sw[1] = summed(m.swa, NJ)
    m.swb[s] = m.sw[1]
    sw_two.start()

    wo_sum(0)
    wo_sum(1)
    for r in range(2):
        m.woy[0, r] = m.wox[1 - ts, r].astype(BF)
    wo_end = links.start(m.woy.at[0], m.woy.at[1], (flip(s, BS - 1), j))

    for n in range(z.CPP):
        for r in range(QN):
            links.arrived(m.upf.at[n, r], up_arrivals + n * QN + r)
        o_up[:, n * CW : (n + 1) * CW] = summed(m.upf.at[n], QN)
    for p in range(2):
        for t in range(2):
            links.arrived(m.dnf.at[p, t], dn_arrivals + 2 * p + t)
        o_dn[p * z.FRH : (p + 1) * z.FRH, :] = summed(m.dnf.at[p], 2)
    for n in range(NJ):
        links.arrived(m.gqf.at[n], gq_arrivals + n)
    for r in range(2):
        total = m.gqf[r].astype(F32)
        for n in range(1, QN):
            total = total + m.gqf[2 * n + r].astype(F32)
        o_wq[r * R2 : (r + 1) * R2, :] = total
    wo_end.wait_recv()
    for r in range(2):
        o_wo[r * R2 : (r + 1) * R2, :] = m.wox[ts, r] + m.woy[1, r].astype(F32)
    sv_two.finish()
    o_sv[...] = summed(m.svb, NS)
    kg_two.finish()
    o_wkv[...] = summed(m.kgx, NS)
    sw_two.finish()
    o_sw[...] = summed(m.swb, NS)
    for copy in out_copies:
        copy.wait()
    links.finish()


class Names:
    pass


def body(
    hidden_in, lengths, out_grad, ln1_gain, ln1_bias, ln2_gain, ln2_bias, w_query, b_query,
    w_keyval, b_keyval, w_out, b_out, w_up, b_up, w_down, b_down,
):
    SL, SPAN, D = hidden_in.shape
    FF = w_up.shape[1]
    z = Sizes(lax.axis_size("seq"), lax.axis_size("slot"), SL, SPAN, D, FF)
    scratch = scratch_of(z)
    names = list(scratch)
    n_in, n_out = 18, 9

    def call(*refs):
        m = Names()
        for name, ref in zip(names, refs[n_in + n_out :]):
            setattr(m, name, ref)
        kernel(z, refs[:n_in], refs[n_in : n_in + n_out], m)

    anywhere = pl.BlockSpec(memory_space=pl.ANY)
    vmem = pl.BlockSpec(memory_space=pltpu.VMEM)
    shape = jax.ShapeDtypeStruct
    lo, gi, up, dn, wo, wq, wkv, sv, sw = pl.pallas_call(
        call,
        out_shape=[
            shape((z.ROWS, D), BF),
            shape((z.ROWS, D), F32),
            shape((z.R, z.W), F32),
            shape((z.CW, z.DW // 2), F32),
            shape((z.R, z.C4), F32),
            shape((z.R, z.C4), F32),
            shape((z.KR, z.R), F32),
            shape((8, D), F32),
            shape((24, 128), F32),
        ],
        in_specs=[anywhere, anywhere, pl.BlockSpec(memory_space=pltpu.SMEM)]
        + [anywhere] * 6
        + [vmem] * 9,
        out_specs=[anywhere, anywhere] + [vmem] * 7,
        scratch_shapes=list(scratch.values()),
        compiler_params=pltpu.CompilerParams(
            collective_id=0, has_side_effects=True, vmem_limit_bytes=62 * 2**20
        ),
    )(
        hidden_in.reshape(z.ROWS, D),
        out_grad.reshape(z.ROWS, D),
        lengths,
        w_query,
        w_keyval,
        w_out,
        w_up,
        w_down,
        jnp.asarray(rotary_tables(z.LEN)),
        ln1_gain,
        ln1_bias,
        ln2_gain,
        ln2_bias,
        b_query,
        b_out,
        b_down,
        b_up,
        b_keyval,
    )
    wide = (lo, gi, up, wo, wq)

    def hand_over(*refs):
        n = len(wide)
        sources, (dn, wkv, sv, sw) = refs[:n], refs[n : n + 4]
        targets, rest = refs[n + 4 : 2 * n + 4], refs[2 * n + 4 : 2 * n + 15]
        held, came, left = refs[2 * n + 15 : 3 * n + 15], refs[-2], refs[-1]
        copies = [
            (
                pltpu.make_async_copy(a, b, came.at[k]),
                pltpu.make_async_copy(b, c, left.at[k]),
            )
            for k, (a, b, c) in enumerate(zip(sources, held, targets))
        ]
        for copy, _ in copies:
            copy.start()
        o_dn, o_wkv, gain_one, shift_one, gain_two, shift_two, bq, bkv, bo, bup, bd = rest
        for at, ref in enumerate((gain_one, shift_one, bq)):
            parts = [sw[k : k + 1, :] for k in range(at * (D // 128), (at + 1) * (D // 128))]
            ref[...] = jnp.concatenate(parts, axis=1).reshape(D)
        bkv[...] = sw[18:19, :].reshape(PAIR)
        gain_two[...] = sv[4:5, :].reshape(D)
        shift_two[...] = sv[5:6, :].reshape(D)
        bo[...] = sv[6:7, :].reshape(D)
        bd[...] = sv[6:7, :].reshape(D)
        parts = [sv[k : k + 1, :] for k in range(FF // D)]
        bup[...] = jnp.concatenate(parts, axis=1).reshape(FF)
        o_dn[...] = jnp.transpose(dn[...])
        o_wkv[...] = wkv[...]
        for copy, out in copies:
            copy.wait()
            out.start()
        for _, out in copies:
            out.wait()

    lo, gi, up, wo, wq, dn, wkv, g1, s1, g2, s2, bq, bkv, bo, bup, bd = pl.pallas_call(
        hand_over,
        out_shape=[shape(v.shape, v.dtype) for v in wide]
        + [shape(dn.shape[::-1], F32), shape(wkv.shape, F32)]
        + [shape((n,), F32) for n in (D, D, D, D, D, PAIR, D, FF, D)],
        in_specs=[anywhere] * 5 + [vmem] * 4,
        out_specs=[anywhere] * 5 + [vmem] * 11,
        scratch_shapes=[pltpu.VMEM(v.shape, v.dtype) for v in wide]
        + [pltpu.SemaphoreType.DMA((5,)), pltpu.SemaphoreType.DMA((5,))],
    )(*wide, dn, wkv, sv, sw)
    return (
        lo.reshape(hidden_in.shape),
        gi.reshape(hidden_in.shape),
        g1, s1, g2, s2, wq, bq, wkv.T, bkv, wo, bo, up, bup, dn.T, bd,
    )


def solution(mesh):
    rows, whole, cut = P("slot", "seq", None), P(), P("seq", "slot")
    return jax.shard_map(
        body,
        mesh=mesh,
        in_specs=(rows, P("slot"), rows) + (whole,) * 14,
        out_specs=(
            rows, rows, whole, whole, whole, whole, cut, whole, cut, whole, cut, whole, cut, whole,
            cut, whole,
        ),
        check_vma=False,
    )
```

```python
import math

import jax
import jax.numpy as jnp
import numpy as np
from jax import lax
from jax.experimental import pallas as pl
from jax.experimental.pallas import tpu as pltpu
from jax.sharding import PartitionSpec as P

HEAD = 64
ROT = 16
DK_PLAN = {
    (0, 1): -2, (0, 2): -1, (0, 3): 1, (1, 1): -1, (1, 2): 2, (1, 3): 4,
    (2, 1): 1, (2, 2): 3, (2, 3): 5, (3, 1): 3, (3, 2): 5, (3, 3): 6,
}
PLAN = {
    "y0": 0, "y1": 0, "y2": 1, "y3": 2, "d00": 2, "d01": 4, "d10": 5, "dn0": 5, "cross": 2,
    "e10": 1, "e11": 3, "e00": 5, "ey": 7, "dn1": 7,
    "u01": 0, "u21": 1, "u02": 2, "u22": 3, "u11": 4, "u12": 5, "u03": 4, "u23": 5, "u13": 7,
}
PAIR = 2 * HEAD
MESH = pl.DeviceIdType.MESH
BF = jnp.bfloat16
F32 = jnp.float32


def dot(a, b, ca=1, cb=0):
    return lax.dot_general(a, b, (((ca,), (cb,)), ((), ())), preferred_element_type=F32)


def gelu_pair(u):
    cdf = 0.5 * (1.0 + lax.erf(u * 0.7071067811865476))
    pdf = 0.3989422804014327 * jnp.exp(-0.5 * u * u)
    return u * cdf, cdf + u * pdf


def bit_of(value, bit):
    return lax.rem(lax.div(value, 2**bit), 2)


def flip(value, bit):
    return value + (1 - 2 * bit_of(value, bit)) * 2**bit


def put(value, bit, new):
    return value + (new - bit_of(value, bit)) * 2**bit


def placed(index, bits):
    at = 0
    for bit in bits:
        at = at * 2 + (index >> bit) % 2
    return at


def turned(value, tables):
    same, after, before = tables
    return value * same + pltpu.roll(value, PAIR - 8, 1) * after + pltpu.roll(value, 8, 1) * before


def turned_back(value, tables):
    same, after, before = tables
    return (
        value * same
        + pltpu.roll(value * after, 8, 1)
        + pltpu.roll(value * before, PAIR - 8, 1)
    )


def rotary_tables(length):
    half = ROT // 2
    inverse = (10000.0 ** (-(np.arange(half, dtype=np.float32) * 2.0 / ROT))).astype(np.float32)
    turns = np.arange(length, dtype=np.float32)[:, None] * inverse[None, :]
    cosine = np.cos(turns.astype(np.float64)).astype(np.float32)
    sine = np.sin(turns.astype(np.float64)).astype(np.float32)
    out = np.zeros((3, length, PAIR), np.float32)
    out[0] = 1.0
    for head in range(2):
        at = head * HEAD
        out[0, :, at : at + half] = cosine
        out[0, :, at + half : at + ROT] = cosine
        out[1, :, at : at + half] = -sine
        out[2, :, at + half : at + ROT] = sine
    return out


class Links:
    def __init__(self, send, recv):
        self.send, self.recv, self.used, self.waits = send, recv, 0, []

    def take(self, count=1):
        first = self.used
        self.used += count
        return first

    def copy(self, src, dst, device, arrival=None):
        k = self.take()
        return pltpu.make_async_remote_copy(
            src_ref=src,
            dst_ref=dst,
            send_sem=self.send.at[k],
            recv_sem=self.recv.at[k if arrival is None else arrival],
            device_id=device,
            device_id_type=MESH,
        )

    def start(self, src, dst, device):
        copy = self.copy(src, dst, device)
        copy.start()
        self.waits.append(copy)
        return copy

    def unless(self, own, src, dst, device, arrival):
        remote = self.copy(src, dst, device, arrival)
        local = pltpu.make_async_copy(src, dst, self.recv.at[arrival])
        other = jnp.logical_not(own)
        self.waits.append((other, remote))

        def start():
            @pl.when(own)
            def _():
                local.start()

            @pl.when(other)
            def _():
                remote.start()

        return start

    def arrived(self, dst, arrival):
        pltpu.make_async_copy(dst, dst, self.recv.at[arrival]).wait()

    def finish(self):
        for copy in self.waits:
            if isinstance(copy, tuple):

                @pl.when(copy[0])
                def _(copy=copy):
                    copy[1].wait_send()

            else:
                copy.wait_send()


class Halving:
    def __init__(self, links, cur, stages, recv):
        blocks = cur.shape[0]
        off, at = jnp.int32(0), 0
        self.cur, self.steps, self.links = cur, [], links
        for mine, partner in stages:
            blocks //= 2
            src = cur.at[pl.ds(off + (1 - mine) * blocks, blocks)]
            dst = recv.at[pl.ds(at, blocks)]
            off = off + mine * blocks
            self.steps.append((links.copy(src, dst, partner), dst, off, blocks))
            at += blocks
        self.end = off

    def start(self, k):
        self.steps[k][0].start()
        self.links.waits.append(self.steps[k][0])

    def finish(self, k):
        copy, recv, off, blocks = self.steps[k]
        cur = self.cur
        copy.wait_recv()

        def add(i, _):
            cur[off + i] = cur[off + i] + recv[i]
            return 0

        lax.fori_loop(0, blocks, add, 0)

    def step(self, k):
        if k:
            self.finish(k - 1)
        if k < len(self.steps):
            self.start(k)


class Direct:
    def __init__(self, links, size, me, device_of, source, dst):
        self.links, self.size, self.me, self.dst = links, size, me, dst
        self.source = source
        self.out = []
        for d in range(1, size):
            target = lax.rem(me + d, size)
            self.out.append(links.copy(source(target), dst.at[me], device_of(target)))

    def start(self):
        for copy in self.out:
            copy.start()
            self.links.waits.append(copy)

    def finish(self):
        for d in range(1, self.size):
            sender = lax.rem(self.me + self.size - d, self.size)
            self.out[d - 1].wait_recv()


class Sizes:
    def __init__(self, NS, NJ, SL, SPAN, D, FF):
        self.NS, self.NJ, self.SL, self.SPAN, self.D, self.FF = NS, NJ, SL, SPAN, D, FF
        self.BS, self.BJ = NS.bit_length() - 1, NJ.bit_length() - 1
        self.ROWS, self.LEN, self.HF = SL * SPAN, NS * SPAN, FF // 2
        self.QN = NJ // 2
        self.R, self.W = D // NS, FF // NJ
        self.CH = self.G = NS // 2
        self.CW = self.HF // self.CH
        self.CPP = self.W // self.CW
        self.FRH, self.DW = self.CW // 2, D // self.QN
        self.R2, self.C4 = self.R // 2, D // NJ
        self.PAIRS = D // PAIR
        self.PG = self.PAIRS // 2
        self.PR = self.PG * SPAN
        self.KR = PAIR // NJ
        self.STEP = self.PG if self.LEN <= 1024 else 1


def scratch_of(z):
    vm = pltpu.VMEM
    rows, d = z.ROWS, z.D
    return dict(
        pars=vm((8 + z.FF // d, d), F32),
        x=vm((rows, d), BF),
        g2=vm((2 * rows, d), BF),
        mlp2=vm((2 * rows, d), BF),
        ain=vm((rows, d), BF),
        wq=vm((d, d), BF),
        wkv=vm((d, PAIR), BF),
        wout=vm((d, d), BF),
        wup=vm((d, z.HF), BF),
        wdn=vm((z.HF, d), BF),
        tab=vm((3, z.SPAN, PAIR), F32),
        act=vm((2 * rows, z.HF), BF),
        dup=vm((2 * rows, z.HF), BF),
        l1=vm((2, z.SL, 2 * z.PR, PAIR), BF),
        l2=vm((2, z.SL, 2 * z.PR, PAIR), BF),
        att=vm((rows, d), BF),
        dq=vm((rows, d), BF),
        kv=vm((z.SL, z.NS, z.SPAN, PAIR), BF),
        kvs=vm((z.LEN, PAIR), BF),
        vks=vm((z.LEN, PAIR), BF),
        r1=vm((2 * z.STEP * z.SPAN, z.LEN), BF),
        r2=vm((2 * z.STEP * z.SPAN, z.LEN), BF),
        bias=vm((z.SPAN, z.LEN), F32),
        dkt=vm((z.SL, PAIR, z.LEN), F32 if z.LEN <= 1024 else BF),
        dks=vm((z.SL, z.NS, PAIR, z.SPAN), BF),
        dkr=vm((z.SL, z.NS - 1, PAIR, z.SPAN), BF),
        up=vm((z.CH, z.NS, z.R, z.CW), BF),
        upr=vm((z.CH if z.CPP == 1 else z.CH // 2 + 1, z.NS - 1, z.R, z.CW), BF),
        upf=vm((z.QN, z.R, z.CW), BF),
        upy=vm((z.QN if z.CPP > 1 else 1, z.NS if z.CPP > 1 else 1, z.R, z.CW), BF),
        dn=vm((z.CH, 2, z.QN, z.FRH, z.DW), BF),
        dnr=vm((z.CH + 1, z.QN - 1, z.FRH, z.DW), BF),
        dnr2=vm((z.CH - 1, z.FRH, z.DW), BF),
        dnr3=vm((z.CH - 1, z.QN, z.FRH, z.DW), BF),
        dnm=vm((4, z.FRH, z.DW // 2), BF),
        dnf=vm((2, 2, z.FRH, z.DW // 2), BF),
        wo=vm((2, z.NS, z.R2, d), BF),
        wor=vm((2, z.G, z.R2, d), BF),
        woq=vm((2, z.G, z.R2, d), BF),
        wos=vm((2, z.NJ, z.R2, z.C4), BF),
        wof=vm((2 * z.NJ, z.R2, z.C4), BF),
        gq=vm((2, 2 * z.NS, z.R2, d // 2), BF),
        gqr=vm((2, z.NS, z.R2, d // 2), BF),
        gqq=vm((2, z.G, 2, z.R2, d // 2), BF),
        gqs=vm((2, 2 * z.QN, z.R2, z.C4), BF),
        gqf=vm((2 * z.NJ, z.R2, z.C4), BF),
        kgs=vm((z.NJ, z.KR, d), BF),
        kgf=vm((z.NJ, z.KR, d), BF),
        kg2=vm((z.NS, z.KR, z.R), BF),
        kgx=vm((z.NS, z.KR, z.R), BF),
        sv=vm((2, 8, d), F32),
        sva=vm((z.NJ, 8, d), F32),
        svb=vm((z.NS, 8, d), F32),
        sw=vm((2, 24, 128), F32),
        swa=vm((z.NJ, 24, 128), F32),
        swb=vm((z.NS, 24, 128), F32),
        own_mlp=vm((rows, d), F32),
        own_d=vm((rows, d), F32 if z.LEN <= 1024 else BF),
        send=pltpu.SemaphoreType.DMA((48 * z.NS // 2,)),
        recv=pltpu.SemaphoreType.DMA((48 * z.NS // 2,)),
        lsem=pltpu.SemaphoreType.DMA((12,)),
    )


def kernel(z, ins, outs, m):
    x_hbm, g_hbm, lens = ins[:3]
    wq_hbm, wkv_hbm, wout_hbm, wup_hbm, wdn_hbm, tab_hbm = ins[3:9]
    vectors = ins[9:]
    o_lo, o_gi, o_up, o_dn, o_wo, o_wq, o_wkv, o_sv, o_sw = outs
    NS, NJ, BS, BJ, SL, SPAN, D, HF = z.NS, z.NJ, z.BS, z.BJ, z.SL, z.SPAN, z.D, z.HF
    ROWS, LEN, QN, R, R2, CW, C4, PG, PR = (
        z.ROWS, z.LEN, z.QN, z.R, z.R2, z.CW, z.C4, z.PG, z.PR,
    )
    links = Links(m.send, m.recv)
    s = lax.axis_index("seq")
    j = lax.axis_index("slot")
    c = bit_of(j, 0)
    ts = bit_of(s, BS - 1)
    rank = lax.div(j, 2)
    buddy = (s, flip(j, 0))
    scale = HEAD**-0.5

    def seq_device(n):
        return (n, j)

    def slot_device(n):
        return (s, n)

    def load(k, src, dst):
        copy = pltpu.make_async_copy(src, dst, m.lsem.at[k])
        copy.start()
        return copy

    load_x = load(0, x_hbm, m.x)
    load_g = load(1, g_hbm, m.g2.at[pl.ds(0, ROWS), :])
    load_tab = load(2, tab_hbm.at[:, pl.ds(pl.multiple_of(s * SPAN, SPAN), SPAN), :], m.tab)
    load_wkv = load(3, wkv_hbm, m.wkv)
    load_wq = load(4, wq_hbm, m.wq)
    load_wout = load(5, wout_hbm, m.wout)
    load_wup = load(6, wup_hbm.at[:, pl.ds(pl.multiple_of(c * HF, HF), HF)], m.wup)
    load_wdn = load(7, wdn_hbm.at[pl.ds(pl.multiple_of(c * HF, HF), HF), :], m.wdn)

    for i in range(SL):
        m.kv[i] = jnp.zeros((NS, SPAN, PAIR), BF)
    near = [seq_device(lax.rem(s + d, NS)) for d in range(1, NS)]
    near += [slot_device(lax.rem(j + d, NJ)) for d in range(1, NJ)]
    near += [(flip(s, BS - 1), flip(j, 0))]
    barrier = pltpu.get_barrier_semaphore()
    for device in near:
        pl.semaphore_signal(barrier, inc=1, device_id=device, device_id_type=MESH)

    pars = m.pars
    for n, vector in enumerate(vectors[:7]):
        pars[n : n + 1, :] = vector[...].astype(F32).reshape(1, D)
    wide = vectors[7][...].astype(F32).reshape(1, z.FF)
    for n in range(z.FF // D):
        pars[7 + n : 8 + n, :] = wide[:, n * D : (n + 1) * D]
    b_keyval = vectors[8][...].astype(F32).reshape(1, PAIR)
    spot = s * SPAN + lax.broadcasted_iota(jnp.int32, (SPAN, 1), 0)
    load_x.wait()
    load_g.wait()
    for i in range(SL):
        rows = slice(i * SPAN, (i + 1) * SPAN)
        v = m.x[rows, :].astype(F32)
        v = v - jnp.mean(v, axis=-1, keepdims=True)
        v = v * lax.rsqrt(jnp.mean(v * v, axis=-1, keepdims=True) + 1e-05)
        m.ain[rows, :] = (v * pars[0:1, :] + pars[1:2, :]).astype(BF)
        m.mlp2[rows, :] = (v * pars[2:3, :] + pars[3:4, :]).astype(BF)
        m.g2[rows, :] = jnp.where(spot < lens[i], m.g2[rows, :].astype(F32), 0.0).astype(BF)
    own, theirs = pl.ds(0, ROWS), pl.ds(ROWS, ROWS)
    msend, dsend = m.g2.at[theirs, :], m.act.at[theirs, pl.ds(0, D)]
    mrecv, drecv = m.mlp2.at[own, :], m.mlp2.at[theirs, :]
    got_m = links.copy(m.mlp2.at[own, :], m.mlp2.at[theirs, :], buddy)
    got_g = links.copy(m.g2.at[own, :], m.g2.at[theirs, :], buddy)

    lane = lax.broadcasted_iota(jnp.int32, (SPAN, PAIR), 1)
    low = lane < HEAD
    load_tab.wait()
    tables = (m.tab[0], m.tab[1], m.tab[2])
    key_tables = (
        jnp.where(low, tables[0], 1.0),
        jnp.where(low, tables[1], 0.0),
        jnp.where(low, tables[2], 0.0),
    )
    load_wkv.wait()
    kv_pre = dot(m.ain[...], m.wkv[...]) + b_keyval
    for i in range(SL):
        m.kv[i, s] = turned(kv_pre[i * SPAN : (i + 1) * SPAN, :], key_tables).astype(BF)
    pl.semaphore_wait(barrier, len(near))
    got_m.start()
    got_g.start()
    inner = lax.rem(s, 2)
    outer = lax.div(s, 2)
    NO = NS // 2
    far, near_by = {}, {}
    for d in range(NO):
        gets = outer - d >= 0
        if d:
            sends = outer + d < NO
            there = seq_device(lax.rem(s + 2 * d, NS))
            far[d] = (links.copy(m.kv.at[:, s], m.kv.at[:, s], there), gets)

            @pl.when(sends)
            def _(d=d):
                far[d][0].start()

            links.waits.append((sends, far[d][0]))
            sends = gets
        else:
            sends, gets = inner == 0, inner == 1
        block = lax.rem(s - 2 * d + NS, NS)
        copy = links.copy(m.kv.at[:, block], m.kv.at[:, block], seq_device(flip(s, 0)))
        near_by[d] = (copy, sends, gets)
        links.waits.append((sends, copy))

    def pass_on(d):
        copy, sends, _ = near_by[d]

        @pl.when(sends)
        def _():
            if d:
                far[d][0].wait_recv()
            copy.start()

    pass_on(0)

    load_wq.wait()
    load_wout.wait()
    for i in range(SL):
        rows = slice(i * SPAN, (i + 1) * SPAN)
        q_pre = dot(m.ain[rows, :], m.wq[...]) + pars[4:5, :]
        back = dot(m.g2[rows, :], m.wout[...], 1, 1)
        for p in range(z.PAIRS):
            hg, at = p // PG, (p % PG) * SPAN
            cols = slice(p * PAIR, (p + 1) * PAIR)
            q = turned(q_pre[:, cols], tables)
            a = back[:, cols]
            m.l1[hg, i, at : at + SPAN, :] = jnp.where(low, q, 0.0).astype(BF)
            m.l2[hg, i, PR + at : PR + at + SPAN, :] = jnp.where(low, 0.0, q).astype(BF)
            m.l2[hg, i, at : at + SPAN, :] = jnp.where(low, a, 0.0).astype(BF)
            m.l1[hg, i, PR + at : PR + at + SPAN, :] = jnp.where(low, 0.0, a).astype(BF)

    load_wup.wait()
    load_wdn.wait()
    m.sv[0] = jnp.zeros((8, D), F32)
    low_bits = list(range(BS - 1))
    turned_bits = low_bits[1:] + low_bits[:1]
    seq_stage = lambda b: (bit_of(s, b), (flip(s, b), j))
    slot_stage = lambda b: (bit_of(j, b), (s, flip(j, b)))
    low_s = lax.rem(s, z.G)
    slot_stages = [slot_stage(b) for b in range(BJ - 1, 0, -1)]
    dn_first = [
        Halving(links, m.dn.at[k, 0], slot_stages, m.dnr.at[k]) for k in range(z.CH)
    ]
    dn_other = {}
    at = 0
    for l in range(BS - 2, -1, -1):
        for n in range(2**l):
            keep = lax.div(low_s, 2**l) * 2**l + n
            give = keep + (1 - 2 * bit_of(s, l)) * 2**l
            copy = links.copy(m.dn.at[give, 1], m.dnr3.at[at], (flip(s, l), j))
            dn_other[l, n] = (copy, keep, at)
            at += 1
    dn_second = Halving(links, m.dn.at[low_s, 1], slot_stages, m.dnr.at[z.CH])

    def other_start(l, n):
        dn_other[l, n][0].start()
        links.waits.append(dn_other[l, n][0])

    def other_finish(l, n):
        copy, keep, at = dn_other[l, n]
        copy.wait_recv()
        for q in range(QN):
            m.dn[keep, 1, q] = m.dn[keep, 1, q] + m.dnr3[at, q]

    up_order = [(low_bits if k % 2 == 0 else turned_bits) + [BS - 1] for k in range(z.CH)]
    crossing = [k for k in range(z.CH) if k % z.CPP == 1]
    staying = [k for k in range(z.CH) if k not in crossing]
    ups = {
        k: Halving(links, m.up.at[k], [seq_stage(b) for b in up_order[k]], m.upr.at[n])
        for n, k in enumerate(staying)
    }
    if crossing:
        stages = [seq_stage(b) for b in up_order[1]]
        ups[1] = Halving(links, m.upy.at[0], stages, m.upr.at[len(staying)])
    upy_arrivals = links.take(QN)
    crossings = {}
    for k in crossing:
        target = c * QN + (k * CW) // z.W
        crossings[k] = links.unless(
            target == j, m.up.at[k], m.upy.at[rank], (s, target), upy_arrivals + rank
        )

    def crossed():
        for n in range(QN):
            links.arrived(m.upy.at[n], upy_arrivals + n)

        def add(i, _):
            m.upy[0, i] = m.upy[0, i] + m.upy[1, i]
            return 0

        lax.fori_loop(0, NS, add, 0)
        ups[1].start(0)

    RB = 256

    def bias_of(at):
        row, col = at // D, at % D
        if col + CW <= D:
            return pars[7 + row : 8 + row, col : col + CW]
        return jnp.concatenate(
            [pars[7 + row : 8 + row, col:], pars[8 + row : 9 + row, : col + CW - D]], axis=1
        )

    def feed(k, first, last):
        cols = slice(k * CW, (k + 1) * CW)
        bias = jnp.where(c == 0, bias_of(k * CW), bias_of(k * CW + HF))

        def block(i, total):
            rows = pl.ds(pl.multiple_of(i * RB, RB), RB)
            up = dot(m.mlp2[rows, :], m.wup[:, cols]) + bias
            back = dot(m.g2[rows, :], m.wdn[cols, :], 1, 1)
            a, slope = gelu_pair(up)
            back = back * slope
            m.act[rows, cols] = a.astype(BF)
            m.dup[rows, cols] = back.astype(BF)
            return total + jnp.sum(back, axis=0, keepdims=True)

        return lax.fori_loop(first, last, block, jnp.zeros((1, CW), F32))

    def feed_grads(k):
        cols = slice(k * CW, (k + 1) * CW)
        part = dot(m.act[:, cols], m.g2[...], 0, 0).astype(BF)
        for p in range(2):
            for q in range(QN):
                m.dn[k, p, q] = part[p * z.FRH : (p + 1) * z.FRH, q * z.DW : (q + 1) * z.DW]
        dn_first[k].start(0)
        if 2 * k >= z.CH:
            other_start(BS - 2, k - z.CH // 2)
        part = dot(m.mlp2[...], m.dup[:, cols], 0, 0).astype(BF)
        for n in range(NS):
            m.up[k, placed(n, up_order[1 if k in crossing else k])] = part[n * R : (n + 1) * R, :]
        if k in crossing:
            crossings[k]()
        else:
            ups[k].start(0)

    halfway = ROWS // RB
    totals = []
    for k in range(z.CH):
        total = feed(k, 0, halfway)
        if k == 0:
            got_m.wait()
            got_g.wait()
        totals.append(total + feed(k, halfway, 2 * halfway))
        feed_grads(k)
        for d in range(1, NO):
            if (k == d if NO == 4 else k == z.CH - 1):
                pass_on(d)
    total = jnp.concatenate(totals, axis=1)
    for q in range(z.FF // D):
        piece = total[:, (q * D) % HF : (q * D) % HF + D]
        m.sv[0, q : q + 1, :] = jnp.where(c == (q * D) // HF, piece, 0.0)

    kept = rank
    dn_levels, at = {}, 0
    for l in range(BS - 1):
        for n in range(z.CH >> (l + 1)):
            base = n * 2 ** (l + 1) + lax.rem(s, 2**l)
            mine = bit_of(s, l)
            keep = base + mine * 2**l
            give = base + (1 - mine) * 2**l
            copy = links.copy(m.dn.at[give, 0, kept], m.dnr2.at[at], (flip(s, l), j))
            dn_levels[l, n] = (copy, keep, at)
            at += 1

    def dn_start(l, n):
        dn_levels[l, n][0].start()
        links.waits.append(dn_levels[l, n][0])

    def dn_finish(l, n):
        copy, keep, at = dn_levels[l, n]
        copy.wait_recv()
        m.dn[keep, 0, kept] = m.dn[keep, 0, kept] + m.dnr2[at]

    dn_arrivals = links.take(4)

    dn_ends = [
        [
            links.unless(
                jnp.logical_and(ts == c, c == h),
                m.dnm.at[2 * p + h],
                m.dnf.at[p, ts],
                (put(s, BS - 1, c), put(j, 0, h)),
                dn_arrivals + 2 * p + ts,
            )
            for h in range(2)
        ]
        for p in range(2)
    ]

    def dn_last(p):
        part = m.dn[low_s, p, kept]
        for h in range(2):
            m.dnm[2 * p + h] = part[:, h * (z.DW // 2) : (h + 1) * (z.DW // 2)]
            dn_ends[p][h]()

    up_arrivals = links.take(QN)

    def up_end(k):
        target = c * QN + (k * CW) // z.W
        return links.unless(
            target == j, m.up.at[k, ups[k].end], m.upf.at[rank], (s, target), up_arrivals + rank
        )

    up_last = {k: up_end(k) for k in range(z.CH) if k not in crossing}

    def group_device(n):
        return (ts * z.G + n, j)

    dk_bits = [
        (low_bits if i % 2 == 0 else turned_bits) + [BS - 1] for i in range(SL)
    ]
    dkvs = [
        Halving(links, m.dks.at[i], [seq_stage(b) for b in dk_bits[i]], m.dkr.at[i])
        for i in range(SL)
    ]
    dk_place = [[placed(n, dk_bits[i]) for n in range(NS)] for i in range(2)]

    coef = scale * math.log2(math.e)
    key_spot = lax.broadcasted_iota(jnp.int32, (SPAN, LEN), 1)
    row_spot = s * SPAN + lax.broadcasted_iota(jnp.int32, (SPAN, LEN), 0)

    def attend(hg, i):
        kv = m.kv[i].reshape(LEN, PAIR)
        m.kvs[...] = kv
        m.vks[...] = pltpu.roll(kv.astype(F32), HEAD, 1).astype(BF)
        length = jnp.int32(0)
        for n in range(SL):
            length = jnp.where(i == n, lens[n], length)
        allowed = jnp.logical_and(key_spot <= row_spot, key_spot < length)
        m.bias[...] = jnp.where(allowed, 0.0, -1e9)
        sides = (m.kvs, m.vks)
        rows = pl.ds(pl.multiple_of(i * SPAN, SPAN), SPAN)
        step = z.STEP
        d_key = d_value = None
        for first in range(0, PG, step):
            count = step * SPAN
            even = slice(first * SPAN, first * SPAN + count)
            odd = slice(PR + first * SPAN, PR + first * SPAN + count)
            halves = (slice(0, count), slice(count, 2 * count))
            q = (m.l1[hg, i, even, :], m.l2[hg, i, odd, :])
            a = (m.l2[hg, i, even, :], m.l1[hg, i, odd, :])
            mask = jnp.concatenate([m.bias[...]] * step, axis=0)
            mixed, dqs = {}, {}
            for group in ((0, 1),) if LEN <= 1024 else ((0,), (1,)):
                raw = {e: dot(q[e], sides[e][...], 1, 1) for e in group}
                dps = {e: dot(a[e], sides[1 - e][...], 1, 1) for e in group}
                probs = {}
                for e in group:
                    score = raw[e] * coef + mask
                    w = jnp.exp2(score - jnp.max(score, axis=-1, keepdims=True))
                    probs[e] = w * (1.0 / jnp.sum(w, axis=-1, keepdims=True))
                for e in group:
                    rounded = probs[e].astype(BF)
                    mixed[e] = dot(rounded, sides[1 - e][...])
                    (m.r2 if e == 0 else m.r1)[halves[e], :] = rounded
                for e in group:
                    pd = probs[e] * dps[e]
                    ds = (pd - probs[e] * jnp.sum(pd, axis=-1, keepdims=True)).astype(BF)
                    (m.r1 if e == 0 else m.r2)[halves[e], :] = ds
                    dqs[e] = dot(ds, sides[e][...])
            for p in range(step):
                at = slice(p * SPAN, (p + 1) * SPAN)
                n = hg * PG + first + p
                cols = slice(n * PAIR, (n + 1) * PAIR)
                m.att[rows, cols] = jnp.where(low, mixed[0][at], mixed[1][at]).astype(BF)
                dq = jnp.where(low, dqs[0][at], dqs[1][at]) * scale
                m.dq[rows, cols] = turned_back(dq, tables).astype(BF)
            if step == PG:
                one = dot(m.l1[hg, i], m.r1[...], 0, 0)
                two = dot(m.l2[hg, i], m.r2[...], 0, 0)
            else:
                one = dot(m.l1[hg, i, even, :], m.r1[halves[0], :], 0, 0)
                one = one + dot(m.l1[hg, i, odd, :], m.r1[halves[1], :], 0, 0)
                two = dot(m.l2[hg, i, even, :], m.r2[halves[0], :], 0, 0)
                two = two + dot(m.l2[hg, i, odd, :], m.r2[halves[1], :], 0, 0)
            key_part = one[:HEAD] + two[HEAD:]
            value_part = one[HEAD:] + two[:HEAD]
            d_key = key_part if d_key is None else d_key + key_part
            d_value = value_part if d_value is None else d_value + value_part
        d_key = d_key * scale
        return jnp.concatenate([d_key, d_value], axis=0)

    def hooked(hooks, i):
        for n, steps in hooks.items():

            @pl.when(i == n)
            def _(steps=steps):
                for step in steps:
                    step()

    for d in range(NO):
        copy, _, gets = near_by[d]

        @pl.when(gets)
        def _(copy=copy):
            copy.wait_recv()

    def up_step(k, n):
        return lambda: ups[k].step(n)

    def slots_done(pipe):
        for n in range(BJ - 1):
            pipe.finish(n)
            if n + 1 < BJ - 1:
                pipe.start(n + 1)

    early = {n: [] for n in range(SL)}
    late = {n: [] for n in range(SL)}
    tail = []
    plan = [early[n] for n in range(SL)] + [late[n] for n in range(SL)] + [tail]

    def at_point(n, step):
        plan[min(n, 2 * SL)].append(step)

    small = BS == 3 and z.CPP == 2
    order = PLAN if small else {}

    def at(name, step):
        plan[order.get(name, 2 * SL)].append(step)

    for k in range(z.CH):
        at(f"y{k}", lambda k=k: slots_done(dn_first[k]))
        if k % 2 == 1:
            at(f"y{k}", lambda k=k: dn_start(0, k // 2))
    for l in range(BS - 1):
        for n in range(z.CH >> (l + 1)):
            at(f"d{l}{n}", lambda l=l, n=n: dn_finish(l, n))
            if l + 1 < BS - 1 and n % 2 == 1:
                at(f"d{l}{n}", lambda l=l, n=n: dn_start(l + 1, n // 2))
    at("dn0", lambda: dn_last(0))
    for l in range(BS - 2, -1, -1):
        for n in range(2**l):
            at(f"e{l}{n}", lambda l=l, n=n: other_finish(l, n))
            if l > 0 and n >= 2 ** (l - 1):
                at(f"e{l}{n}", lambda l=l, n=n: other_start(l - 1, n - 2 ** (l - 1)))
    at("e00", lambda: dn_second.start(0))
    at("ey", lambda: slots_done(dn_second))
    at("dn1", lambda: dn_last(1))
    if crossing:
        at("cross", crossed)
    for k in ups:
        for n in range(1, BS + 1):
            at(f"u{k}{n}", up_step(k, n))
        if k not in crossing:
            at(f"u{k}{BS}", up_last[k])

    def early_body(i, _):
        m.dkt[i] = attend(0, i).astype(m.dkt.dtype)
        hooked(early, i)
        return 0

    lax.fori_loop(0, SL, early_body, 0)

    wo_core = [Halving(links, m.wo.at[hg], [slot_stage(0)], m.wor.at[hg]) for hg in range(2)]
    gq_core = [Halving(links, m.gq.at[hg], [slot_stage(0)], m.gqr.at[hg]) for hg in range(2)]
    wo_group = [
        Direct(
            links,
            z.G,
            low_s,
            group_device,
            lambda n, hg=hg: m.wo.at[hg, c * z.G + n],
            m.woq.at[hg],
        )
        for hg in range(2)
    ]
    gq_group = [
        Direct(
            links,
            z.G,
            low_s,
            group_device,
            lambda n, hg=hg: m.gq.at[hg, pl.ds(c * NS + 2 * n, 2)],
            m.gqq.at[hg],
        )
        for hg in range(2)
    ]
    wo_arrivals = links.take(2 * NJ)
    gq_arrivals = links.take(2 * NJ)
    me = ts * NJ + j
    wo_ends = [
        [
            links.unless(
                jnp.logical_and(ts == hg, j == n),
                m.wos.at[hg, n],
                m.wof.at[me],
                (hg * z.G + low_s, n),
                wo_arrivals + me,
            )
            for n in range(NJ)
        ]
        for hg in range(2)
    ]
    gq_ends = [
        [
            links.unless(
                jnp.logical_and(ts == t, j == hg * QN + n),
                m.gqs.at[hg, t * QN + n],
                m.gqf.at[me],
                (t * z.G + low_s, hg * QN + n),
                gq_arrivals + me,
            )
            for t in range(2)
            for n in range(QN)
        ]
        for hg in range(2)
    ]

    def project(hg):
        cols = slice(hg * (D // 2), (hg + 1) * (D // 2))
        part = dot(m.att[:, cols], m.g2[0:ROWS, :], 0, 0).astype(BF)
        for n in range(z.G):
            for r in range(2):
                at = n * R + r * R2
                m.wo[hg, r * z.G + n] = part[at : at + R2, :]
        wo_core[hg].start(0)
        part = dot(m.ain[...], m.dq[:, cols], 0, 0).astype(BF)
        for n in range(NS):
            for r in range(2):
                at = n * R + r * R2
                m.gq[hg, r * NS + (n % z.G) * 2 + n // z.G] = part[at : at + R2, :]
        gq_core[hg].start(0)

    def project_group(hg):
        wo_core[hg].finish(0)
        wo_group[hg].start()
        gq_core[hg].finish(0)
        gq_group[hg].start()

    def project_last(hg):
        wo_group[hg].finish()
        total = m.wo[hg, c * z.G + low_s].astype(F32)
        for d in range(1, z.G):
            total = total + m.woq[hg, lax.rem(low_s + d, z.G)].astype(F32)
        total = total.astype(BF)
        for n in range(NJ):
            m.wos[hg, n] = total[:, n * C4 : (n + 1) * C4]
            wo_ends[hg][n]()
        gq_group[hg].finish()
        for t in range(2):
            total = m.gq[hg, c * NS + 2 * low_s + t].astype(F32)
            for d in range(1, z.G):
                total = total + m.gqq[hg, lax.rem(low_s + d, z.G), t].astype(F32)
            total = total.astype(BF)
            for n in range(QN):
                m.gqs[hg, t * QN + n] = total[:, n * C4 : (n + 1) * C4]
                gq_ends[hg][t * QN + n]()

    project(0)
    late[0] += [lambda: project_group(0)]
    late[2] += [lambda: project_last(0)]
    marks = {n: [] for n in range(1, 7)}
    for i in range(SL):
        for n in range(1, BS + 1):
            where = DK_PLAN[i, n] if small and SL == 4 else 6
            step = lambda i=i, n=n: dkvs[i].step(n)
            (late[where + 4] if where < 0 else marks[where]).append(step)

    def mark(n):
        for step in marks[n]:
            step()

    def late_body(i, _):
        total = (m.dkt[i] + attend(1, i)).astype(BF)
        for n in range(NS):
            place = jnp.where(lax.rem(i, 2) == 0, dk_place[0][n], dk_place[1][n])
            m.dks[i, place] = total[:, n * SPAN : (n + 1) * SPAN]
        for n in range(SL):

            @pl.when(i == n)
            def _(n=n):
                dkvs[n].start(0)

        hooked(late, i)
        return 0

    lax.fori_loop(0, SL, late_body, 0)

    project(1)
    for k in range(halfway):
        rows = slice(ROWS + k * RB, ROWS + (k + 1) * RB)
        here = slice(k * RB, (k + 1) * RB)
        msend[here, :] = dot(m.act[rows, :], m.wdn[...]).astype(BF)
    project_group(1)
    mark(1)
    for k in range(halfway):
        rows = slice(ROWS + k * RB, ROWS + (k + 1) * RB)
        here = slice(k * RB, (k + 1) * RB)
        dsend[here, :] = dot(m.dup[rows, :], m.wup[...], 1, 1).astype(BF)
    got_out = links.start(msend, mrecv, buddy)
    got_back = links.start(dsend, drecv, buddy)
    mark(2)
    for step in tail:
        step()
    for k in range(halfway):
        here = slice(k * RB, (k + 1) * RB)
        m.own_mlp[here, :] = dot(m.act[here, :], m.wdn[...]) + dot(m.att[here, :], m.wout[...])
    mark(3)
    for k in range(halfway):
        here = slice(k * RB, (k + 1) * RB)
        m.own_d[here, :] = dot(m.dup[here, :], m.wup[...], 1, 1).astype(m.own_d.dtype)
    mark(4)
    got_out.wait_recv()
    got_back.wait_recv()

    def normed(rows):
        v = m.x[rows, :].astype(F32)
        v = v - jnp.mean(v, axis=-1, keepdims=True)
        inv = lax.rsqrt(jnp.mean(v * v, axis=-1, keepdims=True) + 1e-05)
        return v * inv, inv

    g_sum = jnp.zeros((1, D), F32)
    gain_two = jnp.zeros((1, D), F32)
    shift_two = jnp.zeros((1, D), F32)
    out_copies = []
    for i in range(SL):
        rows = slice(i * SPAN, (i + 1) * SPAN)
        total = m.x[rows, :].astype(F32) + m.own_mlp[rows, :] + mrecv[rows, :].astype(F32)
        total = total + (pars[5:6, :] + pars[6:7, :])
        mrecv[rows, :] = jnp.where(spot < lens[i], total, 0.0).astype(BF)
        d_mlp = m.own_d[rows, :] + drecv[rows, :].astype(F32)
        unit, _ = normed(rows)
        gain_two = gain_two + jnp.sum(d_mlp * unit, axis=0, keepdims=True)
        shift_two = shift_two + jnp.sum(d_mlp, axis=0, keepdims=True)
        m.own_d[rows, :] = (d_mlp * pars[2:3, :]).astype(m.own_d.dtype)
        g_sum = g_sum + jnp.sum(m.g2[rows, :].astype(F32), axis=0, keepdims=True)
    copy = pltpu.make_async_copy(mrecv, o_lo, m.lsem.at[8])
    copy.start()
    out_copies.append(copy)
    m.sv[0, 4:5, :] = gain_two
    m.sv[0, 5:6, :] = shift_two
    m.sv[0, 6:7, :] = g_sum
    sv_one = Direct(links, NJ, j, slot_device, lambda n: m.sv.at[0], m.sva)
    sv_two = Direct(links, NS, s, seq_device, lambda n: m.sv.at[1], m.svb)
    m.sva[j] = m.sv[0]
    sv_one.start()
    mark(5)

    bq = jnp.zeros((1, D), F32)
    for i in range(SL):
        rows = slice(i * SPAN, (i + 1) * SPAN)
        dq = m.dq[rows, :]
        bq = bq + jnp.sum(dq.astype(F32), axis=0, keepdims=True)
        m.own_mlp[rows, :] = dot(dq, m.wq[...], 1, 1)
    project_last(1)
    mark(6)

    bkv = jnp.zeros((1, PAIR), F32)
    for i in range(SL):
        d_kv = jnp.transpose(m.dks[i, dkvs[i].end].astype(F32))
        d_kv = turned_back(d_kv, key_tables)
        bkv = bkv + jnp.sum(d_kv, axis=0, keepdims=True)
        m.kvs[i * SPAN : (i + 1) * SPAN, :] = d_kv.astype(BF)
    d_kv_pre = m.kvs[0:ROWS, :]
    part = dot(d_kv_pre, m.ain[...], 0, 0).astype(BF)
    for n in range(NJ):
        m.kgs[n] = part[n * z.KR : (n + 1) * z.KR, :]
    kg_one = Direct(links, NJ, j, slot_device, lambda n: m.kgs.at[n], m.kgf)
    kg_two = Direct(links, NS, s, seq_device, lambda n: m.kg2.at[n], m.kgx)
    m.kgf[j] = m.kgs[j]
    kg_one.start()

    gain_one = jnp.zeros((1, D), F32)
    shift_one = jnp.zeros((1, D), F32)
    for i in range(SL):
        rows = slice(i * SPAN, (i + 1) * SPAN)
        d_in = m.own_mlp[rows, :] + dot(m.kvs[rows, :], m.wkv[...], 1, 1)
        unit, _ = normed(rows)
        gain_one = gain_one + jnp.sum(d_in * unit, axis=0, keepdims=True)
        shift_one = shift_one + jnp.sum(d_in, axis=0, keepdims=True)
        m.own_mlp[rows, :] = d_in
    m.sw[0] = jnp.zeros((24, 128), F32)
    for n in range(D // 128):
        cols = slice(n * 128, (n + 1) * 128)
        m.sw[0, n : n + 1, :] = gain_one[:, cols]
        m.sw[0, 6 + n : 7 + n, :] = shift_one[:, cols]
        m.sw[0, 12 + n : 13 + n, :] = bq[:, cols]
    m.sw[0, 18:19, :] = bkv
    sw_one = Direct(links, NJ, j, slot_device, lambda n: m.sw.at[0], m.swa)
    sw_two = Direct(links, NS, s, seq_device, lambda n: m.sw.at[1], m.swb)
    m.swa[j] = m.sw[0]
    sw_one.start()
    for i in range(SL):
        rows = slice(i * SPAN, (i + 1) * SPAN)
        unit, inv = normed(rows)
        d_unit = m.own_mlp[rows, :] * pars[0:1, :] + m.own_d[rows, :]
        along = jnp.mean(d_unit * unit, axis=-1, keepdims=True)
        d_unit = d_unit - jnp.mean(d_unit, axis=-1, keepdims=True) - unit * along
        m.own_mlp[rows, :] = m.g2[rows, :].astype(F32) + d_unit * inv
    copy = pltpu.make_async_copy(m.own_mlp, o_gi, m.lsem.at[9])
    copy.start()
    out_copies.append(copy)

    def summed(ref, size):
        total = ref[0].astype(F32)
        for n in range(1, size):
            total = total + ref[n].astype(F32)
        return total

    sv_one.finish()
    m.sv[1] = summed(m.sva, NJ)
    m.svb[s] = m.sv[1]
    sv_two.start()
    kg_one.finish()
    part = summed(m.kgf, NJ).astype(BF)
    for n in range(NS):
        m.kg2[n] = part[:, n * R : (n + 1) * R]
    m.kgx[s] = m.kg2[s]
    kg_two.start()
    sw_one.finish()
    m.sw[1] = summed(m.swa, NJ)
    m.swb[s] = m.sw[1]
    sw_two.start()

    if crossing:
        o_up[:, CW:] = m.upy[0, ups[1].end].astype(F32)
    for n in range(QN):
        links.arrived(m.upf.at[n], up_arrivals + n)
    o_up[:, 0:CW] = summed(m.upf, QN)
    for p in range(2):
        for t in range(2):
            links.arrived(m.dnf.at[p, t], dn_arrivals + 2 * p + t)
        o_dn[p * z.FRH : (p + 1) * z.FRH, :] = summed(m.dnf.at[p], 2)
    for n in range(2 * NJ):
        links.arrived(m.gqf.at[n], gq_arrivals + n)
        links.arrived(m.wof.at[n], wo_arrivals + n)
    for r in range(2):
        for out, ref in ((o_wq, m.gqf), (o_wo, m.wof)):
            total = ref[r].astype(F32)
            for n in range(1, NJ):
                total = total + ref[2 * n + r].astype(F32)
            out[r * R2 : (r + 1) * R2, :] = total
    sv_two.finish()
    o_sv[...] = summed(m.svb, NS)
    kg_two.finish()
    o_wkv[...] = summed(m.kgx, NS)
    sw_two.finish()
    o_sw[...] = summed(m.swb, NS)
    for copy in out_copies:
        copy.wait()
    links.finish()


class Names:
    pass


def body(
    hidden_in, lengths, out_grad, ln1_gain, ln1_bias, ln2_gain, ln2_bias, w_query, b_query,
    w_keyval, b_keyval, w_out, b_out, w_up, b_up, w_down, b_down,
):
    SL, SPAN, D = hidden_in.shape
    FF = w_up.shape[1]
    z = Sizes(lax.axis_size("seq"), lax.axis_size("slot"), SL, SPAN, D, FF)
    scratch = scratch_of(z)
    names = list(scratch)
    n_in, n_out = 18, 9

    def call(*refs):
        m = Names()
        for name, ref in zip(names, refs[n_in + n_out :]):
            setattr(m, name, ref)
        kernel(z, refs[:n_in], refs[n_in : n_in + n_out], m)

    anywhere = pl.BlockSpec(memory_space=pl.ANY)
    vmem = pl.BlockSpec(memory_space=pltpu.VMEM)
    shape = jax.ShapeDtypeStruct
    lo, gi, up, dn, wo, wq, wkv, sv, sw = pl.pallas_call(
        call,
        out_shape=[
            shape((z.ROWS, D), BF),
            shape((z.ROWS, D), F32),
            shape((z.R, z.W), F32),
            shape((z.CW, z.DW // 2), F32),
            shape((z.R, z.C4), F32),
            shape((z.R, z.C4), F32),
            shape((z.KR, z.R), F32),
            shape((8, D), F32),
            shape((24, 128), F32),
        ],
        in_specs=[anywhere, anywhere, pl.BlockSpec(memory_space=pltpu.SMEM)]
        + [anywhere] * 6
        + [vmem] * 9,
        out_specs=[anywhere, anywhere] + [vmem] * 7,
        scratch_shapes=list(scratch.values()),
        compiler_params=pltpu.CompilerParams(
            collective_id=0, has_side_effects=True, vmem_limit_bytes=63 * 2**20
        ),
    )(
        hidden_in.reshape(z.ROWS, D),
        out_grad.reshape(z.ROWS, D),
        lengths,
        w_query,
        w_keyval,
        w_out,
        w_up,
        w_down,
        jnp.asarray(rotary_tables(z.LEN)),
        ln1_gain,
        ln1_bias,
        ln2_gain,
        ln2_bias,
        b_query,
        b_out,
        b_down,
        b_up,
        b_keyval,
    )
    wide = (lo, gi, up, wo, wq)

    def hand_over(*refs):
        n = len(wide)
        sources, (dn, wkv, sv, sw) = refs[:n], refs[n : n + 4]
        targets, rest = refs[n + 4 : 2 * n + 4], refs[2 * n + 4 : 2 * n + 15]
        held, came, left = refs[2 * n + 15 : 3 * n + 15], refs[-2], refs[-1]
        copies = [
            (
                pltpu.make_async_copy(a, b, came.at[k]),
                pltpu.make_async_copy(b, c, left.at[k]),
            )
            for k, (a, b, c) in enumerate(zip(sources, held, targets))
        ]
        for copy, _ in copies:
            copy.start()
        o_dn, o_wkv, gain_one, shift_one, gain_two, shift_two, bq, bkv, bo, bup, bd = rest
        for at, ref in enumerate((gain_one, shift_one, bq)):
            parts = [sw[k : k + 1, :] for k in range(at * (D // 128), (at + 1) * (D // 128))]
            ref[...] = jnp.concatenate(parts, axis=1).reshape(D)
        bkv[...] = sw[18:19, :].reshape(PAIR)
        gain_two[...] = sv[4:5, :].reshape(D)
        shift_two[...] = sv[5:6, :].reshape(D)
        bo[...] = sv[6:7, :].reshape(D)
        bd[...] = sv[6:7, :].reshape(D)
        parts = [sv[k : k + 1, :] for k in range(FF // D)]
        bup[...] = jnp.concatenate(parts, axis=1).reshape(FF)
        o_dn[...] = jnp.transpose(dn[...])
        o_wkv[...] = wkv[...]
        for copy, out in copies:
            copy.wait()
            out.start()
        for _, out in copies:
            out.wait()

    lo, gi, up, wo, wq, dn, wkv, g1, s1, g2, s2, bq, bkv, bo, bup, bd = pl.pallas_call(
        hand_over,
        out_shape=[shape(v.shape, v.dtype) for v in wide]
        + [shape(dn.shape[::-1], F32), shape(wkv.shape, F32)]
        + [shape((n,), F32) for n in (D, D, D, D, D, PAIR, D, FF, D)],
        in_specs=[anywhere] * 5 + [vmem] * 4,
        out_specs=[anywhere] * 5 + [vmem] * 11,
        scratch_shapes=[pltpu.VMEM(v.shape, v.dtype) for v in wide]
        + [pltpu.SemaphoreType.DMA((5,)), pltpu.SemaphoreType.DMA((5,))],
    )(*wide, dn, wkv, sv, sw)
    return (
        lo.reshape(hidden_in.shape),
        gi.reshape(hidden_in.shape),
        g1, s1, g2, s2, wq, bq, wkv.T, bkv, wo, bo, up, bup, dn.T, bd,
    )


def solution(mesh):
    rows, whole, cut = P("slot", "seq", None), P(), P("seq", "slot")
    return jax.shard_map(
        body,
        mesh=mesh,
        in_specs=(rows, P("slot"), rows) + (whole,) * 14,
        out_specs=(
            rows, rows, whole, whole, whole, whole, cut, whole, cut, whole, cut, whole, cut, whole,
            cut, whole,
        ),
        check_vma=False,
    )
```

```python
import math

import jax
import jax.numpy as jnp
import numpy as np
from jax import lax
from jax.experimental import pallas as pl
from jax.experimental.pallas import tpu as pltpu
from jax.sharding import PartitionSpec as P

HEAD = 64
ROT = 16
DK_PLAN = {
    (0, 1): -2, (0, 2): -1, (0, 3): 1, (1, 1): -1, (1, 2): 2, (1, 3): 4,
    (2, 1): 1, (2, 2): 3, (2, 3): 5, (3, 1): 3, (3, 2): 5, (3, 3): 6,
}
PLAN = {
    "y0": 0, "y1": 0, "y2": 1, "y3": 2, "d00": 2, "d01": 4, "d10": 5, "dn0": 5, "cross": 2,
    "e10": 1, "e11": 3, "e00": 5, "ey": 7, "dn1": 7,
    "u01": 0, "u21": 1, "u02": 2, "u22": 3, "u11": 4, "u12": 5, "u03": 4, "u23": 5, "u13": 7,
}
PAIR = 2 * HEAD
MESH = pl.DeviceIdType.MESH
BF = jnp.bfloat16
F32 = jnp.float32


def dot(a, b, ca=1, cb=0):
    return lax.dot_general(a, b, (((ca,), (cb,)), ((), ())), preferred_element_type=F32)


def gelu_pair(u):
    cdf = 0.5 * (1.0 + lax.erf(u * 0.7071067811865476))
    pdf = 0.3989422804014327 * jnp.exp(-0.5 * u * u)
    return u * cdf, cdf + u * pdf


def bit_of(value, bit):
    return lax.rem(lax.div(value, 2**bit), 2)


def flip(value, bit):
    return value + (1 - 2 * bit_of(value, bit)) * 2**bit


def put(value, bit, new):
    return value + (new - bit_of(value, bit)) * 2**bit


def placed(index, bits):
    at = 0
    for bit in bits:
        at = at * 2 + (index >> bit) % 2
    return at


def turned(value, tables):
    same, after, before = tables
    return value * same + pltpu.roll(value, PAIR - 8, 1) * after + pltpu.roll(value, 8, 1) * before


def turned_back(value, tables):
    same, after, before = tables
    return (
        value * same
        + pltpu.roll(value * after, 8, 1)
        + pltpu.roll(value * before, PAIR - 8, 1)
    )


def rotary_tables(length):
    half = ROT // 2
    inverse = (10000.0 ** (-(np.arange(half, dtype=np.float32) * 2.0 / ROT))).astype(np.float32)
    turns = np.arange(length, dtype=np.float32)[:, None] * inverse[None, :]
    cosine = np.cos(turns.astype(np.float64)).astype(np.float32)
    sine = np.sin(turns.astype(np.float64)).astype(np.float32)
    out = np.zeros((3, length, PAIR), np.float32)
    out[0] = 1.0
    for head in range(2):
        at = head * HEAD
        out[0, :, at : at + half] = cosine
        out[0, :, at + half : at + ROT] = cosine
        out[1, :, at : at + half] = -sine
        out[2, :, at + half : at + ROT] = sine
    return out


class Links:
    def __init__(self, send, recv):
        self.send, self.recv, self.used, self.waits = send, recv, 0, []

    def take(self, count=1):
        first = self.used
        self.used += count
        return first

    def copy(self, src, dst, device, arrival=None):
        k = self.take()
        return pltpu.make_async_remote_copy(
            src_ref=src,
            dst_ref=dst,
            send_sem=self.send.at[k],
            recv_sem=self.recv.at[k if arrival is None else arrival],
            device_id=device,
            device_id_type=MESH,
        )

    def start(self, src, dst, device):
        copy = self.copy(src, dst, device)
        copy.start()
        self.waits.append(copy)
        return copy

    def unless(self, own, src, dst, device, arrival):
        remote = self.copy(src, dst, device, arrival)
        local = pltpu.make_async_copy(src, dst, self.recv.at[arrival])
        other = jnp.logical_not(own)
        self.waits.append((other, remote))

        def start():
            @pl.when(own)
            def _():
                local.start()

            @pl.when(other)
            def _():
                remote.start()

        return start

    def arrived(self, dst, arrival):
        pltpu.make_async_copy(dst, dst, self.recv.at[arrival]).wait()

    def finish(self):
        for copy in self.waits:
            if isinstance(copy, tuple):

                @pl.when(copy[0])
                def _(copy=copy):
                    copy[1].wait_send()

            else:
                copy.wait_send()


class Halving:
    def __init__(self, links, cur, stages, recv):
        blocks = cur.shape[0]
        off, at = jnp.int32(0), 0
        self.cur, self.steps, self.links = cur, [], links
        for mine, partner in stages:
            blocks //= 2
            src = cur.at[pl.ds(off + (1 - mine) * blocks, blocks)]
            dst = recv.at[pl.ds(at, blocks)]
            off = off + mine * blocks
            self.steps.append((links.copy(src, dst, partner), dst, off, blocks))
            at += blocks
        self.end = off

    def start(self, k):
        self.steps[k][0].start()
        self.links.waits.append(self.steps[k][0])

    def finish(self, k):
        copy, recv, off, blocks = self.steps[k]
        cur = self.cur
        copy.wait_recv()

        def add(i, _):
            cur[off + i] = cur[off + i] + recv[i]
            return 0

        lax.fori_loop(0, blocks, add, 0)

    def step(self, k):
        if k:
            self.finish(k - 1)
        if k < len(self.steps):
            self.start(k)


class Direct:
    def __init__(self, links, size, me, device_of, source, dst):
        self.links, self.size, self.me, self.dst = links, size, me, dst
        self.source = source
        self.out = []
        for d in range(1, size):
            target = lax.rem(me + d, size)
            self.out.append(links.copy(source(target), dst.at[me], device_of(target)))

    def start(self):
        for copy in self.out:
            copy.start()
            self.links.waits.append(copy)

    def finish(self):
        for d in range(1, self.size):
            sender = lax.rem(self.me + self.size - d, self.size)
            self.out[d - 1].wait_recv()


class Sizes:
    def __init__(self, NS, NJ, SL, SPAN, D, FF):
        self.NS, self.NJ, self.SL, self.SPAN, self.D, self.FF = NS, NJ, SL, SPAN, D, FF
        self.BS, self.BJ = NS.bit_length() - 1, NJ.bit_length() - 1
        self.ROWS, self.LEN, self.HF = SL * SPAN, NS * SPAN, FF // 2
        self.QN = NJ // 2
        self.R, self.W = D // NS, FF // NJ
        self.CH = self.G = NS // 2
        self.CW = self.HF // self.CH
        self.CPP = self.W // self.CW
        self.FRH, self.DW = self.CW // 2, D // self.QN
        self.R2, self.C4 = self.R // 2, D // NJ
        self.PAIRS = D // PAIR
        self.PG = self.PAIRS // 2
        self.PR = self.PG * SPAN
        self.KR = PAIR // NJ
        self.STEP = self.PG if self.LEN <= 1024 else 1


def scratch_of(z):
    vm = pltpu.VMEM
    rows, d = z.ROWS, z.D
    return dict(
        pars=vm((8 + z.FF // d, d), F32),
        x=vm((rows, d), BF),
        g2=vm((2 * rows, d), BF),
        mlp2=vm((2 * rows, d), BF),
        ain=vm((rows, d), BF),
        wq=vm((d, d), BF),
        wkv=vm((d, PAIR), BF),
        wout=vm((d, d), BF),
        wup=vm((d, z.HF), BF),
        wdn=vm((z.HF, d), BF),
        tab=vm((3, z.SPAN, PAIR), F32),
        act=vm((2 * rows, z.HF), BF),
        dup=vm((2 * rows, z.HF), BF),
        l1=vm((2, z.SL, 2 * z.PR, PAIR), BF),
        l2=vm((2, z.SL, 2 * z.PR, PAIR), BF),
        att=vm((rows, d), BF),
        dq=vm((rows, d), BF),
        kv=vm((z.SL, z.NS, z.SPAN, PAIR), BF),
        kvs=vm((z.LEN, PAIR), BF),
        vks=vm((z.LEN, PAIR), BF),
        r1=vm((2 * z.STEP * z.SPAN, z.LEN), BF),
        r2=vm((2 * z.STEP * z.SPAN, z.LEN), BF),
        bias=vm((z.SPAN, z.LEN), F32),
        dkt=vm((z.SL, PAIR, z.LEN), F32 if z.LEN <= 1024 else BF),
        dks=vm((z.SL, z.NS, PAIR, z.SPAN), BF),
        dkr=vm((z.SL, z.NS - 1, PAIR, z.SPAN), BF),
        up=vm((z.CH, z.NS, z.R, z.CW), BF),
        upr=vm((z.CH if z.CPP == 1 else z.CH // 2 + 1, z.NS - 1, z.R, z.CW), BF),
        upf=vm((z.QN, z.R, z.CW), BF),
        upy=vm((z.QN if z.CPP > 1 else 1, z.NS if z.CPP > 1 else 1, z.R, z.CW), BF),
        dn=vm((z.CH, 2, z.QN, z.FRH, z.DW), BF),
        dnr=vm((z.CH + 1, z.QN - 1, z.FRH, z.DW), BF),
        dnr2=vm((z.CH - 1, z.FRH, z.DW), BF),
        dnr3=vm((z.CH - 1, z.QN, z.FRH, z.DW), BF),
        dnm=vm((4, z.FRH, z.DW // 2), BF),
        dnf=vm((2, 2, z.FRH, z.DW // 2), BF),
        wo=vm((2, z.NS, z.R2, d), BF),
        wor=vm((2, z.G, z.R2, d), BF),
        woq=vm((2, z.G, z.R2, d), BF),
        wos=vm((2, z.NJ, z.R2, z.C4), BF),
        wof=vm((2 * z.NJ, z.R2, z.C4), BF),
        gq=vm((2, 2 * z.NS, z.R2, d // 2), BF),
        gqr=vm((2, z.NS, z.R2, d // 2), BF),
        gqq=vm((2, z.G, 2, z.R2, d // 2), BF),
        gqs=vm((2, 2 * z.QN, z.R2, z.C4), BF),
        gqf=vm((2 * z.NJ, z.R2, z.C4), BF),
        kgs=vm((z.NJ, z.KR, d), BF),
        kgf=vm((z.NJ, z.KR, d), BF),
        kg2=vm((z.NS, z.KR, z.R), BF),
        kgx=vm((z.NS, z.KR, z.R), BF),
        sv=vm((2, 8, d), F32),
        sva=vm((z.NJ, 8, d), F32),
        svb=vm((z.NS, 8, d), F32),
        sw=vm((2, 24, 128), F32),
        swa=vm((z.NJ, 24, 128), F32),
        swb=vm((z.NS, 24, 128), F32),
        own_mlp=vm((rows, d), F32),
        own_d=vm((rows, d), F32 if z.LEN <= 1024 else BF),
        send=pltpu.SemaphoreType.DMA((48 * z.NS // 2,)),
        recv=pltpu.SemaphoreType.DMA((48 * z.NS // 2,)),
        lsem=pltpu.SemaphoreType.DMA((12,)),
    )


def kernel(z, ins, outs, m):
    x_hbm, g_hbm, lens = ins[:3]
    wq_hbm, wkv_hbm, wout_hbm, wup_hbm, wdn_hbm, tab_hbm = ins[3:9]
    vectors = ins[9:]
    o_lo, o_gi, o_up, o_dn, o_wo, o_wq, o_wkv, o_sv, o_sw = outs
    NS, NJ, BS, BJ, SL, SPAN, D, HF = z.NS, z.NJ, z.BS, z.BJ, z.SL, z.SPAN, z.D, z.HF
    ROWS, LEN, QN, R, R2, CW, C4, PG, PR = (
        z.ROWS, z.LEN, z.QN, z.R, z.R2, z.CW, z.C4, z.PG, z.PR,
    )
    links = Links(m.send, m.recv)
    s = lax.axis_index("seq")
    j = lax.axis_index("slot")
    c = bit_of(j, 0)
    ts = bit_of(s, BS - 1)
    rank = lax.div(j, 2)
    buddy = (s, flip(j, 0))
    scale = HEAD**-0.5

    def seq_device(n):
        return (n, j)

    def slot_device(n):
        return (s, n)

    def load(k, src, dst):
        copy = pltpu.make_async_copy(src, dst, m.lsem.at[k])
        copy.start()
        return copy

    load_x = load(0, x_hbm, m.x)
    load_g = load(1, g_hbm, m.g2.at[pl.ds(0, ROWS), :])
    load_tab = load(2, tab_hbm.at[:, pl.ds(pl.multiple_of(s * SPAN, SPAN), SPAN), :], m.tab)
    load_wkv = load(3, wkv_hbm, m.wkv)
    load_wq = load(4, wq_hbm, m.wq)
    load_wout = load(5, wout_hbm, m.wout)
    load_wup = load(6, wup_hbm.at[:, pl.ds(pl.multiple_of(c * HF, HF), HF)], m.wup)
    load_wdn = load(7, wdn_hbm.at[pl.ds(pl.multiple_of(c * HF, HF), HF), :], m.wdn)

    for i in range(SL):
        m.kv[i] = jnp.zeros((NS, SPAN, PAIR), BF)
    near = [seq_device(lax.rem(s + d, NS)) for d in range(1, NS)]
    near += [slot_device(lax.rem(j + d, NJ)) for d in range(1, NJ)]
    near += [(flip(s, BS - 1), flip(j, 0))]
    barrier = pltpu.get_barrier_semaphore()
    for device in near:
        pl.semaphore_signal(barrier, inc=1, device_id=device, device_id_type=MESH)

    pars = m.pars
    for n, vector in enumerate(vectors[:7]):
        pars[n : n + 1, :] = vector[...].astype(F32).reshape(1, D)
    wide = vectors[7][...].astype(F32).reshape(1, z.FF)
    for n in range(z.FF // D):
        pars[7 + n : 8 + n, :] = wide[:, n * D : (n + 1) * D]
    b_keyval = vectors[8][...].astype(F32).reshape(1, PAIR)
    spot = s * SPAN + lax.broadcasted_iota(jnp.int32, (SPAN, 1), 0)
    load_x.wait()
    load_g.wait()
    for i in range(SL):
        rows = slice(i * SPAN, (i + 1) * SPAN)
        v = m.x[rows, :].astype(F32)
        v = v - jnp.mean(v, axis=-1, keepdims=True)
        v = v * lax.rsqrt(jnp.mean(v * v, axis=-1, keepdims=True) + 1e-05)
        m.ain[rows, :] = (v * pars[0:1, :] + pars[1:2, :]).astype(BF)
        m.mlp2[rows, :] = (v * pars[2:3, :] + pars[3:4, :]).astype(BF)
        m.g2[rows, :] = jnp.where(spot < lens[i], m.g2[rows, :].astype(F32), 0.0).astype(BF)
    own, theirs = pl.ds(0, ROWS), pl.ds(ROWS, ROWS)
    msend, dsend = m.g2.at[theirs, :], m.act.at[theirs, pl.ds(0, D)]
    mrecv, drecv = m.mlp2.at[own, :], m.mlp2.at[theirs, :]
    got_m = links.copy(m.mlp2.at[own, :], m.mlp2.at[theirs, :], buddy)
    got_g = links.copy(m.g2.at[own, :], m.g2.at[theirs, :], buddy)

    lane = lax.broadcasted_iota(jnp.int32, (SPAN, PAIR), 1)
    low = lane < HEAD
    load_tab.wait()
    tables = (m.tab[0], m.tab[1], m.tab[2])
    key_tables = (
        jnp.where(low, tables[0], 1.0),
        jnp.where(low, tables[1], 0.0),
        jnp.where(low, tables[2], 0.0),
    )
    load_wkv.wait()
    kv_pre = dot(m.ain[...], m.wkv[...]) + b_keyval
    for i in range(SL):
        m.kv[i, s] = turned(kv_pre[i * SPAN : (i + 1) * SPAN, :], key_tables).astype(BF)
    pl.semaphore_wait(barrier, len(near))
    got_m.start()
    got_g.start()
    inner = lax.rem(s, 2)
    outer = lax.div(s, 2)
    NO = NS // 2
    far, near_by = {}, {}
    for d in range(NO):
        gets = outer - d >= 0
        if d:
            sends = outer + d < NO
            there = seq_device(lax.rem(s + 2 * d, NS))
            far[d] = (links.copy(m.kv.at[:, s], m.kv.at[:, s], there), gets)

            @pl.when(sends)
            def _(d=d):
                far[d][0].start()

            links.waits.append((sends, far[d][0]))
            sends = gets
        else:
            sends, gets = inner == 0, inner == 1
        block = lax.rem(s - 2 * d + NS, NS)
        copy = links.copy(m.kv.at[:, block], m.kv.at[:, block], seq_device(flip(s, 0)))
        near_by[d] = (copy, sends, gets)
        links.waits.append((sends, copy))

    def pass_on(d):
        copy, sends, _ = near_by[d]

        @pl.when(sends)
        def _():
            if d:
                far[d][0].wait_recv()
            copy.start()

    pass_on(0)

    load_wq.wait()
    load_wout.wait()
    for i in range(SL):
        rows = slice(i * SPAN, (i + 1) * SPAN)
        q_pre = dot(m.ain[rows, :], m.wq[...]) + pars[4:5, :]
        back = dot(m.g2[rows, :], m.wout[...], 1, 1)
        for p in range(z.PAIRS):
            hg, at = p // PG, (p % PG) * SPAN
            cols = slice(p * PAIR, (p + 1) * PAIR)
            q = turned(q_pre[:, cols], tables)
            a = back[:, cols]
            m.l1[hg, i, at : at + SPAN, :] = jnp.where(low, q, 0.0).astype(BF)
            m.l2[hg, i, PR + at : PR + at + SPAN, :] = jnp.where(low, 0.0, q).astype(BF)
            m.l2[hg, i, at : at + SPAN, :] = jnp.where(low, a, 0.0).astype(BF)
            m.l1[hg, i, PR + at : PR + at + SPAN, :] = jnp.where(low, 0.0, a).astype(BF)

    load_wup.wait()
    load_wdn.wait()
    m.sv[0] = jnp.zeros((8, D), F32)
    low_bits = list(range(BS - 1))
    turned_bits = low_bits[1:] + low_bits[:1]
    seq_stage = lambda b: (bit_of(s, b), (flip(s, b), j))
    slot_stage = lambda b: (bit_of(j, b), (s, flip(j, b)))
    low_s = lax.rem(s, z.G)
    slot_stages = [slot_stage(b) for b in range(BJ - 1, 0, -1)]
    dn_first = [
        Halving(links, m.dn.at[k, 0], slot_stages, m.dnr.at[k]) for k in range(z.CH)
    ]
    dn_other = {}
    at = 0
    for l in range(BS - 2, -1, -1):
        for n in range(2**l):
            keep = lax.div(low_s, 2**l) * 2**l + n
            give = keep + (1 - 2 * bit_of(s, l)) * 2**l
            copy = links.copy(m.dn.at[give, 1], m.dnr3.at[at], (flip(s, l), j))
            dn_other[l, n] = (copy, keep, at)
            at += 1
    dn_second = Halving(links, m.dn.at[low_s, 1], slot_stages, m.dnr.at[z.CH])

    def other_start(l, n):
        dn_other[l, n][0].start()
        links.waits.append(dn_other[l, n][0])

    def other_finish(l, n):
        copy, keep, at = dn_other[l, n]
        copy.wait_recv()
        for q in range(QN):
            m.dn[keep, 1, q] = m.dn[keep, 1, q] + m.dnr3[at, q]

    up_order = [(low_bits if k % 2 == 0 else turned_bits) + [BS - 1] for k in range(z.CH)]
    crossing = [k for k in range(z.CH) if k % z.CPP == 1]
    staying = [k for k in range(z.CH) if k not in crossing]
    ups = {
        k: Halving(links, m.up.at[k], [seq_stage(b) for b in up_order[k]], m.upr.at[n])
        for n, k in enumerate(staying)
    }
    if crossing:
        stages = [seq_stage(b) for b in up_order[1]]
        ups[1] = Halving(links, m.upy.at[0], stages, m.upr.at[len(staying)])
    upy_arrivals = links.take(QN)
    crossings = {}
    for k in crossing:
        target = c * QN + (k * CW) // z.W
        crossings[k] = links.unless(
            target == j, m.up.at[k], m.upy.at[rank], (s, target), upy_arrivals + rank
        )

    def crossed():
        for n in range(QN):
            links.arrived(m.upy.at[n], upy_arrivals + n)

        def add(i, _):
            m.upy[0, i] = m.upy[0, i] + m.upy[1, i]
            return 0

        lax.fori_loop(0, NS, add, 0)
        ups[1].start(0)

    RB = 256

    def bias_of(at):
        row, col = at // D, at % D
        if col + CW <= D:
            return pars[7 + row : 8 + row, col : col + CW]
        return jnp.concatenate(
            [pars[7 + row : 8 + row, col:], pars[8 + row : 9 + row, : col + CW - D]], axis=1
        )

    def feed(k, first, last):
        cols = slice(k * CW, (k + 1) * CW)
        bias = jnp.where(c == 0, bias_of(k * CW), bias_of(k * CW + HF))

        def block(i, total):
            rows = pl.ds(pl.multiple_of(i * RB, RB), RB)
            up = dot(m.mlp2[rows, :], m.wup[:, cols]) + bias
            back = dot(m.g2[rows, :], m.wdn[cols, :], 1, 1)
            a, slope = gelu_pair(up)
            back = back * slope
            m.act[rows, cols] = a.astype(BF)
            m.dup[rows, cols] = back.astype(BF)
            return total + jnp.sum(back, axis=0, keepdims=True)

        return lax.fori_loop(first, last, block, jnp.zeros((1, CW), F32))

    def feed_grads(k):
        cols = slice(k * CW, (k + 1) * CW)
        part = dot(m.act[:, cols], m.g2[...], 0, 0).astype(BF)
        for p in range(2):
            for q in range(QN):
                m.dn[k, p, q] = part[p * z.FRH : (p + 1) * z.FRH, q * z.DW : (q + 1) * z.DW]
        dn_first[k].start(0)
        if 2 * k >= z.CH:
            other_start(BS - 2, k - z.CH // 2)
        part = dot(m.mlp2[...], m.dup[:, cols], 0, 0).astype(BF)
        for n in range(NS):
            m.up[k, placed(n, up_order[1 if k in crossing else k])] = part[n * R : (n + 1) * R, :]
        if k in crossing:
            crossings[k]()
        else:
            ups[k].start(0)

    halfway = ROWS // RB
    totals = []
    for k in range(z.CH):
        total = feed(k, 0, halfway)
        if k == 0:
            got_m.wait()
            got_g.wait()
        totals.append(total + feed(k, halfway, 2 * halfway))
        feed_grads(k)
        for d in range(1, NO):
            if (k == d if NO == 4 else k == z.CH - 1):
                pass_on(d)
    total = jnp.concatenate(totals, axis=1)
    for q in range(z.FF // D):
        piece = total[:, (q * D) % HF : (q * D) % HF + D]
        m.sv[0, q : q + 1, :] = jnp.where(c == (q * D) // HF, piece, 0.0)

    kept = rank
    dn_levels, at = {}, 0
    for l in range(BS - 1):
        for n in range(z.CH >> (l + 1)):
            base = n * 2 ** (l + 1) + lax.rem(s, 2**l)
            mine = bit_of(s, l)
            keep = base + mine * 2**l
            give = base + (1 - mine) * 2**l
            copy = links.copy(m.dn.at[give, 0, kept], m.dnr2.at[at], (flip(s, l), j))
            dn_levels[l, n] = (copy, keep, at)
            at += 1

    def dn_start(l, n):
        dn_levels[l, n][0].start()
        links.waits.append(dn_levels[l, n][0])

    def dn_finish(l, n):
        copy, keep, at = dn_levels[l, n]
        copy.wait_recv()
        m.dn[keep, 0, kept] = m.dn[keep, 0, kept] + m.dnr2[at]

    dn_arrivals = links.take(4)

    dn_ends = [
        [
            links.unless(
                jnp.logical_and(ts == c, c == h),
                m.dnm.at[2 * p + h],
                m.dnf.at[p, ts],
                (put(s, BS - 1, c), put(j, 0, h)),
                dn_arrivals + 2 * p + ts,
            )
            for h in range(2)
        ]
        for p in range(2)
    ]

    def dn_last(p):
        part = m.dn[low_s, p, kept]
        for h in range(2):
            m.dnm[2 * p + h] = part[:, h * (z.DW // 2) : (h + 1) * (z.DW // 2)]
            dn_ends[p][h]()

    up_arrivals = links.take(QN)

    def up_end(k):
        target = c * QN + (k * CW) // z.W
        return links.unless(
            target == j, m.up.at[k, ups[k].end], m.upf.at[rank], (s, target), up_arrivals + rank
        )

    up_last = {k: up_end(k) for k in range(z.CH) if k not in crossing}

    def group_device(n):
        return (ts * z.G + n, j)

    dk_bits = [
        (low_bits if i % 2 == 0 else turned_bits) + [BS - 1] for i in range(SL)
    ]
    dkvs = [
        Halving(links, m.dks.at[i], [seq_stage(b) for b in dk_bits[i]], m.dkr.at[i])
        for i in range(SL)
    ]
    dk_place = [[placed(n, dk_bits[i]) for n in range(NS)] for i in range(2)]

    coef = scale * math.log2(math.e)
    key_spot = lax.broadcasted_iota(jnp.int32, (SPAN, LEN), 1)
    row_spot = s * SPAN + lax.broadcasted_iota(jnp.int32, (SPAN, LEN), 0)

    def attend(hg, i):
        kv = m.kv[i].reshape(LEN, PAIR)
        m.kvs[...] = kv
        m.vks[...] = pltpu.roll(kv.astype(F32), HEAD, 1).astype(BF)
        length = jnp.int32(0)
        for n in range(SL):
            length = jnp.where(i == n, lens[n], length)
        allowed = jnp.logical_and(key_spot <= row_spot, key_spot < length)
        m.bias[...] = jnp.where(allowed, 0.0, -1e9)
        sides = (m.kvs, m.vks)
        rows = pl.ds(pl.multiple_of(i * SPAN, SPAN), SPAN)
        step = z.STEP
        d_key = d_value = None
        for first in range(0, PG, step):
            count = step * SPAN
            even = slice(first * SPAN, first * SPAN + count)
            odd = slice(PR + first * SPAN, PR + first * SPAN + count)
            halves = (slice(0, count), slice(count, 2 * count))
            q = (m.l1[hg, i, even, :], m.l2[hg, i, odd, :])
            a = (m.l2[hg, i, even, :], m.l1[hg, i, odd, :])
            mask = jnp.concatenate([m.bias[...]] * step, axis=0)
            mixed, dqs = {}, {}
            for group in ((0, 1),) if LEN <= 1024 else ((0,), (1,)):
                raw = {e: dot(q[e], sides[e][...], 1, 1) for e in group}
                dps = {e: dot(a[e], sides[1 - e][...], 1, 1) for e in group}
                probs = {}
                for e in group:
                    score = raw[e] * coef + mask
                    w = jnp.exp2(score - jnp.max(score, axis=-1, keepdims=True))
                    probs[e] = w * (1.0 / jnp.sum(w, axis=-1, keepdims=True))
                for e in group:
                    rounded = probs[e].astype(BF)
                    mixed[e] = dot(rounded, sides[1 - e][...])
                    (m.r2 if e == 0 else m.r1)[halves[e], :] = rounded
                for e in group:
                    pd = probs[e] * dps[e]
                    ds = (pd - probs[e] * jnp.sum(pd, axis=-1, keepdims=True)).astype(BF)
                    (m.r1 if e == 0 else m.r2)[halves[e], :] = ds
                    dqs[e] = dot(ds, sides[e][...])
            for p in range(step):
                at = slice(p * SPAN, (p + 1) * SPAN)
                n = hg * PG + first + p
                cols = slice(n * PAIR, (n + 1) * PAIR)
                m.att[rows, cols] = jnp.where(low, mixed[0][at], mixed[1][at]).astype(BF)
                dq = jnp.where(low, dqs[0][at], dqs[1][at]) * scale
                m.dq[rows, cols] = turned_back(dq, tables).astype(BF)
            if step == PG:
                one = dot(m.l1[hg, i], m.r1[...], 0, 0)
                two = dot(m.l2[hg, i], m.r2[...], 0, 0)
            else:
                one = dot(m.l1[hg, i, even, :], m.r1[halves[0], :], 0, 0)
                one = one + dot(m.l1[hg, i, odd, :], m.r1[halves[1], :], 0, 0)
                two = dot(m.l2[hg, i, even, :], m.r2[halves[0], :], 0, 0)
                two = two + dot(m.l2[hg, i, odd, :], m.r2[halves[1], :], 0, 0)
            key_part = one[:HEAD] + two[HEAD:]
            value_part = one[HEAD:] + two[:HEAD]
            d_key = key_part if d_key is None else d_key + key_part
            d_value = value_part if d_value is None else d_value + value_part
        d_key = d_key * scale
        return jnp.concatenate([d_key, d_value], axis=0)

    def hooked(hooks, i):
        for n, steps in hooks.items():

            @pl.when(i == n)
            def _(steps=steps):
                for step in steps:
                    step()

    for d in range(NO):
        copy, _, gets = near_by[d]

        @pl.when(gets)
        def _(copy=copy):
            copy.wait_recv()

    def up_step(k, n):
        return lambda: ups[k].step(n)

    def slots_done(pipe):
        for n in range(BJ - 1):
            pipe.finish(n)
            if n + 1 < BJ - 1:
                pipe.start(n + 1)

    early = {n: [] for n in range(SL)}
    late = {n: [] for n in range(SL)}
    tail = []
    plan = [early[n] for n in range(SL)] + [late[n] for n in range(SL)] + [tail]

    def at_point(n, step):
        plan[min(n, 2 * SL)].append(step)

    small = BS == 3 and z.CPP == 2
    order = PLAN if small else {}

    def at(name, step):
        plan[order.get(name, 2 * SL)].append(step)

    for k in range(z.CH):
        at(f"y{k}", lambda k=k: slots_done(dn_first[k]))
        if k % 2 == 1:
            at(f"y{k}", lambda k=k: dn_start(0, k // 2))
    for l in range(BS - 1):
        for n in range(z.CH >> (l + 1)):
            at(f"d{l}{n}", lambda l=l, n=n: dn_finish(l, n))
            if l + 1 < BS - 1 and n % 2 == 1:
                at(f"d{l}{n}", lambda l=l, n=n: dn_start(l + 1, n // 2))
    at("dn0", lambda: dn_last(0))
    for l in range(BS - 2, -1, -1):
        for n in range(2**l):
            at(f"e{l}{n}", lambda l=l, n=n: other_finish(l, n))
            if l > 0 and n >= 2 ** (l - 1):
                at(f"e{l}{n}", lambda l=l, n=n: other_start(l - 1, n - 2 ** (l - 1)))
    at("e00", lambda: dn_second.start(0))
    at("ey", lambda: slots_done(dn_second))
    at("dn1", lambda: dn_last(1))
    if crossing:
        at("cross", crossed)
    for k in ups:
        for n in range(1, BS + 1):
            at(f"u{k}{n}", up_step(k, n))
        if k not in crossing:
            at(f"u{k}{BS}", up_last[k])

    def early_body(i, _):
        m.dkt[i] = attend(0, i).astype(m.dkt.dtype)
        hooked(early, i)
        return 0

    lax.fori_loop(0, SL, early_body, 0)

    wo_core = [Halving(links, m.wo.at[hg], [slot_stage(0)], m.wor.at[hg]) for hg in range(2)]
    gq_core = [Halving(links, m.gq.at[hg], [slot_stage(0)], m.gqr.at[hg]) for hg in range(2)]
    wo_group = [
        Direct(
            links,
            z.G,
            low_s,
            group_device,
            lambda n, hg=hg: m.wo.at[hg, c * z.G + n],
            m.woq.at[hg],
        )
        for hg in range(2)
    ]
    gq_group = [
        Direct(
            links,
            z.G,
            low_s,
            group_device,
            lambda n, hg=hg: m.gq.at[hg, pl.ds(c * NS + 2 * n, 2)],
            m.gqq.at[hg],
        )
        for hg in range(2)
    ]
    wo_arrivals = links.take(2 * NJ)
    gq_arrivals = links.take(2 * NJ)
    me = ts * NJ + j
    wo_ends = [
        [
            links.unless(
                jnp.logical_and(ts == hg, j == n),
                m.wos.at[hg, n],
                m.wof.at[me],
                (hg * z.G + low_s, n),
                wo_arrivals + me,
            )
            for n in range(NJ)
        ]
        for hg in range(2)
    ]
    gq_ends = [
        [
            links.unless(
                jnp.logical_and(ts == t, j == hg * QN + n),
                m.gqs.at[hg, t * QN + n],
                m.gqf.at[me],
                (t * z.G + low_s, hg * QN + n),
                gq_arrivals + me,
            )
            for t in range(2)
            for n in range(QN)
        ]
        for hg in range(2)
    ]

    def project(hg):
        cols = slice(hg * (D // 2), (hg + 1) * (D // 2))
        part = dot(m.att[:, cols], m.g2[0:ROWS, :], 0, 0).astype(BF)
        for n in range(z.G):
            for r in range(2):
                at = n * R + r * R2
                m.wo[hg, r * z.G + n] = part[at : at + R2, :]
        wo_core[hg].start(0)
        part = dot(m.ain[...], m.dq[:, cols], 0, 0).astype(BF)
        for n in range(NS):
            for r in range(2):
                at = n * R + r * R2
                m.gq[hg, r * NS + (n % z.G) * 2 + n // z.G] = part[at : at + R2, :]
        gq_core[hg].start(0)

    def project_group(hg):
        wo_core[hg].finish(0)
        wo_group[hg].start()
        gq_core[hg].finish(0)
        gq_group[hg].start()

    def project_last(hg):
        wo_group[hg].finish()
        total = m.wo[hg, c * z.G + low_s].astype(F32)
        for d in range(1, z.G):
            total = total + m.woq[hg, lax.rem(low_s + d, z.G)].astype(F32)
        total = total.astype(BF)
        for n in range(NJ):
            m.wos[hg, n] = total[:, n * C4 : (n + 1) * C4]
            wo_ends[hg][n]()
        gq_group[hg].finish()
        for t in range(2):
            total = m.gq[hg, c * NS + 2 * low_s + t].astype(F32)
            for d in range(1, z.G):
                total = total + m.gqq[hg, lax.rem(low_s + d, z.G), t].astype(F32)
            total = total.astype(BF)
            for n in range(QN):
                m.gqs[hg, t * QN + n] = total[:, n * C4 : (n + 1) * C4]
                gq_ends[hg][t * QN + n]()

    project(0)
    late[0] += [lambda: project_group(0)]
    late[1] += [lambda: project_last(0)]
    marks = {n: [] for n in range(1, 7)}
    for i in range(SL):
        for n in range(1, BS + 1):
            where = DK_PLAN[i, n] if small and SL == 4 else 6
            step = lambda i=i, n=n: dkvs[i].step(n)
            (late[where + 4] if where < 0 else marks[where]).append(step)

    def mark(n):
        for step in marks[n]:
            step()

    def late_body(i, _):
        total = (m.dkt[i] + attend(1, i)).astype(BF)
        for n in range(NS):
            place = jnp.where(lax.rem(i, 2) == 0, dk_place[0][n], dk_place[1][n])
            m.dks[i, place] = total[:, n * SPAN : (n + 1) * SPAN]
        for n in range(SL):

            @pl.when(i == n)
            def _(n=n):
                dkvs[n].start(0)

        hooked(late, i)
        return 0

    lax.fori_loop(0, SL, late_body, 0)

    project(1)
    for k in range(halfway):
        rows = slice(ROWS + k * RB, ROWS + (k + 1) * RB)
        here = slice(k * RB, (k + 1) * RB)
        msend[here, :] = dot(m.act[rows, :], m.wdn[...]).astype(BF)
    project_group(1)
    mark(1)
    for k in range(halfway):
        rows = slice(ROWS + k * RB, ROWS + (k + 1) * RB)
        here = slice(k * RB, (k + 1) * RB)
        dsend[here, :] = dot(m.dup[rows, :], m.wup[...], 1, 1).astype(BF)
    got_out = links.start(msend, mrecv, buddy)
    got_back = links.start(dsend, drecv, buddy)
    mark(2)
    for step in tail:
        step()
    for k in range(halfway):
        here = slice(k * RB, (k + 1) * RB)
        m.own_mlp[here, :] = dot(m.act[here, :], m.wdn[...]) + dot(m.att[here, :], m.wout[...])
    mark(3)
    for k in range(halfway):
        here = slice(k * RB, (k + 1) * RB)
        m.own_d[here, :] = dot(m.dup[here, :], m.wup[...], 1, 1).astype(m.own_d.dtype)
    mark(4)
    got_out.wait_recv()
    got_back.wait_recv()

    def normed(rows):
        v = m.x[rows, :].astype(F32)
        v = v - jnp.mean(v, axis=-1, keepdims=True)
        inv = lax.rsqrt(jnp.mean(v * v, axis=-1, keepdims=True) + 1e-05)
        return v * inv, inv

    g_sum = jnp.zeros((1, D), F32)
    gain_two = jnp.zeros((1, D), F32)
    shift_two = jnp.zeros((1, D), F32)
    out_copies = []
    for i in range(SL):
        rows = slice(i * SPAN, (i + 1) * SPAN)
        total = m.x[rows, :].astype(F32) + m.own_mlp[rows, :] + mrecv[rows, :].astype(F32)
        total = total + (pars[5:6, :] + pars[6:7, :])
        mrecv[rows, :] = jnp.where(spot < lens[i], total, 0.0).astype(BF)
        d_mlp = m.own_d[rows, :] + drecv[rows, :].astype(F32)
        unit, _ = normed(rows)
        gain_two = gain_two + jnp.sum(d_mlp * unit, axis=0, keepdims=True)
        shift_two = shift_two + jnp.sum(d_mlp, axis=0, keepdims=True)
        m.own_d[rows, :] = (d_mlp * pars[2:3, :]).astype(m.own_d.dtype)
        g_sum = g_sum + jnp.sum(m.g2[rows, :].astype(F32), axis=0, keepdims=True)
    copy = pltpu.make_async_copy(mrecv, o_lo, m.lsem.at[8])
    copy.start()
    out_copies.append(copy)
    m.sv[0, 4:5, :] = gain_two
    m.sv[0, 5:6, :] = shift_two
    m.sv[0, 6:7, :] = g_sum
    sv_one = Direct(links, NJ, j, slot_device, lambda n: m.sv.at[0], m.sva)
    sv_two = Direct(links, NS, s, seq_device, lambda n: m.sv.at[1], m.svb)
    m.sva[j] = m.sv[0]
    sv_one.start()
    mark(5)

    bq = jnp.zeros((1, D), F32)
    for i in range(SL):
        rows = slice(i * SPAN, (i + 1) * SPAN)
        dq = m.dq[rows, :]
        bq = bq + jnp.sum(dq.astype(F32), axis=0, keepdims=True)
        m.own_mlp[rows, :] = dot(dq, m.wq[...], 1, 1)
    project_last(1)
    mark(6)

    bkv = jnp.zeros((1, PAIR), F32)
    for i in range(SL):
        d_kv = jnp.transpose(m.dks[i, dkvs[i].end].astype(F32))
        d_kv = turned_back(d_kv, key_tables)
        bkv = bkv + jnp.sum(d_kv, axis=0, keepdims=True)
        m.kvs[i * SPAN : (i + 1) * SPAN, :] = d_kv.astype(BF)
    d_kv_pre = m.kvs[0:ROWS, :]
    part = dot(d_kv_pre, m.ain[...], 0, 0).astype(BF)
    for n in range(NJ):
        m.kgs[n] = part[n * z.KR : (n + 1) * z.KR, :]
    kg_one = Direct(links, NJ, j, slot_device, lambda n: m.kgs.at[n], m.kgf)
    kg_two = Direct(links, NS, s, seq_device, lambda n: m.kg2.at[n], m.kgx)
    m.kgf[j] = m.kgs[j]
    kg_one.start()

    gain_one = jnp.zeros((1, D), F32)
    shift_one = jnp.zeros((1, D), F32)
    for i in range(SL):
        rows = slice(i * SPAN, (i + 1) * SPAN)
        d_in = m.own_mlp[rows, :] + dot(m.kvs[rows, :], m.wkv[...], 1, 1)
        unit, _ = normed(rows)
        gain_one = gain_one + jnp.sum(d_in * unit, axis=0, keepdims=True)
        shift_one = shift_one + jnp.sum(d_in, axis=0, keepdims=True)
        m.own_mlp[rows, :] = d_in
    m.sw[0] = jnp.zeros((24, 128), F32)
    for n in range(D // 128):
        cols = slice(n * 128, (n + 1) * 128)
        m.sw[0, n : n + 1, :] = gain_one[:, cols]
        m.sw[0, 6 + n : 7 + n, :] = shift_one[:, cols]
        m.sw[0, 12 + n : 13 + n, :] = bq[:, cols]
    m.sw[0, 18:19, :] = bkv
    sw_one = Direct(links, NJ, j, slot_device, lambda n: m.sw.at[0], m.swa)
    sw_two = Direct(links, NS, s, seq_device, lambda n: m.sw.at[1], m.swb)
    m.swa[j] = m.sw[0]
    sw_one.start()
    for i in range(SL):
        rows = slice(i * SPAN, (i + 1) * SPAN)
        unit, inv = normed(rows)
        d_unit = m.own_mlp[rows, :] * pars[0:1, :] + m.own_d[rows, :]
        along = jnp.mean(d_unit * unit, axis=-1, keepdims=True)
        d_unit = d_unit - jnp.mean(d_unit, axis=-1, keepdims=True) - unit * along
        m.own_mlp[rows, :] = m.g2[rows, :].astype(F32) + d_unit * inv
    copy = pltpu.make_async_copy(m.own_mlp, o_gi, m.lsem.at[9])
    copy.start()
    out_copies.append(copy)

    def summed(ref, size):
        total = ref[0].astype(F32)
        for n in range(1, size):
            total = total + ref[n].astype(F32)
        return total

    sv_one.finish()
    m.sv[1] = summed(m.sva, NJ)
    m.svb[s] = m.sv[1]
    sv_two.start()
    kg_one.finish()
    part = summed(m.kgf, NJ).astype(BF)
    for n in range(NS):
        m.kg2[n] = part[:, n * R : (n + 1) * R]
    m.kgx[s] = m.kg2[s]
    kg_two.start()
    sw_one.finish()
    m.sw[1] = summed(m.swa, NJ)
    m.swb[s] = m.sw[1]
    sw_two.start()

    if crossing:
        o_up[:, CW:] = m.upy[0, ups[1].end].astype(F32)
    for n in range(QN):
        links.arrived(m.upf.at[n], up_arrivals + n)
    o_up[:, 0:CW] = summed(m.upf, QN)
    for p in range(2):
        for t in range(2):
            links.arrived(m.dnf.at[p, t], dn_arrivals + 2 * p + t)
        o_dn[p * z.FRH : (p + 1) * z.FRH, :] = summed(m.dnf.at[p], 2)
    for n in range(2 * NJ):
        links.arrived(m.gqf.at[n], gq_arrivals + n)
        links.arrived(m.wof.at[n], wo_arrivals + n)
    for r in range(2):
        for out, ref in ((o_wq, m.gqf), (o_wo, m.wof)):
            total = ref[r].astype(F32)
            for n in range(1, NJ):
                total = total + ref[2 * n + r].astype(F32)
            out[r * R2 : (r + 1) * R2, :] = total
    sv_two.finish()
    o_sv[...] = summed(m.svb, NS)
    kg_two.finish()
    o_wkv[...] = summed(m.kgx, NS)
    sw_two.finish()
    o_sw[...] = summed(m.swb, NS)
    for copy in out_copies:
        copy.wait()
    links.finish()


class Names:
    pass


def body(
    hidden_in, lengths, out_grad, ln1_gain, ln1_bias, ln2_gain, ln2_bias, w_query, b_query,
    w_keyval, b_keyval, w_out, b_out, w_up, b_up, w_down, b_down,
):
    SL, SPAN, D = hidden_in.shape
    FF = w_up.shape[1]
    z = Sizes(lax.axis_size("seq"), lax.axis_size("slot"), SL, SPAN, D, FF)
    scratch = scratch_of(z)
    names = list(scratch)
    n_in, n_out = 18, 9

    def call(*refs):
        m = Names()
        for name, ref in zip(names, refs[n_in + n_out :]):
            setattr(m, name, ref)
        kernel(z, refs[:n_in], refs[n_in : n_in + n_out], m)

    anywhere = pl.BlockSpec(memory_space=pl.ANY)
    vmem = pl.BlockSpec(memory_space=pltpu.VMEM)
    shape = jax.ShapeDtypeStruct
    lo, gi, up, dn, wo, wq, wkv, sv, sw = pl.pallas_call(
        call,
        out_shape=[
            shape((z.ROWS, D), BF),
            shape((z.ROWS, D), F32),
            shape((z.R, z.W), F32),
            shape((z.CW, z.DW // 2), F32),
            shape((z.R, z.C4), F32),
            shape((z.R, z.C4), F32),
            shape((z.KR, z.R), F32),
            shape((8, D), F32),
            shape((24, 128), F32),
        ],
        in_specs=[anywhere, anywhere, pl.BlockSpec(memory_space=pltpu.SMEM)]
        + [anywhere] * 6
        + [vmem] * 9,
        out_specs=[anywhere, anywhere] + [vmem] * 7,
        scratch_shapes=list(scratch.values()),
        compiler_params=pltpu.CompilerParams(
            collective_id=0, has_side_effects=True, vmem_limit_bytes=63 * 2**20
        ),
    )(
        hidden_in.reshape(z.ROWS, D),
        out_grad.reshape(z.ROWS, D),
        lengths,
        w_query,
        w_keyval,
        w_out,
        w_up,
        w_down,
        jnp.asarray(rotary_tables(z.LEN)),
        ln1_gain,
        ln1_bias,
        ln2_gain,
        ln2_bias,
        b_query,
        b_out,
        b_down,
        b_up,
        b_keyval,
    )
    wide = (lo, gi, up, wo, wq)

    def hand_over(*refs):
        n = len(wide)
        sources, (dn, wkv, sv, sw) = refs[:n], refs[n : n + 4]
        targets, rest = refs[n + 4 : 2 * n + 4], refs[2 * n + 4 : 2 * n + 15]
        held, came, left = refs[2 * n + 15 : 3 * n + 15], refs[-2], refs[-1]
        copies = [
            (
                pltpu.make_async_copy(a, b, came.at[k]),
                pltpu.make_async_copy(b, c, left.at[k]),
            )
            for k, (a, b, c) in enumerate(zip(sources, held, targets))
        ]
        for copy, _ in copies:
            copy.start()
        o_dn, o_wkv, gain_one, shift_one, gain_two, shift_two, bq, bkv, bo, bup, bd = rest
        for at, ref in enumerate((gain_one, shift_one, bq)):
            parts = [sw[k : k + 1, :] for k in range(at * (D // 128), (at + 1) * (D // 128))]
            ref[...] = jnp.concatenate(parts, axis=1).reshape(D)
        bkv[...] = sw[18:19, :].reshape(PAIR)
        gain_two[...] = sv[4:5, :].reshape(D)
        shift_two[...] = sv[5:6, :].reshape(D)
        bo[...] = sv[6:7, :].reshape(D)
        bd[...] = sv[6:7, :].reshape(D)
        parts = [sv[k : k + 1, :] for k in range(FF // D)]
        bup[...] = jnp.concatenate(parts, axis=1).reshape(FF)
        o_dn[...] = jnp.transpose(dn[...])
        o_wkv[...] = wkv[...]
        for copy, out in copies:
            copy.wait()
            out.start()
        for _, out in copies:
            out.wait()

    lo, gi, up, wo, wq, dn, wkv, g1, s1, g2, s2, bq, bkv, bo, bup, bd = pl.pallas_call(
        hand_over,
        out_shape=[shape(v.shape, v.dtype) for v in wide]
        + [shape(dn.shape[::-1], F32), shape(wkv.shape, F32)]
        + [shape((n,), F32) for n in (D, D, D, D, D, PAIR, D, FF, D)],
        in_specs=[anywhere] * 5 + [vmem] * 4,
        out_specs=[anywhere] * 5 + [vmem] * 11,
        scratch_shapes=[pltpu.VMEM(v.shape, v.dtype) for v in wide]
        + [pltpu.SemaphoreType.DMA((5,)), pltpu.SemaphoreType.DMA((5,))],
    )(*wide, dn, wkv, sv, sw)
    return (
        lo.reshape(hidden_in.shape),
        gi.reshape(hidden_in.shape),
        g1, s1, g2, s2, wq, bq, wkv.T, bkv, wo, bo, up, bup, dn.T, bd,
    )


def solution(mesh):
    rows, whole, cut = P("slot", "seq", None), P(), P("seq", "slot")
    return jax.shard_map(
        body,
        mesh=mesh,
        in_specs=(rows, P("slot"), rows) + (whole,) * 14,
        out_specs=(
            rows, rows, whole, whole, whole, whole, cut, whole, cut, whole, cut, whole, cut, whole,
            cut, whole,
        ),
        check_vma=False,
    )
```
